32 devices in a mesh: seq: 8 (over z, x), tp: 4 (over y, core).
Axes of the slice: x: 2, y: 2, z: 4, core: 2. Of those that a mesh axis runs over, the one named last changes fastest.
Arguments:
- tokens: bfloat16 [4096, 1536], P('seq'), may hold values from -6 to 6
- cotangent: bfloat16 [4096, 1536], P('seq'), may hold values from -6 to 6
- doc_lengths: int32 [4], replicated, may hold values from 1 to 4096, as said below
- norm_gains: float32 [4, 1536], replicated, may hold values from 0.5 to 1.5
- input_branch: bfloat16 [1536, 2048], P('seq', 'tp'), may hold values from -0.15625 to 0.15625
- gate_branch: bfloat16 [1536, 2048], P('seq', 'tp'), may hold values from -0.15625 to 0.15625
- conv_taps: float32 [4, 2048], P(None, 'tp'), may hold values from -3 to 3
- conv_bias: float32 [2048], P('tp'), may hold values from -2 to 2
- recur_gate: bfloat16 [2048, 128], P('tp', 'seq'), may hold values from -0.5 to 0.5
- input_gate: bfloat16 [2048, 128], P('tp', 'seq'), may hold values from -0.5 to 0.5
- gate_biases: float32 [2, 2048], P(None, 'tp'), may hold values from -4 to 4
- decay_param: float32 [2048], P('tp'), may hold values from 2 to 12
- recur_output: bfloat16 [2048, 1536], P('tp', 'seq'), may hold values from -0.125 to 0.125
- dense_gate_one: bfloat16 [1536, 4608], P('seq', 'tp'), may hold values from -0.15625 to 0.15625
- dense_up_one: bfloat16 [1536, 4608], P('seq', 'tp'), may hold values from -0.15625 to 0.15625
- dense_down_one: bfloat16 [4608, 1536], P('tp', 'seq'), may hold values from -0.09375 to 0.09375
- query_weight: bfloat16 [1536, 1536], P('seq', 'tp'), may hold values from -0.15625 to 0.15625
- keyvalue_weight: bfloat16 [1536, 256], P(('seq', 'tp')), may hold values from -0.15625 to 0.15625
- attention_out: bfloat16 [1536, 1536], P('tp', 'seq'), may hold values from -0.875 to 0.875
- dense_gate_two: bfloat16 [1536, 4608], P('seq', 'tp'), may hold values from -0.15625 to 0.15625
- dense_up_two: bfloat16 [1536, 4608], P('seq', 'tp'), may hold values from -0.15625 to 0.15625
- dense_down_two: bfloat16 [4608, 1536], P('tp', 'seq'), may hold values from -0.09375 to 0.09375
Outputs:
- layer_out: bfloat16 [4096, 1536], P('seq')
- input_grad: float32 [4096, 1536], P('seq')
- norm_gains_grad: float32 [4, 1536], replicated
- input_branch_grad: float32 [1536, 2048], P('seq', 'tp')
- gate_branch_grad: float32 [1536, 2048], P('seq', 'tp')
- conv_taps_grad: float32 [4, 2048], P(None, 'tp')
- conv_bias_grad: float32 [2048], P('tp')
- recur_gate_grad: float32 [2048, 128], P('tp', 'seq')
- input_gate_grad: float32 [2048, 128], P('tp', 'seq')
- gate_biases_grad: float32 [2, 2048], P(None, 'tp')
- decay_param_grad: float32 [2048], P('tp')
- recur_output_grad: float32 [2048, 1536], P('tp', 'seq')
- dense_gate_one_grad: float32 [1536, 4608], P('seq', 'tp')
- dense_up_one_grad: float32 [1536, 4608], P('seq', 'tp')
- dense_down_one_grad: float32 [4608, 1536], P('tp', 'seq')
- query_weight_grad: float32 [1536, 1536], P('seq', 'tp')
- keyvalue_weight_grad: float32 [1536, 256], P(('seq', 'tp'))
- attention_out_grad: float32 [1536, 1536], P('tp', 'seq')
- dense_gate_two_grad: float32 [1536, 4608], P('seq', 'tp')
- dense_up_two_grad: float32 [1536, 4608], P('seq', 'tp')
- dense_down_two_grad: float32 [4608, 1536], P('tp', 'seq')
The draws below stay inside these ranges and needn't reach their ends.
Inputs may be any that keep to these rules, and one draw needn't show every extreme that they name: `doc_lengths`: lengths of 4 documents packed in order from slot 0; they sum to less than 4096, and the slots after them are padding.
All inputs are finite; a program needn't handle non-finite values.
Results may differ from the reference program's by a relative error of at most 0.02.
Values may be sent and summed in bfloat16 or wider, within the bound.
A program may use at most 192 MiB of HBM per device.

```python
import jax
import jax.numpy as jnp
from jax import lax

D = 1536
LRU = 2048
FF = 4608
HEADS = 12
HD = 128
BLOCK = 128
CONV = 4
WINDOW = 1024
NDOC = 4
TOK_DEV = 512
TOKENS = 4096


def draw_doc_lengths(key, part):
    key = jax.random.fold_in(key, 7)
    short_key, tail_key, pick_key = jax.random.split(key, 3)
    short_lengths = jax.random.randint(short_key, (NDOC,), TOK_DEV // 8, TOK_DEV // 5 + 1)
    tail_slots = jax.random.randint(tail_key, (), TOK_DEV // 8, TOK_DEV // 5 + 1)
    chosen = jax.random.randint(pick_key, (), 0, NDOC)
    picked = jnp.arange(NDOC) == chosen
    longest = TOKENS - tail_slots - jnp.sum(jnp.where(picked, 0, short_lengths))
    return jnp.where(picked, longest, short_lengths).astype(jnp.int32)


def shard_levels(rng, shape, shards, low, top_value):
    level = 1.0
    for dim, parts in shards:
        steps = jax.random.uniform(jax.random.fold_in(jax.random.fold_in(rng, 6), dim), (parts,), jnp.float32, low / len(shards), top_value / len(shards))
        level = level * jnp.repeat(jnp.exp(steps), shape[dim] // parts).reshape((-1,) + (1,) * (len(shape) - 1 - dim))
    return level


def centred(own_key, extent, width, reach, cuts=(), held_as=jnp.bfloat16):
    array = width * jax.random.normal(own_key, extent, jnp.float32)
    if cuts:
        array = array * shard_levels(own_key, extent, cuts, -0.22, 0.18)
    return jnp.clip(array, -reach, reach).astype(held_as)


def setup_inputs(seed: int = 0) -> dict:
    streams_of = jax.random.split(jax.random.key(seed), 23)
    return {
        "tokens": centred(streams_of[0], (TOKENS, D), 1.0, 6.0, ((0, 8),)),
        "cotangent": centred(streams_of[1], (TOKENS, D), 1.0, 6.0, ((0, 8),)),
        "doc_lengths": draw_doc_lengths(jax.random.fold_in(streams_of[22], 71), 0),
        "norm_gains": jnp.clip(1.0 + 0.1 * jax.random.normal(streams_of[3], (4, D), jnp.float32), 0.5, 1.5),
        "input_branch": centred(streams_of[4], (D, LRU), D ** -0.5, 0.15625, ((0, 8), (1, 4))),
        "gate_branch": centred(streams_of[5], (D, LRU), D ** -0.5, 0.15625, ((0, 8), (1, 4))),
        "conv_taps": centred(streams_of[6], (CONV, LRU), 0.5, 3.0, ((1, 4),), jnp.float32),
        "conv_bias": centred(streams_of[7], (LRU,), 0.3, 2.0, ((0, 4),), jnp.float32),
        "recur_gate": centred(streams_of[8], (LRU, BLOCK), BLOCK ** -0.5, 0.5, ((0, 4), (1, 8))),
        "input_gate": centred(streams_of[9], (LRU, BLOCK), BLOCK ** -0.5, 0.5, ((0, 4), (1, 8))),
        "gate_biases": centred(streams_of[10], (2, LRU), 1.0, 4.0, ((1, 4),), jnp.float32),
        "decay_param": jnp.clip(2.0 + 10.0 * jax.random.uniform(streams_of[11], (LRU,), jnp.float32) ** shard_levels(streams_of[11], (LRU,), ((0, 4),), -0.2, 0.2), 2.0, 12.0),
        "recur_output": centred(streams_of[12], (LRU, D), LRU ** -0.5, 0.125, ((0, 4), (1, 8))),
        "dense_gate_one": centred(streams_of[13], (D, FF), D ** -0.5, 0.15625, ((0, 8), (1, 4))),
        "dense_up_one": centred(streams_of[14], (D, FF), D ** -0.5, 0.15625, ((0, 8), (1, 4))),
        "dense_down_one": centred(streams_of[15], (FF, D), FF ** -0.5, 0.09375, ((0, 4), (1, 8))),
        "query_weight": centred(streams_of[16], (D, HEADS * HD), D ** -0.5, 0.15625, ((0, 8), (1, 4))),
        "keyvalue_weight": centred(streams_of[17], (D, 2 * HD), D ** -0.5, 0.15625, ((0, 32),)),
        "attention_out": centred(streams_of[18], (HEADS * HD, D), (HEADS * HD // 32) ** -0.5, 0.875, ((0, 4), (1, 8))),
        "dense_gate_two": centred(streams_of[19], (D, FF), D ** -0.5, 0.15625, ((0, 8), (1, 4))),
        "dense_up_two": centred(streams_of[20], (D, FF), D ** -0.5, 0.15625, ((0, 8), (1, 4))),
        "dense_down_two": centred(streams_of[21], (FF, D), FF ** -0.5, 0.09375, ((0, 4), (1, 8))),
    }


@jax.custom_vjp
def low(v):
    return lax.optimization_barrier(v.astype(jnp.bfloat16)).astype(jnp.float32)

@jax.custom_vjp
def low_back(v):
    return v

def low_keep(v):
    return (low(v), None)

def low_pass(kept, grad):
    return (grad,)

def back_keep(v):
    return (v, None)

def back_low(kept, grad):
    return (low(grad),)
low.defvjp(low_keep, low_pass)
low_back.defvjp(back_keep, back_low)

def matmul(left, right):
    return jnp.dot(left, right, precision=lax.Precision.HIGHEST, preferred_element_type=jnp.float32)

def rms_norm(values, gain):
    return values * lax.rsqrt(lax.optimization_barrier(jnp.mean(values * values, axis=-1, keepdims=True)) + 1e-06) * gain

def layout(doc_lengths, first_slot, count):
    ends = jnp.cumsum(doc_lengths, dtype=jnp.int32)
    slots = first_slot + jnp.arange(count, dtype=jnp.int32)
    passed = slots[:, None] >= ends[None, :]
    segment = lax.optimization_barrier(jnp.sum(passed.astype(jnp.int32), axis=1))
    begin = lax.optimization_barrier(jnp.max(jnp.where(passed, ends[None, :], 0), axis=1))
    segment = jnp.where(slots < 0, -1, segment)
    position = slots - begin
    reset = (slots != begin).astype(jnp.float32)
    valid = (segment < doc_lengths.shape[0]).astype(jnp.float32)
    return (segment, position, reset, valid)

def rotate(values, position):
    half_width = values.shape[-1] // 2
    frequency = 10000.0 ** (-jnp.arange(half_width, dtype=jnp.float32) / half_width)
    angle = position.astype(jnp.float32)[:, None] * frequency[None, :]
    if values.ndim == 3:
        angle = angle[:, None, :]
    cosine = jnp.cos(angle)
    sine = jnp.sin(angle)
    first_half = values[..., :half_width]
    second_half = values[..., half_width:]
    return jnp.concatenate([first_half * cosine - second_half * sine, second_half * cosine + first_half * sine], axis=-1)

def convolve(extended, taps, bias, segment):
    leading = CONV - 1
    total_rows = extended.shape[0] - leading
    result = bias[None, :] + taps[0][None, :] * extended[leading:]
    for lag_index in range(1, CONV):
        same = (segment[leading:] == segment[leading - lag_index:leading - lag_index + total_rows]).astype(jnp.float32)
        result = result + same[:, None] * taps[lag_index][None, :] * extended[leading - lag_index:leading - lag_index + total_rows]
    return result

def coefficients(recur_raw, input_raw, conv_values, bias_pair, decay_values, reset):
    recur_rate = jax.nn.sigmoid(recur_raw + bias_pair[0][None, :])
    input_rate = jax.nn.sigmoid(input_raw + bias_pair[1][None, :])
    log_decay = -8.0 * recur_rate * jax.nn.softplus(-decay_values)[None, :]
    multiplier = jnp.sqrt(jnp.maximum(-jnp.expm1(2.0 * log_decay), 0.01))
    return (jnp.exp(log_decay) * reset[:, None], multiplier * input_rate * conv_values)

def combine_state(earlier, later):
    return (earlier[0] * later[0], later[0] * earlier[1] + later[1])

def block_product(values, weight):
    total_rows = values.shape[0]
    block_width = weight.shape[1]
    block_count = weight.shape[0] // block_width
    left = values.reshape(total_rows, block_count, block_width)
    right = weight.reshape(block_count, block_width, block_width)
    result = jnp.einsum('tni,nic->tnc', left, right, precision=lax.Precision.HIGHEST)
    return result.reshape(total_rows, block_count * block_width)

def dense(stream, gain, gate_weight, up_weight, down_weight):
    normed = low(rms_norm(stream, gain))
    gate_values = low_back(matmul(normed, gate_weight))
    up_values = low_back(matmul(normed, up_weight))
    hidden = low(jax.nn.gelu(gate_values) * up_values)
    return low_back(matmul(hidden, down_weight))

def attention(query, keys, values, segment):
    total_rows = query.shape[0]
    block_rows = min(512, total_rows)
    padded_keys = jnp.pad(keys, ((WINDOW, 0), (0, 0)))
    padded_values = jnp.pad(values, ((WINDOW, 0), (0, 0)))
    padded_segment = jnp.concatenate([jnp.full((WINDOW,), -1, jnp.int32), segment])
    score_scale = HD ** (-0.5)

    def one_block(index):
        start = (index * block_rows).astype(jnp.int32)
        query_block = lax.dynamic_slice_in_dim(query, start, block_rows, 0)
        key_block = lax.dynamic_slice_in_dim(padded_keys, start, block_rows + WINDOW, 0)
        value_block = lax.dynamic_slice_in_dim(padded_values, start, block_rows + WINDOW, 0)
        query_segment = lax.dynamic_slice_in_dim(segment, start, block_rows, 0)
        key_segment = lax.dynamic_slice_in_dim(padded_segment, start, block_rows + WINDOW, 0)
        distance = jnp.arange(block_rows, dtype=jnp.int32)[:, None] - (jnp.arange(block_rows + WINDOW, dtype=jnp.int32) - WINDOW)[None, :]
        allowed = (query_segment[:, None] == key_segment[None, :]) & (distance >= 0) & (distance < WINDOW)
        raw = low_back(jnp.einsum('qhd,kd->hqk', query_block, key_block, precision=lax.Precision.HIGHEST))
        scores = jnp.where(allowed[None], raw * score_scale, -1e+30)
        weights = low(jax.nn.softmax(scores, axis=-1))
        return low_back(jnp.einsum('hqk,kd->qhd', weights, value_block, precision=lax.Precision.HIGHEST))
    blocks = lax.map(jax.checkpoint(one_block), jnp.arange(total_rows // block_rows, dtype=jnp.int32))
    return blocks.reshape(total_rows, query.shape[1], query.shape[2])

def reference(tokens, cotangent, doc_lengths, norm_gains, input_branch, gate_branch, conv_taps, conv_bias, recur_gate, input_gate, gate_biases, decay_param, recur_output, dense_gate_one, dense_up_one, dense_down_one, query_weight, keyvalue_weight, attention_out, dense_gate_two, dense_up_two, dense_down_two):
    total_rows = tokens.shape[0]
    segment, position, reset, valid = layout(doc_lengths, 0, total_rows)
    conv_segment = jnp.concatenate([jnp.full((CONV - 1,), -1, jnp.int32), segment])

    def forward(stream, gains, branch_weight, gating_weight, taps, bias, recur_weight, input_weight, bias_pair, decay_values, output_weight, gate_one, up_one, down_one, query_full, keyvalue_full, attn_full, gate_two, up_two, down_two):
        normed_one = low(rms_norm(stream, gains[0]))
        branch = low_back(matmul(normed_one, branch_weight))
        gating = low_back(matmul(normed_one, gating_weight))
        padded = jnp.pad(branch, ((CONV - 1, 0), (0, 0)))
        conv_out = convolve(padded, taps, bias, conv_segment)
        conv_low = low(conv_out)
        recur_raw = low_back(block_product(conv_low, recur_weight))
        input_raw = low_back(block_product(conv_low, input_weight))
        decay, drive = coefficients(recur_raw, input_raw, conv_out, bias_pair, decay_values, reset)
        state = lax.associative_scan(combine_state, (decay, drive), axis=0)[1]
        mixed = low(state * jax.nn.gelu(gating))
        stream = stream + low_back(matmul(mixed, output_weight))
        stream = stream + dense(stream, gains[1], gate_one, up_one, down_one)
        normed_three = low(rms_norm(stream, gains[2]))
        query = low_back(matmul(normed_three, query_full)).reshape(total_rows, query_full.shape[1] // HD, HD)
        keyval = low_back(matmul(normed_three, keyvalue_full))
        query_rot = low(rotate(query, position))
        key_rot = low(rotate(keyval[:, :HD], position))
        value_low = low(keyval[:, HD:])
        attended = low(attention(query_rot, key_rot, value_low, segment)).reshape(total_rows, query_full.shape[1])
        stream = stream + low_back(matmul(attended, attn_full))
        stream = stream + dense(stream, gains[3], gate_two, up_two, down_two)
        return stream * valid[:, None]
    weights = (norm_gains, input_branch.astype(jnp.float32), gate_branch.astype(jnp.float32), conv_taps, conv_bias, recur_gate.astype(jnp.float32), input_gate.astype(jnp.float32), gate_biases, decay_param, recur_output.astype(jnp.float32), dense_gate_one.astype(jnp.float32), dense_up_one.astype(jnp.float32), dense_down_one.astype(jnp.float32), query_weight.astype(jnp.float32), keyvalue_weight.astype(jnp.float32), attention_out.astype(jnp.float32), dense_gate_two.astype(jnp.float32), dense_up_two.astype(jnp.float32), dense_down_two.astype(jnp.float32))
    result, pullback = jax.vjp(forward, tokens.astype(jnp.float32), *weights)
    grads = pullback(cotangent.astype(jnp.float32))
    return (result.astype(jnp.bfloat16), grads[0], grads[1], grads[2], grads[3], grads[4], grads[5], grads[6], grads[7], grads[8], grads[9], grads[10], grads[11], grads[12], grads[13], grads[14], grads[15], grads[16], grads[17], grads[18], grads[19])
```

```python
import functools

import jax
import jax.numpy as jnp
from jax import lax
from jax.experimental import pallas as pl
from jax.experimental.pallas import tpu as pltpu
from jax.sharding import PartitionSpec as P

HD = 128
CONV = 4
WINDOW = 1024


def product(left, right):
    return jnp.dot(left, right, preferred_element_type=jnp.float32)


def product_left(left, right):
    return lax.dot_general(
        left, right, (((0,), (0,)), ((), ())), preferred_element_type=jnp.float32
    )


def product_right(left, right):
    return lax.dot_general(
        left, right, (((1,), (1,)), ((), ())), preferred_element_type=jnp.float32
    )


def lowered(values):
    return values.astype(jnp.bfloat16)


def rms_norm(values, gain):
    return values * lax.rsqrt(jnp.mean(values * values, axis=-1, keepdims=True) + 1e-06) * gain


def gated(gate_values, up_values):
    return jax.nn.gelu(gate_values) * up_values


def layout(doc_lengths, first_slot, count):
    ends = jnp.cumsum(doc_lengths, dtype=jnp.int32)
    slots = first_slot + jnp.arange(count, dtype=jnp.int32)
    passed = slots[:, None] >= ends[None, :]
    segment = jnp.sum(passed.astype(jnp.int32), axis=1)
    begin = jnp.max(jnp.where(passed, ends[None, :], 0), axis=1)
    segment = jnp.where(slots < 0, -1, segment)
    position = slots - begin
    reset = (slots != begin).astype(jnp.float32)
    valid = (segment < doc_lengths.shape[0]).astype(jnp.float32)
    return (segment, position, reset, valid)


def rotate(values, position):
    half_width = values.shape[-1] // 2
    frequency = 10000.0 ** (-jnp.arange(half_width, dtype=jnp.float32) / half_width)
    angle = position.astype(jnp.float32)[:, None] * frequency[None, :]
    if values.ndim == 3:
        angle = angle[:, None, :]
    cosine = jnp.cos(angle)
    sine = jnp.sin(angle)
    first_half = values[..., :half_width]
    second_half = values[..., half_width:]
    return jnp.concatenate(
        [first_half * cosine - second_half * sine, second_half * cosine + first_half * sine],
        axis=-1,
    )


def convolve(extended, taps, bias, segment):
    leading = CONV - 1
    total_rows = extended.shape[0] - leading
    result = bias[None, :] + taps[0][None, :] * extended[leading:]
    for lag_index in range(1, CONV):
        same = (
            segment[leading:] == segment[leading - lag_index : leading - lag_index + total_rows]
        ).astype(jnp.float32)
        result = (
            result
            + same[:, None]
            * taps[lag_index][None, :]
            * extended[leading - lag_index : leading - lag_index + total_rows]
        )
    return result


def coefficients(recur_raw, input_raw, conv_values, bias_pair, decay_values, reset):
    recur_rate = jax.nn.sigmoid(recur_raw + bias_pair[0][None, :])
    input_rate = jax.nn.sigmoid(input_raw + bias_pair[1][None, :])
    log_decay = -8.0 * recur_rate * jax.nn.softplus(-decay_values)[None, :]
    multiplier = jnp.sqrt(jnp.maximum(-jnp.expm1(2.0 * log_decay), 0.01))
    return (jnp.exp(log_decay) * reset[:, None], multiplier * input_rate * conv_values)


def combine_state(earlier, later):
    return (earlier[0] * later[0], later[0] * earlier[1] + later[1])


MESH = pl.DeviceIdType.MESH
LO = 2
EIGHTEEN_US = pl.CostEstimate(flops=0, bytes_accessed=60_000_000, transcendentals=0)
TEN_US = pl.CostEstimate(flops=0, bytes_accessed=33_000_000, transcendentals=0)
ANY = pl.BlockSpec(memory_space=pl.ANY)
VMEM = pl.BlockSpec(memory_space=pltpu.VMEM)


def cube():
    seq = lax.axis_index("seq")
    tp = lax.axis_index("tp")
    a = lax.rem(seq, LO)
    b = tp // 2
    c = lax.rem(tp, 2)
    across_a = (seq - a + 1 - a, tp)
    across_b = (seq, (1 - b) * 2 + c)
    across_c = (seq, b * 2 + 1 - c)
    return (a, b, c, across_a, across_b, across_c)


def greet(devices):
    barrier = pltpu.get_barrier_semaphore()
    for device in devices:
        pl.semaphore_signal(barrier, inc=1, device_id=device, device_id_type=MESH)
    pl.semaphore_wait(barrier, len(devices))


def remote(src, dst, send_sem, recv_sem, slot, device):
    return pltpu.make_async_remote_copy(
        src_ref=src,
        dst_ref=dst,
        send_sem=send_sem.at[slot],
        recv_sem=recv_sem.at[slot],
        device_id=device,
        device_id_type=MESH,
    )


def gather_kernel(full, in_ref, out_ref, send_sem, recv_sem, local_sem):
    a, b, c, across_a, across_b, across_c = cube()
    half = in_ref.shape[0] // 2

    def index(pa, pb, pc):
        return pa * 4 + pb * 2 + pc if full else pb * 2 + pc

    me, an, bn, dn = (
        index(a, b, c),
        index(1 - a, b, c),
        index(a, 1 - b, c),
        index(1 - a, 1 - b, c),
    )
    greet([across_c, across_b] + ([across_a] if full else []))
    low, high = (pl.ds(0, half), pl.ds(half, half))

    def own(part, slot, device):
        return remote(in_ref.at[part], out_ref.at[me, part], send_sem, recv_sem, slot, device)

    def onward(block, part, slot, device):
        here = out_ref.at[block, part]
        return remote(here, here, send_sem, recv_sem, slot, device)

    sent = {}

    def go(slot, copy):
        copy.start()
        sent[slot] = copy

    if full:
        go(0, own(low, 0, across_a))
    go(1, own(high, 1, across_b))
    if full:
        go(2, own(high, 2, across_a))
    go(3, own(low, 3, across_b))
    go(4, remote(in_ref, out_ref.at[me], send_sem, recv_sem, 4, across_c))
    mine = pltpu.make_async_copy(in_ref, out_ref.at[me], local_sem)
    mine.start()
    if full:
        sent[0].wait_recv()
        go(5, onward(an, low, 5, across_b))
        go(6, onward(an, low, 6, across_c))
    sent[1].wait_recv()
    if full:
        go(7, onward(bn, high, 7, across_a))
    go(8, onward(bn, high, 8, across_c))
    if full:
        sent[2].wait_recv()
        go(9, onward(an, high, 9, across_c))
    sent[3].wait_recv()
    go(10, onward(bn, low, 10, across_c))
    if full:
        sent[5].wait_recv()
        go(11, onward(dn, low, 11, across_c))
        sent[7].wait_recv()
        go(12, onward(dn, high, 12, across_c))
    for slot in (4, 6, 8, 9, 10, 11, 12):
        if slot in sent:
            sent[slot].wait_recv()
    for copy in sent.values():
        copy.wait_send()
    mine.wait()


def gather(block, full, collective_id):
    count = 8 if full else 4
    rows, width = block.shape
    result = pl.pallas_call(
        functools.partial(gather_kernel, full),
        out_shape=jax.ShapeDtypeStruct((count, rows, width), block.dtype),
        in_specs=[ANY],
        out_specs=ANY,
        scratch_shapes=[
            pltpu.SemaphoreType.DMA((13,)),
            pltpu.SemaphoreType.DMA((13,)),
            pltpu.SemaphoreType.DMA,
        ],
        name="gather_full" if full else "gather_half",
        cost_estimate=EIGHTEEN_US,
        compiler_params=pltpu.CompilerParams(collective_id=collective_id, has_side_effects=True),
    )(block)
    return result.reshape(count * rows, width)


def scatter_kernel(
    full, part_ref, out_ref, cbuf, sx, sy, tx, ty, ax, by, rx, ry, csend, crecv, send_sem, recv_sem
):
    a, b, c, across_a, across_b, across_c = cube()
    half = part_ref.shape[1] // 2

    def index(pa, pb, pc):
        return pa * 4 + pb * 2 + pc if full else pb * 2 + pc

    def pair(pa, pb):
        return pa * 2 + pb if full else pb

    low, high = (pl.ds(0, half), pl.ds(half, half))
    if full:
        order = [
            (1 - a, 1 - b, low),
            (1 - a, 1 - b, high),
            (1 - a, b, low),
            (a, 1 - b, high),
            (a, 1 - b, low),
            (1 - a, b, high),
            (a, b, low),
            (a, b, high),
        ]
    else:
        order = [(a, 1 - b, low), (a, 1 - b, high), (a, b, low), (a, b, high)]
    greet([across_c, across_b] + ([across_a] if full else []))
    core = []
    for k, (pa, pb, part) in enumerate(order):
        copy = remote(
            part_ref.at[index(pa, pb, 1 - c), part],
            cbuf.at[pair(pa, pb), part],
            csend,
            crecv,
            k,
            across_c,
        )
        copy.start()
        core.append(copy)

    def summed(k):
        pa, pb, part = order[k]
        core[k].wait_recv()
        return part_ref[index(pa, pb, c), part].astype(jnp.float32) + cbuf[
            pair(pa, pb), part
        ].astype(jnp.float32)

    sent = []

    def go(src, dst, slot, device):
        copy = remote(src, dst, send_sem, recv_sem, slot, device)
        copy.start()
        sent.append(copy)
        return copy

    if full:
        sx[0] = lowered(summed(0))
        x0 = go(sx.at[0], ax.at[0], 0, across_a)
        sy[0] = lowered(summed(1))
        y0 = go(sy.at[0], by.at[0], 1, across_b)
        sx[1] = lowered(summed(2))
        x1 = go(sx.at[1], ax.at[1], 2, across_a)
        sy[1] = lowered(summed(3))
        y1 = go(sy.at[1], by.at[1], 3, across_b)
        total = summed(4)
        x0.wait_recv()
        ty[...] = lowered(total + ax[0].astype(jnp.float32))
        last_y = go(ty, ry, 4, across_b)
        total = summed(5)
        y0.wait_recv()
        tx[...] = lowered(total + by[0].astype(jnp.float32))
        last_x = go(tx, rx, 5, across_a)
        total = summed(6)
        x1.wait_recv()
        total = total + ax[1].astype(jnp.float32)
        last_y.wait_recv()
        out_ref[low] = total + ry[...].astype(jnp.float32)
        total = summed(7)
        y1.wait_recv()
        total = total + by[1].astype(jnp.float32)
        last_x.wait_recv()
        out_ref[high] = total + rx[...].astype(jnp.float32)
    else:
        sy[0] = lowered(summed(0))
        y0 = go(sy.at[0], by.at[0], 1, across_b)
        sy[1] = lowered(summed(1))
        y1 = go(sy.at[1], by.at[1], 3, across_b)
        total = summed(2)
        y0.wait_recv()
        out_ref[low] = total + by[0].astype(jnp.float32)
        total = summed(3)
        y1.wait_recv()
        out_ref[high] = total + by[1].astype(jnp.float32)
    for copy in core + sent:
        copy.wait_send()


def scatter(partial, full, collective_id):
    count = 8 if full else 4
    rows, width = (partial.shape[0] // count, partial.shape[1])
    half = rows // 2
    low = jnp.bfloat16
    return pl.pallas_call(
        functools.partial(scatter_kernel, full),
        out_shape=jax.ShapeDtypeStruct((rows, width), jnp.float32),
        in_specs=[VMEM],
        out_specs=VMEM,
        scratch_shapes=[
            pltpu.VMEM((count // 2, rows, width), low),
            pltpu.VMEM((2, half, width), low),
            pltpu.VMEM((2, half, width), low),
            pltpu.VMEM((half, width), low),
            pltpu.VMEM((half, width), low),
            pltpu.VMEM((2, half, width), low),
            pltpu.VMEM((2, half, width), low),
            pltpu.VMEM((half, width), low),
            pltpu.VMEM((half, width), low),
            pltpu.SemaphoreType.DMA((8,)),
            pltpu.SemaphoreType.DMA((8,)),
            pltpu.SemaphoreType.DMA((6,)),
            pltpu.SemaphoreType.DMA((6,)),
        ],
        name="scatter_full" if full else "scatter_half",
        cost_estimate=EIGHTEEN_US,
        compiler_params=pltpu.CompilerParams(
            collective_id=collective_id, has_side_effects=True, vmem_limit_bytes=40 * 2**20
        ),
    )(lowered(partial).reshape(count, rows, width))


def scan_kernel(
    high, reverse, decay_ref, drive_ref, end_ref, state_ref, carry_ref, cum, strips, sendbuf, recvbuf, send_sem, recv_sem
):
    rows, width = decay_ref.shape
    strands = 8
    steps = rows // strands
    lanes = 128
    blocks = width // lanes
    seq = lax.axis_index("seq")
    tp = lax.axis_index("tp")
    lo = lax.rem(seq, LO)
    mine = seq // LO
    peers = [(lax.rem(mine + k, high) * LO + lo, tp) for k in range(1, high)]
    greet(peers)
    for n in range(blocks):
        cum[n] = decay_ref[:, n * lanes : (n + 1) * lanes]
        strips[n] = drive_ref[:, n * lanes : (n + 1) * lanes]

    def step(i, carry):
        r = steps - 1 - i if reverse else i
        at = pl.ds(r, strands, stride=steps)
        new = []
        for n in range(blocks):
            a = cum[n, at, :]
            product_now = carry[2 * n] * a
            state_now = carry[2 * n + 1] * a + strips[n, at, :]
            cum[n, at, :] = product_now
            strips[n, at, :] = state_now
            new += [product_now, state_now]
        return tuple(new)

    ones = jnp.ones((strands, lanes), jnp.float32)
    ends = lax.fori_loop(0, steps, step, (ones, jnp.zeros_like(ones)) * blocks, unroll=8)
    strand_order = list(range(strands - 1, -1, -1)) if reverse else list(range(strands))
    before = {}
    for n in range(blocks):
        total_a = jnp.ones((1, lanes), jnp.float32)
        total_h = jnp.zeros((1, lanes), jnp.float32)
        for k in strand_order:
            before[n, k] = (total_a, total_h)
            a, h = (ends[2 * n][k : k + 1], ends[2 * n + 1][k : k + 1])
            total_h = a * total_h + h
            total_a = a * total_a
        scale = end_ref[0:1, n * lanes : (n + 1) * lanes]
        sendbuf[n, 0:1, :] = total_a * scale
        sendbuf[n, 1:2, :] = total_h * scale
        sendbuf[n, 2:8, :] = jnp.zeros((6, lanes), jnp.float32)
    copies = []
    for k, peer in enumerate(peers):
        copy = remote(sendbuf, recvbuf.at[k], send_sem, recv_sem, k, peer)
        copy.start()
        copies.append(copy)
    for copy in copies:
        copy.wait_recv()
    for n in range(blocks):
        carry = jnp.zeros((1, lanes), jnp.float32)
        for turn in range(high - 1):
            plane = high - 1 - turn if reverse else turn
            away = lax.rem(mine - plane + high, high)
            reached = plane > mine if reverse else plane < mine
            got = recvbuf[jnp.where(reached, away - 1, 0), n]
            carry = jnp.where(reached, got[0:1] * carry + got[1:2], carry)
        span = pl.ds(n * lanes, lanes)
        carry_ref[:, span] = jnp.broadcast_to(carry, (carry_ref.shape[0], lanes))
        for k in range(strands):
            enter = before[n, k][0] * carry + before[n, k][1]
            at = pl.ds(k * steps, steps)
            state_ref[at, span] = strips[n, at, :] + cum[n, at, :] * enter
    for copy in copies:
        copy.wait_send()


def plane_scan(decay, drive, end_scale, high, reverse, collective_id):
    rows, width = decay.shape
    return pl.pallas_call(
        functools.partial(scan_kernel, high, reverse),
        out_shape=(
            jax.ShapeDtypeStruct((rows, width), jnp.float32),
            jax.ShapeDtypeStruct((8, width), jnp.float32),
        ),
        in_specs=[VMEM] * 3,
        out_specs=(VMEM, VMEM),
        scratch_shapes=[
            pltpu.VMEM((width // 128, rows, 128), jnp.float32),
            pltpu.VMEM((width // 128, rows, 128), jnp.float32),
            pltpu.VMEM((width // 128, 8, 128), jnp.float32),
            pltpu.VMEM((high - 1, width // 128, 8, 128), jnp.float32),
            pltpu.SemaphoreType.DMA((high - 1,)),
            pltpu.SemaphoreType.DMA((high - 1,)),
        ],
        name="scan_back" if reverse else "scan",
        cost_estimate=TEN_US,
        compiler_params=pltpu.CompilerParams(
            collective_id=collective_id, has_side_effects=True, vmem_limit_bytes=32 * 2**20
        ),
    )(decay, drive, end_scale)


def small_kernel(high, gains_ref, rest_ref, gains_out, rest_out, gbuf, rbuf, ghold, rhold, gpair, rpair, send_sem, recv_sem):
    a, b, c, across_a, across_b, across_c = cube()
    seq = lax.axis_index("seq")
    tp = lax.axis_index("tp")
    mine = seq // LO
    peers = [(lax.rem(mine + k, high) * LO + a, tp) for k in range(1, high)]
    greet(peers + [across_a, across_b, across_c])
    copies = []
    for k, peer in enumerate(peers):
        for n, (src, dst) in enumerate(((gains_ref, gbuf.at[k]), (rest_ref, rbuf.at[k]))):
            copy = remote(src, dst, send_sem, recv_sem, 2 * k + n, peer)
            copy.start()
            copies.append(copy)
    for copy in copies:
        copy.wait_recv()
    gains = gains_ref[...]
    rest = rest_ref[...]
    for k in range(high - 1):
        gains = gains + gbuf[k]
        rest = rest + rbuf[k]
    rhold[...] = rest
    slot = 2 * (high - 1)
    swap = remote(rhold, rpair, send_sem, recv_sem, slot, across_a)
    swap.start()
    copies.append(swap)
    for n, device in enumerate((across_a, across_b, across_c)):
        ghold[n] = gains
        copy = remote(ghold.at[n], gpair.at[n], send_sem, recv_sem, slot + 1 + n, device)
        copy.start()
        copies.append(copy)
        copy.wait_recv()
        gains = gains + gpair[n]
    swap.wait_recv()
    gains_out[...] = gains
    other = rpair[...]
    width = rest.shape[1]
    rest_out[:, :width] = jnp.where(a == 0, rest, other)
    rest_out[:, width:] = jnp.where(a == 0, other, rest)
    for copy in copies:
        copy.wait_send()


def small_sums(gains, rest, high, collective_id):
    count = 2 * (high - 1) + 4
    return pl.pallas_call(
        functools.partial(small_kernel, high),
        out_shape=(
            jax.ShapeDtypeStruct(gains.shape, jnp.float32),
            jax.ShapeDtypeStruct((rest.shape[0], LO * rest.shape[1]), jnp.float32),
        ),
        in_specs=[VMEM] * 2,
        out_specs=(VMEM, VMEM),
        scratch_shapes=[
            pltpu.VMEM((high - 1, *gains.shape), jnp.float32),
            pltpu.VMEM((high - 1, *rest.shape), jnp.float32),
            pltpu.VMEM((3, *gains.shape), jnp.float32),
            pltpu.VMEM(rest.shape, jnp.float32),
            pltpu.VMEM((3, *gains.shape), jnp.float32),
            pltpu.VMEM(rest.shape, jnp.float32),
            pltpu.SemaphoreType.DMA((count,)),
            pltpu.SemaphoreType.DMA((count,)),
        ],
        name="small_sums",
        cost_estimate=TEN_US,
        compiler_params=pltpu.CompilerParams(collective_id=collective_id, has_side_effects=True),
    )(gains, rest)


def stacked_by_low(mine, other):
    lo = lax.rem(lax.axis_index("seq"), LO)
    return jnp.stack([jnp.where(lo == 0, mine, other), jnp.where(lo == 0, other, mine)])


def swap_low(block):
    count = lax.axis_size("seq")
    return lax.ppermute(block, "seq", [(s, s // LO * LO + (1 - s % LO)) for s in range(count)])


def high_groups():
    count = lax.axis_size("seq")
    return [[h * LO + l for h in range(count // LO)] for l in range(LO)]


def gather_weight(halves):
    lo = lax.rem(lax.axis_index("seq"), LO)
    kept = jnp.where(lo == 0, halves[0], halves[1])
    given = jnp.where(lo == 0, halves[1], halves[0])
    both = stacked_by_low(kept, swap_low(given))
    rows = both.shape[1]
    return lax.all_gather(
        both.reshape(LO * rows, both.shape[2]),
        "seq",
        axis=0,
        tiled=True,
        axis_index_groups=high_groups(),
    )


def reduce_weight(grad):
    lo = lax.rem(lax.axis_index("seq"), LO)
    both = lax.psum_scatter(
        lowered(grad), "seq", scatter_dimension=0, tiled=True, axis_index_groups=high_groups()
    )
    rows = both.shape[0] // LO
    both = both.reshape(LO, rows, both.shape[1])
    kept = jnp.where(lo == 0, both[0], both[1])
    given = jnp.where(lo == 0, both[1], both[0])
    return stacked_by_low(kept, swap_low(given))


def split_columns(block):
    width = block.shape[1] // LO
    return [block[:, l * width : (l + 1) * width] for l in range(LO)]


def joined(blocks):
    return jnp.concatenate([blocks[l] for l in range(LO)], axis=1).astype(jnp.float32)


def dense_forward(stream, gain, weights, cid):
    gate_up, down = weights
    width = down.shape[1]
    normed = gather(lowered(rms_norm(stream, gain)), True, cid["gather_full"])
    both = product(normed, gate_up)
    hidden = lowered(gated(both[:, :width], both[:, width:]))
    out = scatter(product_right(hidden, down), True, cid["scatter_full"])
    return (out, (normed, both, hidden))


def dense_backward(stream, gain, grad_out, kept, weights, cid):
    gate_up, down = weights
    width = down.shape[1]
    normed, both, hidden = kept
    grad_low = gather(lowered(grad_out), True, cid["gather_full"])
    grad_down = product_left(grad_low, hidden)
    grad_hidden = product(grad_low, down)
    gate_grad, up_grad = jax.vjp(gated, both[:, :width], both[:, width:])[1](grad_hidden)
    both_low = jnp.concatenate([lowered(gate_grad), lowered(up_grad)], axis=1)
    grad_both = product_left(normed, both_low)
    partial = product_right(both_low, gate_up)
    partial, grad_both, grad_down = lax.optimization_barrier(
        (lowered(partial), lowered(grad_both), lowered(grad_down))
    )
    grad_normed = scatter(partial, True, cid["scatter_full"])
    stream_grad, gain_grad = jax.vjp(rms_norm, stream, gain)[1](grad_normed)
    return (grad_out + stream_grad, gain_grad, grad_both, grad_down)


def block_product(values, weight):
    block_width = weight.shape[0]
    blocks = weight.shape[1] // block_width
    return jnp.concatenate(
        [
            product_right(
                values[:, n * block_width : (n + 1) * block_width],
                weight[:, n * block_width : (n + 1) * block_width],
            )
            for n in range(blocks)
        ],
        axis=1,
    )


def block_grads(values, weight, upstream):
    block_width = weight.shape[0]
    cuts = [slice(n * block_width, (n + 1) * block_width) for n in range(weight.shape[1] // block_width)]
    return (
        jnp.concatenate([product_left(upstream[:, s], values[:, s]) for s in cuts], axis=1),
        jnp.concatenate([product(upstream[:, s], weight[:, s]) for s in cuts], axis=1),
    )


def shifted(block, distance):
    count = lax.axis_size("seq")
    route = [(i - distance, i) for i in range(count) if 0 <= i - distance < count]
    return lax.ppermute(block, "seq", route)


def score_block(query_rot, keys_ext, allowed, score_scale):
    raw = jnp.einsum("qhd,kd->hqk", query_rot, keys_ext, preferred_element_type=jnp.float32)
    return jnp.where(allowed[None], raw * score_scale, -1e30)


CIDS = {
    "gather_full": 0,
    "gather_half": 1,
    "scatter_full": 2,
    "scatter_half": 3,
    "scan": 4,
    "scan_back": 5,
    "scatter_wide": 6,
    "small_sums": 7,
    "gather_narrow": 8,
}


def dense_weights(gate_part, up_part, down_part, *more):
    pieces = [split_columns(part) for part in (gate_part, up_part, *more)]
    wide = gather_weight([jnp.concatenate(each, axis=1) for each in zip(*pieces)])
    down = gather_weight(split_columns(down_part.T))
    width = 2 * down.shape[1]
    return (wide[:, :width], down) + ((wide[:, width:],) if more else ())


def dense_grads(grad_both, grad_down):
    width = grad_down.shape[1]
    both = reduce_weight(jnp.concatenate([grad_both, grad_down], axis=1))
    return (
        joined(both[:, :, :width]),
        joined(both[:, :, width : 2 * width]),
        joined(both[:, :, 2 * width :]).T,
    )


def gather_whole(part):
    count = lax.axis_size("seq")
    lanes = lax.all_gather(part, "seq", axis_index_groups=high_groups())
    other = swap_low(lanes)
    lo = lax.rem(lax.axis_index("seq"), LO)
    both = jnp.stack([jnp.where(lo == 0, lanes, other), jnp.where(lo == 0, other, lanes)], axis=1)
    return both.reshape(count * part.shape[0], part.shape[1])


def reduce_whole(blocks):
    count, rows, width = blocks.shape
    lo = lax.rem(lax.axis_index("seq"), LO)
    pairs = blocks.reshape(count // LO, LO, rows, width)
    kept = jnp.where(lo == 0, pairs[:, 0], pairs[:, 1])
    given = jnp.where(lo == 0, pairs[:, 1], pairs[:, 0])
    total = lowered(kept.astype(jnp.float32) + swap_low(given).astype(jnp.float32))
    return lax.psum_scatter(
        total.reshape(-1, width),
        "seq",
        scatter_dimension=0,
        tiled=True,
        axis_index_groups=high_groups(),
    )


def local(
    tokens,
    cotangent,
    doc_lengths,
    norm_gains,
    input_branch,
    gate_branch,
    conv_taps,
    conv_bias,
    recur_gate,
    input_gate,
    gate_biases,
    decay_param,
    recur_output,
    dense_gate_one,
    dense_up_one,
    dense_down_one,
    query_weight,
    keyvalue_weight,
    attention_out,
    dense_gate_two,
    dense_up_two,
    dense_down_two,
):
    cid = CIDS
    shard_rows = tokens.shape[0]
    seq = lax.axis_index("seq")
    tp = lax.axis_index("tp")
    lo = lax.rem(seq, LO)
    high = lax.axis_size("seq") // LO
    ways = lax.axis_size("tp")
    own_rows = shard_rows // ways
    plane_rows = shard_rows * LO
    channels = conv_bias.shape[0] // LO
    leading = CONV - 1
    halo_shards = WINDOW // shard_rows
    first_slot = seq * shard_rows
    plane_slot = (seq // LO) * plane_rows
    own_slot = first_slot + tp * own_rows
    valid = layout(doc_lengths, own_slot, own_rows)[3]
    segment, position, _, _ = layout(doc_lengths, first_slot, shard_rows)
    plane_reset = layout(doc_lengths, plane_slot, plane_rows)[2]
    conv_segment = layout(doc_lengths, plane_slot - leading, plane_rows + leading)[0]
    key_segment = layout(
        doc_lengths, first_slot - halo_shards * shard_rows, (halo_shards + 1) * shard_rows
    )[0]

    def ours(block, axis):
        return lax.dynamic_slice_in_dim(block, lo * channels, channels, axis)

    taps, bias = (ours(conv_taps, 1), ours(conv_bias, 0))
    bias_pair, decay_values = (ours(gate_biases, 1), ours(decay_param, 0))

    gate_rows = recur_gate.shape[1]
    weight_rows = input_branch.shape[0]
    ins = zip(split_columns(input_branch), split_columns(gate_branch))
    gates = zip(split_columns(recur_gate.T), split_columns(input_gate.T))
    first = gather_weight(
        [
            jnp.concatenate(
                [jnp.concatenate(pair, axis=1), jnp.concatenate(gate, axis=1)], axis=0
            )
            for pair, gate in zip(ins, gates)
        ]
    ).reshape(high * LO, weight_rows + gate_rows, 2 * channels)
    in_full = first[:, :weight_rows].reshape(-1, 2 * channels)
    recur_full = first[:, weight_rows:, :channels].reshape(-1, channels)
    input_gate_full = first[:, weight_rows:, channels:].reshape(-1, channels)
    *weights_one, output_full = dense_weights(
        dense_gate_one, dense_up_one, dense_down_one, recur_output.T
    )

    stream_in = lax.dynamic_slice_in_dim(tokens, tp * own_rows, own_rows, 0).astype(jnp.float32)
    normed_one = gather(lowered(rms_norm(stream_in, norm_gains[0])), True, cid["gather_full"])
    normed_one, query_weight, keyvalue_weight, attention_out = lax.optimization_barrier(
        (normed_one, query_weight, keyvalue_weight, attention_out)
    )
    both = product(normed_one, in_full)
    both, dense_gate_two, dense_up_two, dense_down_two = lax.optimization_barrier(
        (both, dense_gate_two, dense_up_two, dense_down_two)
    )

    keyvalue_part = keyvalue_weight[None]
    for step in (1, 2):
        other = lax.ppermute(keyvalue_part, "tp", [(i, i ^ step) for i in range(ways)])
        low_bit = lax.rem(tp // step, 2)
        keyvalue_part = jnp.concatenate(
            [
                jnp.where(low_bit == 0, keyvalue_part, other),
                jnp.where(low_bit == 0, other, keyvalue_part),
            ],
            axis=0,
        )
    keyvalue_part = keyvalue_part.reshape(weight_rows, keyvalue_weight.shape[1])
    third = gather_whole(
        jnp.concatenate([query_weight, attention_out.T, keyvalue_part], axis=1)
    )
    query_width = query_weight.shape[1]
    attn_width = attention_out.shape[0]
    query_full = third[:, :query_width]
    attn_full = third[:, query_width : query_width + attn_width]
    keyvalue_full = third[:, query_width + attn_width :]
    weights_two = dense_weights(dense_gate_two, dense_up_two, dense_down_two)

    branch = both[:, :channels]
    gating = both[:, channels:]
    rim = shifted(branch[plane_rows - leading :], LO)
    branch_ext = jnp.concatenate([rim, branch], axis=0)
    conv_local = functools.partial(convolve, segment=conv_segment)
    conv_out, conv_pull = jax.vjp(conv_local, branch_ext, taps, bias)
    conv_low = lowered(conv_out)
    recur_raw = block_product(conv_low, recur_full)
    input_raw = block_product(conv_low, input_gate_full)
    rate_local = functools.partial(coefficients, reset=plane_reset)
    (decay, drive), rate_pull = jax.vjp(
        rate_local, recur_raw, input_raw, conv_out, bias_pair, decay_values
    )
    ones = jnp.ones((8, channels), jnp.float32)
    state, state_in = plane_scan(decay, drive, ones, high, False, cid["scan"])
    gate_act, gate_pull = jax.vjp(jax.nn.gelu, gating)
    mixed = lowered(state * gate_act)
    stream_one = stream_in + scatter(product_right(mixed, output_full), True, cid["scatter_full"])

    dense_out, kept_one = dense_forward(stream_one, norm_gains[1], weights_one, cid)
    stream_two = stream_one + dense_out

    normed_own = lowered(rms_norm(stream_two, norm_gains[2]))
    normed_three = gather(normed_own, False, cid["gather_half"])
    query = product(normed_three, query_full)
    keyval = product(normed_three, keyvalue_full)
    local_heads = query.shape[1] // HD
    query_heads = query.reshape(shard_rows, local_heads, HD)
    rotate_here = functools.partial(rotate, position=position)
    query_rot = lowered(rotate_here(query_heads))
    key_rot = lowered(rotate_here(keyval[:, :HD]))
    packed = jnp.concatenate([key_rot, lowered(keyval[:, HD:])], axis=1)
    earlier = [shifted(packed, offset) for offset in range(halo_shards, 0, -1)]
    extended = jnp.concatenate(earlier + [packed], axis=0)
    keys_ext = extended[:, :HD]
    values_ext = extended[:, HD:]
    query_slots = first_slot + jnp.arange(shard_rows, dtype=jnp.int32)
    key_slots = (
        first_slot
        - halo_shards * shard_rows
        + jnp.arange((halo_shards + 1) * shard_rows, dtype=jnp.int32)
    )
    distance = query_slots[:, None] - key_slots[None, :]
    allowed = (segment[:, None] == key_segment[None, :]) & (distance >= 0) & (distance < WINDOW)
    score_scale = HD ** (-0.5)
    scores = score_block(query_rot, keys_ext, allowed, score_scale)
    row_top = jnp.max(scores, axis=-1, keepdims=True)
    row_total = jnp.sum(jnp.exp(scores - row_top), axis=-1, keepdims=True)
    log_total = row_top + jnp.log(row_total)
    probs_low = lowered(jnp.exp(scores - row_top) / row_total)
    attended = lowered(
        jnp.einsum("hqk,kd->qhd", probs_low, values_ext, preferred_element_type=jnp.float32)
    ).reshape(shard_rows, local_heads * HD)
    stream_three = stream_two + scatter(
        product_right(attended, attn_full), False, cid["scatter_half"]
    )

    dense_out, kept_two = dense_forward(stream_three, norm_gains[3], weights_two, cid)
    stream_four = stream_three + dense_out
    out_own = lowered(stream_four * valid[:, None])
    layer_out = gather(out_own, False, cid["gather_half"])

    grad_stream = (
        lax.dynamic_slice_in_dim(cotangent, tp * own_rows, own_rows, 0).astype(jnp.float32)
        * valid[:, None]
    )
    grad_stream, gain_four, grad_both_two, grad_down_two = dense_backward(
        stream_three, norm_gains[3], grad_stream, kept_two, weights_two, cid
    )

    done_two = dense_grads(grad_both_two, grad_down_two)
    grad_attn_low = gather(lowered(grad_stream), False, cid["gather_half"])
    grad_attn_out = product_left(grad_attn_low, attended)
    grad_attended = lowered(product(grad_attn_low, attn_full)).reshape(
        shard_rows, local_heads, HD
    )
    scores = score_block(query_rot, keys_ext, allowed, score_scale)
    probs = jnp.exp(scores - log_total)
    grad_probs = jnp.einsum(
        "qhd,kd->hqk", grad_attended, values_ext, preferred_element_type=jnp.float32
    )
    grad_scores = lowered(
        probs * (grad_probs - jnp.sum(probs * grad_probs, axis=-1, keepdims=True)) * score_scale
    )
    grad_query_rot = jnp.einsum(
        "hqk,kd->qhd", grad_scores, keys_ext, preferred_element_type=jnp.float32
    )
    grad_keys = jnp.einsum(
        "hqk,qhd->kd", grad_scores, query_rot, preferred_element_type=jnp.float32
    )
    grad_values = jnp.einsum(
        "hqk,qhd->kd", lowered(probs), grad_attended, preferred_element_type=jnp.float32
    )
    grad_ext = jnp.concatenate([grad_keys, grad_values], axis=1)
    grad_own = grad_ext[halo_shards * shard_rows :]
    for offset in range(1, halo_shards + 1):
        grad_piece = grad_ext[
            (halo_shards - offset) * shard_rows : (halo_shards - offset + 1) * shard_rows
        ]
        grad_own = grad_own + shifted(lowered(grad_piece), -offset).astype(jnp.float32)
    key_pre_grad = jax.vjp(rotate_here, keyval[:, :HD])[1](grad_own[:, :HD])[0]
    query_pre_grad = jax.vjp(rotate_here, query_heads)[1](grad_query_rot)[0]
    grad_query_low = lowered(query_pre_grad).reshape(shard_rows, local_heads * HD)
    keyvalue_partial = jnp.concatenate([key_pre_grad, grad_own[:, HD:]], axis=1)
    grad_query = product_left(normed_three, grad_query_low)
    partial = lowered(
        jnp.concatenate([product_right(grad_query_low, query_full), keyvalue_partial], axis=1)
    )
    partial, grad_query, grad_attn_out = lax.optimization_barrier(
        (partial, lowered(grad_query), lowered(grad_attn_out))
    )
    summed = scatter(partial, False, cid["scatter_wide"])
    width = normed_own.shape[1]
    keyvalue_low = lowered(summed[:, width:])
    grad_normed = summed[:, :width] + product_right(keyvalue_low, keyvalue_full)
    keyvalue_grads = gather(keyvalue_low, False, cid["gather_narrow"])
    part_rows = keyvalue_weight.shape[0]
    ways_view = normed_three.reshape(shard_rows, high * LO, ways, part_rows)
    ours_only = lax.dynamic_slice_in_dim(ways_view, tp, 1, 2).reshape(shard_rows, -1)
    grad_keyvalue = lowered(product_left(ours_only, keyvalue_grads))
    attn_wire = jnp.concatenate([grad_query, grad_attn_out], axis=1)
    attn_wire = attn_wire.reshape(high * LO, weight_rows, attn_wire.shape[1])
    keyvalue_wire = grad_keyvalue.reshape(high * LO, -1, attn_wire.shape[2])
    done_attn = reduce_whole(jnp.concatenate([attn_wire, keyvalue_wire], axis=1))
    stream_grad, gain_three = jax.vjp(rms_norm, stream_two, norm_gains[2])[1](grad_normed)
    grad_stream = grad_stream + stream_grad

    grad_stream, gain_two, grad_both_one, grad_down_one = dense_backward(
        stream_one, norm_gains[1], grad_stream, kept_one, weights_one, cid
    )

    done_one = dense_grads(grad_both_one, grad_down_one)
    grad_stream, done_two = lax.optimization_barrier((grad_stream, done_two))
    grad_out_low = gather(lowered(grad_stream), True, cid["gather_full"])
    grad_recur_out = product_left(grad_out_low, mixed)
    grad_mixed = product(grad_out_low, output_full)
    grad_mixed, done_attn = lax.optimization_barrier((grad_mixed, done_attn))
    grad_state = grad_mixed * gate_act
    grad_gating = lowered(gate_pull(grad_mixed * state)[0])
    decay_next = jnp.concatenate([decay[1:], jnp.ones((1, channels), jnp.float32)], axis=0)
    first_decay = jnp.broadcast_to(decay[:1], (8, channels))
    grad_drive, _ = plane_scan(decay_next, grad_state, first_decay, high, True, cid["scan_back"])
    state_prev = jnp.concatenate([state_in[:1], state[:-1]], axis=0)
    grad_decay = grad_drive * state_prev
    grad_recur_raw, grad_input_raw, grad_conv, grad_biases, grad_decay_param = rate_pull(
        (grad_decay, grad_drive)
    )
    grad_recur_gate, conv_back_recur = block_grads(conv_low, recur_full, lowered(grad_recur_raw))
    grad_input_gate, conv_back_input = block_grads(
        conv_low, input_gate_full, lowered(grad_input_raw)
    )
    grad_branch_ext, grad_taps, grad_conv_bias = conv_pull(
        grad_conv + conv_back_recur + conv_back_input
    )
    returned_rim = shifted(grad_branch_ext[:leading], -LO)
    grad_branch = grad_branch_ext[leading:] + jnp.pad(
        returned_rim, ((plane_rows - leading, 0), (0, 0))
    )
    both_low = jnp.concatenate([lowered(grad_branch), grad_gating], axis=1)
    grad_in = product_left(normed_one, both_low)
    partial = lowered(product_right(both_low, in_full))
    partial, grad_in, grad_recur_out = lax.optimization_barrier(
        (partial, lowered(grad_in), lowered(grad_recur_out))
    )
    grad_normed = scatter(partial, True, cid["scatter_full"])
    stream_grad, gain_one = jax.vjp(rms_norm, stream_in, norm_gains[0])[1](grad_normed)
    input_own = grad_stream + stream_grad
    input_grad = gather(lowered(input_own), False, cid["gather_half"]).astype(jnp.float32)

    in_grad = reduce_weight(grad_in)
    rest_grad = jnp.concatenate(
        [
            grad_recur_out.reshape(high * LO, weight_rows, channels),
            lowered(grad_recur_gate).reshape(high * LO, gate_rows, channels),
            lowered(grad_input_gate).reshape(high * LO, gate_rows, channels),
        ],
        axis=1,
    )
    rest_grad = joined(reduce_weight(rest_grad.reshape(-1, channels))).T
    gains_sum, small = small_sums(
        jnp.concatenate(
            [jnp.stack([gain_one, gain_two, gain_three, gain_four]), jnp.zeros_like(norm_gains)]
        ),
        jnp.concatenate(
            [grad_taps, grad_conv_bias[None], grad_biases, grad_decay_param[None]], axis=0
        ),
        high,
        cid["small_sums"],
    )
    gains_sum = gains_sum[: norm_gains.shape[0]]
    return (
        layer_out,
        input_grad,
        gains_sum,
        joined(in_grad[:, :, :channels]),
        joined(in_grad[:, :, channels:]),
        small[:CONV],
        small[CONV],
        rest_grad[:, weight_rows : weight_rows + gate_rows],
        rest_grad[:, weight_rows + gate_rows :],
        small[CONV + 1 : CONV + 3],
        small[CONV + 3],
        rest_grad[:, :weight_rows],
        *done_one,
        done_attn[:weight_rows, :query_width].astype(jnp.float32),
        done_attn[weight_rows:].reshape(keyvalue_weight.shape).astype(jnp.float32),
        done_attn[:weight_rows, query_width:].astype(jnp.float32).T,
        *done_two,
    )


def solution(mesh):
    placed = (
        P("seq", None),
        P("seq", None),
        P(),
        P(),
        P("seq", "tp"),
        P("seq", "tp"),
        P(None, "tp"),
        P("tp"),
        P("tp", "seq"),
        P("tp", "seq"),
        P(None, "tp"),
        P("tp"),
        P("tp", "seq"),
        P("seq", "tp"),
        P("seq", "tp"),
        P("tp", "seq"),
        P("seq", "tp"),
        P(("seq", "tp"), None),
        P("tp", "seq"),
        P("seq", "tp"),
        P("seq", "tp"),
        P("tp", "seq"),
    )
    return jax.shard_map(
        local,
        mesh=mesh,
        in_specs=placed,
        out_specs=(
            P("seq", None),
            P("seq", None),
            P(),
            P("seq", "tp"),
            P("seq", "tp"),
            P(None, "tp"),
            P("tp"),
            P("tp", "seq"),
            P("tp", "seq"),
            P(None, "tp"),
            P("tp"),
            P("tp", "seq"),
            P("seq", "tp"),
            P("seq", "tp"),
            P("tp", "seq"),
            P("seq", "tp"),
            P(("seq", "tp"), None),
            P("tp", "seq"),
            P("seq", "tp"),
            P("seq", "tp"),
            P("tp", "seq"),
        ),
        check_vma=False,
    )
```

```python
import functools

import jax
import jax.numpy as jnp
from jax import lax
from jax.experimental import pallas as pl
from jax.experimental.pallas import tpu as pltpu
from jax.sharding import PartitionSpec as P

HD = 128
CONV = 4
WINDOW = 1024


def product(left, right):
    return jnp.dot(left, right, preferred_element_type=jnp.float32)


def product_left(left, right):
    return lax.dot_general(
        left, right, (((0,), (0,)), ((), ())), preferred_element_type=jnp.float32
    )


def product_right(left, right):
    return lax.dot_general(
        left, right, (((1,), (1,)), ((), ())), preferred_element_type=jnp.float32
    )


def lowered(values):
    return values.astype(jnp.bfloat16)


def rms_norm(values, gain):
    return values * lax.rsqrt(jnp.mean(values * values, axis=-1, keepdims=True) + 1e-06) * gain


def gated(gate_values, up_values):
    return jax.nn.gelu(gate_values) * up_values


def layout(doc_lengths, first_slot, count):
    ends = jnp.cumsum(doc_lengths, dtype=jnp.int32)
    slots = first_slot + jnp.arange(count, dtype=jnp.int32)
    passed = slots[:, None] >= ends[None, :]
    segment = jnp.sum(passed.astype(jnp.int32), axis=1)
    begin = jnp.max(jnp.where(passed, ends[None, :], 0), axis=1)
    segment = jnp.where(slots < 0, -1, segment)
    position = slots - begin
    reset = (slots != begin).astype(jnp.float32)
    valid = (segment < doc_lengths.shape[0]).astype(jnp.float32)
    return (segment, position, reset, valid)


def rotate(values, position):
    half_width = values.shape[-1] // 2
    frequency = 10000.0 ** (-jnp.arange(half_width, dtype=jnp.float32) / half_width)
    angle = position.astype(jnp.float32)[:, None] * frequency[None, :]
    if values.ndim == 3:
        angle = angle[:, None, :]
    cosine = jnp.cos(angle)
    sine = jnp.sin(angle)
    first_half = values[..., :half_width]
    second_half = values[..., half_width:]
    return jnp.concatenate(
        [first_half * cosine - second_half * sine, second_half * cosine + first_half * sine],
        axis=-1,
    )


def convolve(extended, taps, bias, segment):
    leading = CONV - 1
    total_rows = extended.shape[0] - leading
    result = bias[None, :] + taps[0][None, :] * extended[leading:]
    for lag_index in range(1, CONV):
        same = (
            segment[leading:] == segment[leading - lag_index : leading - lag_index + total_rows]
        ).astype(jnp.float32)
        result = (
            result
            + same[:, None]
            * taps[lag_index][None, :]
            * extended[leading - lag_index : leading - lag_index + total_rows]
        )
    return result


def coefficients(recur_raw, input_raw, conv_values, bias_pair, decay_values, reset):
    recur_rate = jax.nn.sigmoid(recur_raw + bias_pair[0][None, :])
    input_rate = jax.nn.sigmoid(input_raw + bias_pair[1][None, :])
    log_decay = -8.0 * recur_rate * jax.nn.softplus(-decay_values)[None, :]
    multiplier = jnp.sqrt(jnp.maximum(-jnp.expm1(2.0 * log_decay), 0.01))
    return (jnp.exp(log_decay) * reset[:, None], multiplier * input_rate * conv_values)


def combine_state(earlier, later):
    return (earlier[0] * later[0], later[0] * earlier[1] + later[1])


MESH = pl.DeviceIdType.MESH
LO = 2
EIGHTEEN_US = pl.CostEstimate(flops=0, bytes_accessed=60_000_000, transcendentals=0)
TEN_US = pl.CostEstimate(flops=0, bytes_accessed=33_000_000, transcendentals=0)
ANY = pl.BlockSpec(memory_space=pl.ANY)
VMEM = pl.BlockSpec(memory_space=pltpu.VMEM)


def cube():
    seq = lax.axis_index("seq")
    tp = lax.axis_index("tp")
    a = lax.rem(seq, LO)
    b = tp // 2
    c = lax.rem(tp, 2)
    across_a = (seq - a + 1 - a, tp)
    across_b = (seq, (1 - b) * 2 + c)
    across_c = (seq, b * 2 + 1 - c)
    return (a, b, c, across_a, across_b, across_c)


def greet(devices):
    barrier = pltpu.get_barrier_semaphore()
    for device in devices:
        pl.semaphore_signal(barrier, inc=1, device_id=device, device_id_type=MESH)
    pl.semaphore_wait(barrier, len(devices))


def remote(src, dst, send_sem, recv_sem, slot, device):
    return pltpu.make_async_remote_copy(
        src_ref=src,
        dst_ref=dst,
        send_sem=send_sem.at[slot],
        recv_sem=recv_sem.at[slot],
        device_id=device,
        device_id_type=MESH,
    )


def in_turn(*runs):
    runs = list(runs)
    while runs:
        for run in list(runs):
            if next(run, "end") == "end":
                runs.remove(run)


def neighbours(full):
    across_a, across_b, across_c = cube()[3:]
    return [across_c, across_b] + ([across_a] if full else [])


def gather_steps(full, in_ref, out_ref, send_sem, recv_sem, local_sem):
    a, b, c, across_a, across_b, across_c = cube()
    half = in_ref.shape[0] // 2

    def index(pa, pb, pc):
        return pa * 4 + pb * 2 + pc if full else pb * 2 + pc

    me, an, bn, dn = (
        index(a, b, c),
        index(1 - a, b, c),
        index(a, 1 - b, c),
        index(1 - a, 1 - b, c),
    )
    low, high = (pl.ds(0, half), pl.ds(half, half))
    sent = {}

    def go(slot, src, dst, device):
        copy = remote(src, dst, send_sem, recv_sem, slot, device)
        copy.start()
        sent[slot] = copy

    def own(slot, part, device):
        go(slot, in_ref.at[part], out_ref.at[me, part], device)

    def onward(slot, block, part, device):
        go(slot, out_ref.at[block, part], out_ref.at[block, part], device)

    if full:
        own(0, low, across_a)
    own(1, high, across_b)
    if full:
        own(2, high, across_a)
    own(3, low, across_b)
    go(4, in_ref, out_ref.at[me], across_c)
    mine = pltpu.make_async_copy(in_ref, out_ref.at[me], local_sem)
    mine.start()
    yield
    if full:
        sent[0].wait_recv()
        onward(5, an, low, across_b)
        onward(6, an, low, across_c)
        yield
    sent[1].wait_recv()
    if full:
        onward(7, bn, high, across_a)
    onward(8, bn, high, across_c)
    yield
    if full:
        sent[2].wait_recv()
        onward(9, an, high, across_c)
        yield
    sent[3].wait_recv()
    onward(10, bn, low, across_c)
    yield
    if full:
        sent[5].wait_recv()
        onward(11, dn, low, across_c)
        yield
        sent[7].wait_recv()
        onward(12, dn, high, across_c)
        yield
    for slot in (4, 6, 8, 9, 10, 11, 12):
        if slot in sent:
            sent[slot].wait_recv()
    for copy in sent.values():
        copy.wait_send()
    mine.wait()


def gather_kernel(full, count, *refs):
    in_refs, out_refs = (refs[:count], refs[count : 2 * count])
    send_sem, recv_sem, local_sem = refs[2 * count :]
    greet(neighbours(full))
    in_turn(
        *[
            gather_steps(
                full, in_refs[k], out_refs[k], send_sem.at[k], recv_sem.at[k], local_sem.at[k]
            )
            for k in range(count)
        ]
    )


def gather(blocks, full, collective_id):
    ways = 8 if full else 4
    count = len(blocks)
    results = pl.pallas_call(
        functools.partial(gather_kernel, full, count),
        out_shape=[
            jax.ShapeDtypeStruct((ways, *block.shape), block.dtype) for block in blocks
        ],
        in_specs=[ANY] * count,
        out_specs=[ANY] * count,
        scratch_shapes=[
            pltpu.SemaphoreType.DMA((count, 13)),
            pltpu.SemaphoreType.DMA((count, 13)),
            pltpu.SemaphoreType.DMA((count,)),
        ],
        name="gather_full" if full else "gather_half",
        cost_estimate=EIGHTEEN_US,
        compiler_params=pltpu.CompilerParams(collective_id=collective_id, has_side_effects=True),
    )(*blocks)
    return [
        result.reshape(ways * block.shape[0], block.shape[1])
        for result, block in zip(results, blocks)
    ]


def scatter_steps(
    full, part_ref, out_ref, cbuf, sx, sy, tx, ty, ax, by, rx, ry, csend, crecv, send_sem, recv_sem
):
    a, b, c, across_a, across_b, across_c = cube()
    half = part_ref.shape[1] // 2

    def index(pa, pb, pc):
        return pa * 4 + pb * 2 + pc if full else pb * 2 + pc

    def pair(pa, pb):
        return pa * 2 + pb if full else pb

    low, high = (pl.ds(0, half), pl.ds(half, half))
    if full:
        order = [
            (1 - a, 1 - b, low),
            (1 - a, 1 - b, high),
            (1 - a, b, low),
            (a, 1 - b, high),
            (a, 1 - b, low),
            (1 - a, b, high),
            (a, b, low),
            (a, b, high),
        ]
    else:
        order = [(a, 1 - b, low), (a, 1 - b, high), (a, b, low), (a, b, high)]
    core = []
    for k, (pa, pb, part) in enumerate(order):
        copy = remote(
            part_ref.at[index(pa, pb, 1 - c), part],
            cbuf.at[pair(pa, pb), part],
            csend,
            crecv,
            k,
            across_c,
        )
        copy.start()
        core.append(copy)
    yield

    def summed(k):
        pa, pb, part = order[k]
        core[k].wait_recv()
        return part_ref[index(pa, pb, c), part].astype(jnp.float32) + cbuf[
            pair(pa, pb), part
        ].astype(jnp.float32)

    sent = []

    def go(src, dst, slot, device):
        copy = remote(src, dst, send_sem, recv_sem, slot, device)
        copy.start()
        sent.append(copy)
        return copy

    if full:
        sx[0] = lowered(summed(0))
        x0 = go(sx.at[0], ax.at[0], 0, across_a)
        sy[0] = lowered(summed(1))
        y0 = go(sy.at[0], by.at[0], 1, across_b)
        yield
        sx[1] = lowered(summed(2))
        x1 = go(sx.at[1], ax.at[1], 2, across_a)
        sy[1] = lowered(summed(3))
        y1 = go(sy.at[1], by.at[1], 3, across_b)
        yield
        total = summed(4)
        x0.wait_recv()
        ty[...] = lowered(total + ax[0].astype(jnp.float32))
        last_y = go(ty, ry, 4, across_b)
        total = summed(5)
        y0.wait_recv()
        tx[...] = lowered(total + by[0].astype(jnp.float32))
        last_x = go(tx, rx, 5, across_a)
        yield
        total = summed(6)
        x1.wait_recv()
        total = total + ax[1].astype(jnp.float32)
        last_y.wait_recv()
        out_ref[low] = total + ry[...].astype(jnp.float32)
        total = summed(7)
        y1.wait_recv()
        total = total + by[1].astype(jnp.float32)
        last_x.wait_recv()
        out_ref[high] = total + rx[...].astype(jnp.float32)
        yield
    else:
        sy[0] = lowered(summed(0))
        y0 = go(sy.at[0], by.at[0], 1, across_b)
        sy[1] = lowered(summed(1))
        y1 = go(sy.at[1], by.at[1], 3, across_b)
        yield
        total = summed(2)
        y0.wait_recv()
        out_ref[low] = total + by[0].astype(jnp.float32)
        total = summed(3)
        y1.wait_recv()
        out_ref[high] = total + by[1].astype(jnp.float32)
        yield
    for copy in core + sent:
        copy.wait_send()


def scatter_kernel(full, count, *refs):
    greet(neighbours(full))
    in_turn(
        *[
            scatter_steps(full, refs[k], refs[count + k], *refs[2 * count + 13 * k :][:13])
            for k in range(count)
        ]
    )


def scatter_scratch(ways, rows, width):
    half = rows // 2
    shapes = [(ways // 2, rows, width)] + [(2, half, width)] * 2 + [(half, width)] * 2
    shapes += [(2, half, width)] * 2 + [(half, width)] * 2
    return [pltpu.VMEM(shape, jnp.bfloat16) for shape in shapes] + [
        pltpu.SemaphoreType.DMA((k,)) for k in (8, 8, 6, 6)
    ]


def scatter(partials, full, collective_id):
    ways = 8 if full else 4
    count = len(partials)
    rows = partials[0].shape[0] // ways
    scratch = []
    for partial in partials:
        scratch += scatter_scratch(ways, rows, partial.shape[1])
    return pl.pallas_call(
        functools.partial(scatter_kernel, full, count),
        out_shape=[
            jax.ShapeDtypeStruct((rows, partial.shape[1]), jnp.float32) for partial in partials
        ],
        in_specs=[VMEM] * count,
        out_specs=[VMEM] * count,
        scratch_shapes=scratch,
        name="scatter_full" if full else "scatter_half",
        cost_estimate=EIGHTEEN_US,
        compiler_params=pltpu.CompilerParams(
            collective_id=collective_id, has_side_effects=True, vmem_limit_bytes=48 * 2**20
        ),
    )(*[lowered(partial).reshape(ways, rows, -1) for partial in partials])


def scan_kernel(
    high, reverse, decay_ref, drive_ref, end_ref, state_ref, carry_ref, cum, strips, sendbuf, recvbuf, send_sem, recv_sem
):
    rows, width = decay_ref.shape
    strands = 8
    steps = rows // strands
    lanes = 128
    blocks = width // lanes
    mine = lax.axis_index("seq") // LO
    peers = high_peers(high)
    greet(peers)
    for n in range(blocks):
        cum[n] = decay_ref[:, n * lanes : (n + 1) * lanes]
        strips[n] = drive_ref[:, n * lanes : (n + 1) * lanes]

    def step(i, carry):
        r = steps - 1 - i if reverse else i
        at = pl.ds(r, strands, stride=steps)
        new = []
        for n in range(blocks):
            a = cum[n, at, :]
            product_now = carry[2 * n] * a
            state_now = carry[2 * n + 1] * a + strips[n, at, :]
            cum[n, at, :] = product_now
            strips[n, at, :] = state_now
            new += [product_now, state_now]
        return tuple(new)

    ones = jnp.ones((strands, lanes), jnp.float32)
    ends = lax.fori_loop(0, steps, step, (ones, jnp.zeros_like(ones)) * blocks, unroll=8)
    strand_order = list(range(strands - 1, -1, -1)) if reverse else list(range(strands))
    before = {}
    for n in range(blocks):
        total_a = jnp.ones((1, lanes), jnp.float32)
        total_h = jnp.zeros((1, lanes), jnp.float32)
        for k in strand_order:
            before[n, k] = (total_a, total_h)
            a, h = (ends[2 * n][k : k + 1], ends[2 * n + 1][k : k + 1])
            total_h = a * total_h + h
            total_a = a * total_a
        scale = end_ref[0:1, n * lanes : (n + 1) * lanes]
        sendbuf[n, 0:1, :] = total_a * scale
        sendbuf[n, 1:2, :] = total_h * scale
        sendbuf[n, 2:8, :] = jnp.zeros((6, lanes), jnp.float32)
    copies = []
    for k, peer in enumerate(peers):
        copy = remote(sendbuf, recvbuf.at[k], send_sem, recv_sem, k, peer)
        copy.start()
        copies.append(copy)
    for copy in copies:
        copy.wait_recv()
    for n in range(blocks):
        carry = jnp.zeros((1, lanes), jnp.float32)
        for turn in range(high - 1):
            plane = high - 1 - turn if reverse else turn
            away = lax.rem(mine - plane + high, high)
            reached = plane > mine if reverse else plane < mine
            got = recvbuf[jnp.where(reached, away - 1, 0), n]
            carry = jnp.where(reached, got[0:1] * carry + got[1:2], carry)
        span = pl.ds(n * lanes, lanes)
        carry_ref[:, span] = jnp.broadcast_to(carry, (carry_ref.shape[0], lanes))
        for k in range(strands):
            enter = before[n, k][0] * carry + before[n, k][1]
            at = pl.ds(k * steps, steps)
            state_ref[at, span] = strips[n, at, :] + cum[n, at, :] * enter
    for copy in copies:
        copy.wait_send()


def plane_scan(decay, drive, end_scale, high, reverse, collective_id):
    rows, width = decay.shape
    return pl.pallas_call(
        functools.partial(scan_kernel, high, reverse),
        out_shape=(
            jax.ShapeDtypeStruct((rows, width), jnp.float32),
            jax.ShapeDtypeStruct((8, width), jnp.float32),
        ),
        in_specs=[VMEM] * 3,
        out_specs=(VMEM, VMEM),
        scratch_shapes=[
            pltpu.VMEM((width // 128, rows, 128), jnp.float32),
            pltpu.VMEM((width // 128, rows, 128), jnp.float32),
            pltpu.VMEM((width // 128, 8, 128), jnp.float32),
            pltpu.VMEM((high - 1, width // 128, 8, 128), jnp.float32),
            pltpu.SemaphoreType.DMA((high - 1,)),
            pltpu.SemaphoreType.DMA((high - 1,)),
        ],
        name="scan_back" if reverse else "scan",
        cost_estimate=TEN_US,
        compiler_params=pltpu.CompilerParams(
            collective_id=collective_id, has_side_effects=True, vmem_limit_bytes=32 * 2**20
        ),
    )(decay, drive, end_scale)


def small_steps(high, gains_ref, rest_ref, gains_out, rest_out, gbuf, rbuf, ghold, rhold, gpair, rpair, send_sem, recv_sem):
    a, b, c, across_a, across_b, across_c = cube()
    peers = high_peers(high)
    copies = []
    for k, peer in enumerate(peers):
        for n, (src, dst) in enumerate(((gains_ref, gbuf.at[k]), (rest_ref, rbuf.at[k]))):
            copy = remote(src, dst, send_sem, recv_sem, 2 * k + n, peer)
            copy.start()
            copies.append(copy)
    yield
    for copy in copies:
        copy.wait_recv()
    gains = gains_ref[...]
    rest = rest_ref[...]
    for k in range(high - 1):
        gains = gains + gbuf[k]
        rest = rest + rbuf[k]
    rhold[...] = rest
    slot = 2 * (high - 1)
    swap = remote(rhold, rpair, send_sem, recv_sem, slot, across_a)
    swap.start()
    copies.append(swap)
    for n, device in enumerate((across_a, across_b, across_c)):
        ghold[n] = gains
        copy = remote(ghold.at[n], gpair.at[n], send_sem, recv_sem, slot + 1 + n, device)
        copy.start()
        copies.append(copy)
        yield
        copy.wait_recv()
        gains = gains + gpair[n]
    swap.wait_recv()
    gains_out[...] = gains
    other = rpair[...]
    width = rest.shape[1]
    rest_out[:, :width] = jnp.where(a == 0, rest, other)
    rest_out[:, width:] = jnp.where(a == 0, other, rest)
    for copy in copies:
        copy.wait_send()


def high_peers(high):
    seq = lax.axis_index("seq")
    tp = lax.axis_index("tp")
    return [(lax.rem(seq // LO + k, high) * LO + lax.rem(seq, LO), tp) for k in range(1, high)]


def last_kernel(high, part_ref, gains_ref, rest_ref, out_ref, gains_out, rest_out, *more):
    greet(high_peers(high) + neighbours(True))
    in_turn(
        scatter_steps(True, part_ref, out_ref, *more[:13]),
        small_steps(high, gains_ref, rest_ref, gains_out, rest_out, *more[13:]),
    )


def scatter_and_sums(partial, gains, rest, high, collective_id):
    slots = 2 * (high - 1) + 4
    ways = 8
    width = partial.shape[1]
    rows = partial.shape[0] // ways
    return pl.pallas_call(
        functools.partial(last_kernel, high),
        out_shape=[
            jax.ShapeDtypeStruct((rows, width), jnp.float32),
            jax.ShapeDtypeStruct(gains.shape, jnp.float32),
            jax.ShapeDtypeStruct((rest.shape[0], LO * rest.shape[1]), jnp.float32),
        ],
        in_specs=[VMEM] * 3,
        out_specs=[VMEM] * 3,
        scratch_shapes=scatter_scratch(ways, rows, width)
        + [
            pltpu.VMEM((high - 1, *gains.shape), jnp.float32),
            pltpu.VMEM((high - 1, *rest.shape), jnp.float32),
            pltpu.VMEM((3, *gains.shape), jnp.float32),
            pltpu.VMEM(rest.shape, jnp.float32),
            pltpu.VMEM((3, *gains.shape), jnp.float32),
            pltpu.VMEM(rest.shape, jnp.float32),
            pltpu.SemaphoreType.DMA((slots,)),
            pltpu.SemaphoreType.DMA((slots,)),
        ],
        name="scatter_and_sums",
        cost_estimate=EIGHTEEN_US,
        compiler_params=pltpu.CompilerParams(
            collective_id=collective_id, has_side_effects=True, vmem_limit_bytes=40 * 2**20
        ),
    )(lowered(partial).reshape(ways, rows, width), gains, rest)


def attention_back_kernel(
    shift, query_ref, ext_ref, grad_ref, log_ref, here_ref, there_ref, cos_ref, sin_ref, dquery_ref, dext_ref, total
):
    tile = 256
    rows, width = query_ref.shape
    heads = width // HD
    reach = shift + tile
    scale = HD ** (-0.5)
    total[...] = jnp.zeros_like(total)

    def turn(n, carry):
        h = n // (rows // tile)
        first = pl.multiple_of(lax.rem(n, rows // tile) * tile, tile)
        lanes = pl.ds(pl.multiple_of(h * HD, HD), HD)
        at = pl.ds(first, tile)
        seen = pl.ds(first, reach)
        query = query_ref[at, lanes]
        grad = grad_ref[at, lanes]
        keys = ext_ref[seen, :HD]
        values = ext_ref[seen, HD:]
        distance = (
            lax.broadcasted_iota(jnp.int32, (reach, tile), 1)
            - lax.broadcasted_iota(jnp.int32, (reach, tile), 0)
            + shift
        )
        allowed = (
            (there_ref[seen, :] == here_ref[0:1, at]) & (distance >= 0) & (distance < WINDOW)
        )
        scores = jnp.where(allowed, product_right(keys, query) * scale, -1e30)
        probs = jnp.exp(scores - log_ref[pl.ds(h, 1), at])
        grad_probs = product_right(values, grad)
        mean = jnp.sum(probs * grad_probs, axis=0, keepdims=True)
        grad_scores = lowered(probs * (grad_probs - mean) * scale)
        total[seen, :HD] += product(grad_scores, query)
        total[seen, HD:] += product(lowered(probs), grad)
        turned = product_left(grad_scores, keys)
        turned = turned * cos_ref[at, :] - pltpu.roll(turned, HD // 2, 1) * sin_ref[at, :]
        dquery_ref[at, lanes] = lowered(turned)
        return carry

    lax.fori_loop(0, heads * (rows // tile), turn, 0)
    dext_ref[...] = lowered(total[...])


def attention_back(query_rot, extended, grad, log_total, segment, key_segment, cosine, sine):
    rows, width = query_rot.shape
    seen = extended.shape[0]
    log_rows = jnp.concatenate(
        [log_total, jnp.zeros((8 - log_total.shape[0], rows), jnp.float32)], axis=0
    )
    return pl.pallas_call(
        functools.partial(attention_back_kernel, seen - rows),
        out_shape=[
            jax.ShapeDtypeStruct((rows, width), jnp.bfloat16),
            jax.ShapeDtypeStruct((seen, 2 * HD), jnp.bfloat16),
        ],
        in_specs=[VMEM] * 8,
        out_specs=[VMEM] * 2,
        scratch_shapes=[pltpu.VMEM((seen, 2 * HD), jnp.float32)],
        name="attention_back",
        cost_estimate=EIGHTEEN_US,
        compiler_params=pltpu.CompilerParams(vmem_limit_bytes=48 * 2**20),
    )(
        query_rot,
        extended,
        grad,
        log_rows,
        jnp.broadcast_to(segment[None], (8, rows)),
        key_segment[:, None],
        cosine,
        sine,
    )


def stacked_by_low(mine, other):
    lo = lax.rem(lax.axis_index("seq"), LO)
    return jnp.stack([jnp.where(lo == 0, mine, other), jnp.where(lo == 0, other, mine)])


def swap_low(block):
    count = lax.axis_size("seq")
    return lax.ppermute(block, "seq", [(s, s // LO * LO + (1 - s % LO)) for s in range(count)])


def high_groups():
    count = lax.axis_size("seq")
    return [[h * LO + l for h in range(count // LO)] for l in range(LO)]


def swap_columns(*parts):
    lo = lax.rem(lax.axis_index("seq"), LO)
    halves = [jnp.concatenate(each, axis=1) for each in zip(*map(split_columns, parts))]
    kept = jnp.where(lo == 0, halves[0], halves[1])
    given = jnp.where(lo == 0, halves[1], halves[0])
    both = stacked_by_low(kept, swap_low(given))
    return both.reshape(-1, both.shape[2])


def gather_high(rows):
    return lax.all_gather(rows, "seq", axis=0, tiled=True, axis_index_groups=high_groups())


def reduce_high(grad):
    return lax.psum_scatter(
        lowered(grad), "seq", scatter_dimension=0, tiled=True, axis_index_groups=high_groups()
    )


def exchanged(both):
    lo = lax.rem(lax.axis_index("seq"), LO)
    both = both.reshape(LO, -1, both.shape[1])
    kept = jnp.where(lo == 0, both[0], both[1])
    given = jnp.where(lo == 0, both[1], both[0])
    return stacked_by_low(kept, swap_low(given))


def split_columns(block):
    width = block.shape[1] // LO
    return [block[:, l * width : (l + 1) * width] for l in range(LO)]


def joined(blocks):
    return jnp.concatenate([blocks[l] for l in range(LO)], axis=1).astype(jnp.float32)


def dense_forward(normed, weights):
    gate_up, down = weights
    width = down.shape[1]
    both = product(normed, gate_up)
    hidden = lowered(gated(both[:, :width], both[:, width:]))
    return (lowered(product_right(hidden, down)), (normed, both, hidden))


def dense_backward(stream, gain, grad_out, grad_low, kept, weights, cid, tied=()):
    gate_up, down = weights
    width = down.shape[1]
    normed, both, hidden = kept
    grad_down = product_left(grad_low, hidden)
    grad_hidden = product(grad_low, down)
    gate_grad, up_grad = jax.vjp(gated, both[:, :width], both[:, width:])[1](grad_hidden)
    both_low = jnp.concatenate([lowered(gate_grad), lowered(up_grad)], axis=1)
    grad_both = product_left(normed, both_low)
    partial = product_right(both_low, gate_up)
    partial, grad_both, grad_down, tied = lax.optimization_barrier(
        (lowered(partial), lowered(grad_both), lowered(grad_down), tied)
    )
    (grad_normed,) = scatter([partial], True, cid["scatter_full"])
    stream_grad, gain_grad = jax.vjp(rms_norm, stream, gain)[1](grad_normed)
    return (grad_out + stream_grad, gain_grad, grad_both, grad_down, tied)


def block_product(values, weight):
    block_width = weight.shape[0]
    blocks = weight.shape[1] // block_width
    return jnp.concatenate(
        [
            product_right(
                values[:, n * block_width : (n + 1) * block_width],
                weight[:, n * block_width : (n + 1) * block_width],
            )
            for n in range(blocks)
        ],
        axis=1,
    )


def block_grads(values, weight, upstream):
    block_width = weight.shape[0]
    cuts = [slice(n * block_width, (n + 1) * block_width) for n in range(weight.shape[1] // block_width)]
    return (
        jnp.concatenate([product_left(upstream[:, s], values[:, s]) for s in cuts], axis=1),
        jnp.concatenate([product(upstream[:, s], weight[:, s]) for s in cuts], axis=1),
    )


def shifted(block, distance):
    count = lax.axis_size("seq")
    route = [(i - distance, i) for i in range(count) if 0 <= i - distance < count]
    return lax.ppermute(block, "seq", route)


def score_block(query_rot, keys_ext, allowed, score_scale):
    raw = jnp.einsum("qhd,kd->hqk", query_rot, keys_ext, preferred_element_type=jnp.float32)
    return jnp.where(allowed[None], raw * score_scale, -1e30)


CIDS = {
    "gather_full": 0,
    "gather_half": 1,
    "scatter_full": 2,
    "scatter_half": 3,
    "scan": 4,
    "scan_back": 5,
    "scatter_wide": 6,
    "last": 7,
    "gather_narrow": 8,
    "gather_two": 9,
    "scatter_two": 10,
}


def dense_grads(both):
    width = both.shape[1] // 3
    both = exchanged(both)
    return (
        joined(both[:, :, :width]),
        joined(both[:, :, width : 2 * width]),
        joined(both[:, :, 2 * width :]).T,
    )


def turns(position):
    half_width = HD // 2
    frequency = 10000.0 ** (-jnp.arange(half_width, dtype=jnp.float32) / half_width)
    angle = position.astype(jnp.float32)[:, None] * frequency[None, :]
    cosine, sine = (jnp.cos(angle), jnp.sin(angle))
    return (
        jnp.concatenate([cosine, cosine], axis=1),
        jnp.concatenate([-sine, sine], axis=1),
    )


def both_lows(lanes):
    other = swap_low(lanes)
    lo = lax.rem(lax.axis_index("seq"), LO)
    both = jnp.stack([jnp.where(lo == 0, lanes, other), jnp.where(lo == 0, other, lanes)], axis=1)
    return both.reshape(-1, lanes.shape[2])


def dense_weights(wide):
    width = wide.shape[1] // 3
    return (wide[:, : 2 * width], wide[:, 2 * width :])


def summed_low(both):
    lo = lax.rem(lax.axis_index("seq"), LO)
    both = both.reshape(LO, -1, both.shape[1])
    kept = jnp.where(lo == 0, both[0], both[1])
    given = jnp.where(lo == 0, both[1], both[0])
    return kept.astype(jnp.float32) + swap_low(given).astype(jnp.float32)


def local(
    tokens,
    cotangent,
    doc_lengths,
    norm_gains,
    input_branch,
    gate_branch,
    conv_taps,
    conv_bias,
    recur_gate,
    input_gate,
    gate_biases,
    decay_param,
    recur_output,
    dense_gate_one,
    dense_up_one,
    dense_down_one,
    query_weight,
    keyvalue_weight,
    attention_out,
    dense_gate_two,
    dense_up_two,
    dense_down_two,
):
    cid = CIDS
    shard_rows = tokens.shape[0]
    seq = lax.axis_index("seq")
    tp = lax.axis_index("tp")
    lo = lax.rem(seq, LO)
    high = lax.axis_size("seq") // LO
    ways = lax.axis_size("tp")
    own_rows = shard_rows // ways
    plane_rows = shard_rows * LO
    channels = conv_bias.shape[0] // LO
    leading = CONV - 1
    halo_shards = WINDOW // shard_rows
    first_slot = seq * shard_rows
    plane_slot = (seq // LO) * plane_rows
    own_slot = first_slot + tp * own_rows
    valid = layout(doc_lengths, own_slot, own_rows)[3]
    segment, position, _, _ = layout(doc_lengths, first_slot, shard_rows)
    plane_reset = layout(doc_lengths, plane_slot, plane_rows)[2]
    conv_segment = layout(doc_lengths, plane_slot - leading, plane_rows + leading)[0]
    key_segment = layout(
        doc_lengths, first_slot - halo_shards * shard_rows, (halo_shards + 1) * shard_rows
    )[0]

    def ours(block, axis):
        return lax.dynamic_slice_in_dim(block, lo * channels, channels, axis)

    taps, bias = (ours(conv_taps, 1), ours(conv_bias, 0))
    bias_pair, decay_values = (ours(gate_biases, 1), ours(decay_param, 0))

    gate_rows = recur_gate.shape[1]
    weight_rows = input_branch.shape[0]
    first = swap_columns(
        jnp.concatenate([input_branch, recur_gate.T], axis=0),
        jnp.concatenate([gate_branch, input_gate.T], axis=0),
        jnp.concatenate([recur_output.T, jnp.zeros_like(recur_gate.T)], axis=0),
    )
    first_full = gather_high(first).reshape(high * LO, weight_rows + gate_rows, 3 * channels)
    in_full = first_full[:, :weight_rows, : 2 * channels].reshape(-1, 2 * channels)
    output_full = first_full[:, :weight_rows, 2 * channels :].reshape(-1, channels)
    recur_full = first_full[:, weight_rows:, :channels].reshape(-1, channels)
    input_gate_full = first_full[:, weight_rows:, channels : 2 * channels].reshape(-1, channels)
    second = swap_columns(dense_gate_one, dense_up_one, dense_down_one.T)

    own_tokens = lax.dynamic_slice_in_dim(tokens, tp * own_rows, own_rows, 0)
    own_cotangent = lax.dynamic_slice_in_dim(cotangent, tp * own_rows, own_rows, 0)
    stream_in = own_tokens.astype(jnp.float32)
    grad_stream = own_cotangent.astype(jnp.float32) * valid[:, None]
    normed_one, grad_low = gather(
        [lowered(rms_norm(stream_in, norm_gains[0])), lowered(grad_stream)],
        True,
        cid["gather_two"],
    )
    normed_one, second, query_weight, keyvalue_weight, attention_out = lax.optimization_barrier(
        (normed_one, second, query_weight, keyvalue_weight, attention_out)
    )
    weights_one = dense_weights(gather_high(second))
    both = product(normed_one, in_full)
    both, dense_gate_two, dense_up_two, dense_down_two = lax.optimization_barrier(
        (both, dense_gate_two, dense_up_two, dense_down_two)
    )

    keyvalue_part = keyvalue_weight[None]
    for step in (1, 2):
        other = lax.ppermute(keyvalue_part, "tp", [(i, i ^ step) for i in range(ways)])
        low_bit = lax.rem(tp // step, 2)
        keyvalue_part = jnp.concatenate(
            [
                jnp.where(low_bit == 0, keyvalue_part, other),
                jnp.where(low_bit == 0, other, keyvalue_part),
            ],
            axis=0,
        )
    keyvalue_part = keyvalue_part.reshape(weight_rows, keyvalue_weight.shape[1])
    third = jnp.concatenate([query_weight, keyvalue_part, attention_out.T], axis=1)
    fourth = swap_columns(dense_gate_two, dense_up_two, dense_down_two.T)

    branch = both[:, :channels]
    gating = both[:, channels:]
    rim = shifted(branch[plane_rows - leading :], LO)
    branch_ext = jnp.concatenate([rim, branch], axis=0)
    conv_local = functools.partial(convolve, segment=conv_segment)
    conv_out, conv_pull = jax.vjp(conv_local, branch_ext, taps, bias)
    conv_low = lowered(conv_out)
    recur_raw = block_product(conv_low, recur_full)
    input_raw = block_product(conv_low, input_gate_full)
    rate_local = functools.partial(coefficients, reset=plane_reset)
    (decay, drive), rate_pull = jax.vjp(
        rate_local, recur_raw, input_raw, conv_out, bias_pair, decay_values
    )
    ones = jnp.ones((8, channels), jnp.float32)
    state, state_in = plane_scan(decay, drive, ones, high, False, cid["scan"])
    gate_act, gate_pull = jax.vjp(jax.nn.gelu, gating)
    mixed = lowered(state * gate_act)
    (summed,) = scatter([product_right(mixed, output_full)], True, cid["scatter_full"])
    stream_one = stream_in + summed
    (normed_two,) = gather([lowered(rms_norm(stream_one, norm_gains[1]))], True, cid["gather_full"])
    normed_two, weights_one, third = lax.optimization_barrier((normed_two, weights_one, third))
    third = lax.all_gather(third, "seq", axis_index_groups=high_groups())

    partial, kept_one = dense_forward(normed_two, weights_one)
    partial, fourth = lax.optimization_barrier((partial, fourth))
    weights_two = dense_weights(gather_high(fourth))
    query_width = query_weight.shape[1]
    early_width = query_width + keyvalue_part.shape[1]
    early_full = both_lows(third[:, :, :early_width])
    query_full = early_full[:, :query_width]
    keyvalue_full = early_full[:, query_width:]
    attn_full = both_lows(third[:, :, early_width:])

    (summed,) = scatter([partial], True, cid["scatter_full"])
    stream_two = stream_one + summed

    normed_own = lowered(rms_norm(stream_two, norm_gains[2]))
    (normed_three,) = gather([normed_own], False, cid["gather_half"])
    query = product(normed_three, query_full)
    keyval = product(normed_three, keyvalue_full)
    local_heads = query.shape[1] // HD
    query_heads = query.reshape(shard_rows, local_heads, HD)
    rotate_here = functools.partial(rotate, position=position)
    query_rot = lowered(rotate_here(query_heads))
    key_rot = lowered(rotate_here(keyval[:, :HD]))
    packed = jnp.concatenate([key_rot, lowered(keyval[:, HD:])], axis=1)
    earlier = [shifted(packed, offset) for offset in range(halo_shards, 0, -1)]
    extended = jnp.concatenate(earlier + [packed], axis=0)
    keys_ext = extended[:, :HD]
    values_ext = extended[:, HD:]
    query_slots = first_slot + jnp.arange(shard_rows, dtype=jnp.int32)
    key_slots = (
        first_slot
        - halo_shards * shard_rows
        + jnp.arange((halo_shards + 1) * shard_rows, dtype=jnp.int32)
    )
    distance = query_slots[:, None] - key_slots[None, :]
    allowed = (segment[:, None] == key_segment[None, :]) & (distance >= 0) & (distance < WINDOW)
    score_scale = HD ** (-0.5)
    scores = score_block(query_rot, keys_ext, allowed, score_scale)
    row_top = jnp.max(scores, axis=-1, keepdims=True)
    row_total = jnp.sum(jnp.exp(scores - row_top), axis=-1, keepdims=True)
    log_total = row_top + jnp.log(row_total)
    probs_low = lowered(jnp.exp(scores - row_top) / row_total)
    attended = lowered(
        jnp.einsum("hqk,kd->qhd", probs_low, values_ext, preferred_element_type=jnp.float32)
    ).reshape(shard_rows, local_heads * HD)
    (summed,) = scatter([product_right(attended, attn_full)], False, cid["scatter_half"])
    stream_three = stream_two + summed

    (normed_four,) = gather(
        [lowered(rms_norm(stream_three, norm_gains[3]))], True, cid["gather_full"]
    )
    partial_four, kept_two = dense_forward(normed_four, weights_two)
    grad_stream, gain_four, grad_both_two, grad_down_two, _ = dense_backward(
        stream_three, norm_gains[3], grad_stream, grad_low, kept_two, weights_two, cid
    )

    done_two = reduce_high(jnp.concatenate([grad_both_two, grad_down_two], axis=1))
    (grad_attn_low,) = gather([lowered(grad_stream)], False, cid["gather_half"])
    grad_attn_out = product_left(grad_attn_low, attended)
    grad_attended = lowered(product(grad_attn_low, attn_full))
    grad_query_low, grad_ext = attention_back(
        query_rot.reshape(shard_rows, local_heads * HD),
        extended,
        grad_attended,
        log_total[:, :, 0],
        segment,
        key_segment,
        *turns(position),
    )
    grad_query = product_left(normed_three, grad_query_low)
    grad_pieces = grad_ext.reshape(halo_shards + 1, shard_rows, 2 * HD)
    partial = jnp.concatenate(
        [lowered(product_right(grad_query_low, query_full))] + list(grad_pieces), axis=1
    )
    partial, grad_query, grad_attn_out = lax.optimization_barrier(
        (partial, lowered(grad_query), lowered(grad_attn_out))
    )
    attn_wire = jnp.concatenate([grad_query, grad_attn_out], axis=1)
    (summed,) = scatter([partial], False, cid["scatter_wide"])
    summed, partial_four = lax.optimization_barrier((summed, partial_four))
    (summed_four,) = scatter([partial_four], True, cid["scatter_full"])
    width = normed_own.shape[1]
    pieces = [
        summed[:, width + 2 * HD * k : width + 2 * HD * (k + 1)] for k in range(halo_shards + 1)
    ]
    keyvalue_total = pieces[halo_shards]
    for offset in range(1, halo_shards + 1):
        piece = shifted(lowered(pieces[halo_shards - offset]), -offset)
        keyvalue_total = keyvalue_total + piece.astype(jnp.float32)
    keyvalue_total, attn_wire, done_two, summed_four = lax.optimization_barrier(
        (keyvalue_total, attn_wire, done_two, summed_four)
    )
    done_attn = reduce_high(attn_wire)
    own_position = lax.dynamic_slice_in_dim(position, tp * own_rows, own_rows, 0)
    rotate_own = functools.partial(rotate, position=own_position)
    key_grad = jax.vjp(rotate_own, keyvalue_total[:, :HD])[1](keyvalue_total[:, :HD])[0]
    keyvalue_low = lowered(jnp.concatenate([key_grad, keyvalue_total[:, HD:]], axis=1))
    grad_normed = summed[:, :width] + product_right(keyvalue_low, keyvalue_full)
    (keyvalue_grads,) = gather([keyvalue_low], False, cid["gather_narrow"])
    part_rows = keyvalue_weight.shape[0]
    ways_view = normed_three.reshape(shard_rows, high * LO, ways, part_rows)
    ours_only = lax.dynamic_slice_in_dim(ways_view, tp, 1, 2).reshape(shard_rows, -1)
    grad_keyvalue = lowered(product_left(ours_only, keyvalue_grads))
    stream_grad, gain_three = jax.vjp(rms_norm, stream_two, norm_gains[2])[1](grad_normed)
    grad_stream = grad_stream + stream_grad

    (grad_low,) = gather([lowered(grad_stream)], True, cid["gather_full"])
    grad_low, done_two = lax.optimization_barrier((grad_low, done_two))
    done_two = dense_grads(done_two)
    grad_stream, gain_two, grad_both_one, grad_down_one, done_attn = dense_backward(
        stream_one,
        norm_gains[1],
        grad_stream,
        grad_low,
        kept_one,
        weights_one,
        cid,
        done_attn,
    )

    one_wire = jnp.concatenate([grad_both_one, grad_down_one], axis=1)
    grad_stream, one_wire, done_attn = lax.optimization_barrier(
        (grad_stream, one_wire, done_attn)
    )
    done_one = reduce_high(one_wire)
    (grad_out_low,) = gather([lowered(grad_stream)], True, cid["gather_full"])
    grad_recur_out = product_left(grad_out_low, mixed)
    grad_mixed = product(grad_out_low, output_full)
    grad_mixed, done_attn, done_two = lax.optimization_barrier((grad_mixed, done_attn, done_two))
    done_attn = summed_low(done_attn)
    grad_state = grad_mixed * gate_act
    grad_gating = lowered(gate_pull(grad_mixed * state)[0])
    decay_next = jnp.concatenate([decay[1:], jnp.ones((1, channels), jnp.float32)], axis=0)
    first_decay = jnp.broadcast_to(decay[:1], (8, channels))
    grad_drive, _ = plane_scan(decay_next, grad_state, first_decay, high, True, cid["scan_back"])
    state_prev = jnp.concatenate([state_in[:1], state[:-1]], axis=0)
    grad_decay = grad_drive * state_prev
    grad_recur_raw, grad_input_raw, grad_conv, grad_biases, grad_decay_param = rate_pull(
        (grad_decay, grad_drive)
    )
    grad_recur_gate, conv_back_recur = block_grads(conv_low, recur_full, lowered(grad_recur_raw))
    grad_input_gate, conv_back_input = block_grads(
        conv_low, input_gate_full, lowered(grad_input_raw)
    )
    grad_branch_ext, grad_taps, grad_conv_bias = conv_pull(
        grad_conv + conv_back_recur + conv_back_input
    )
    returned_rim = shifted(grad_branch_ext[:leading], -LO)
    grad_branch = grad_branch_ext[leading:] + jnp.pad(
        returned_rim, ((plane_rows - leading, 0), (0, 0))
    )
    both_low = jnp.concatenate([lowered(grad_branch), grad_gating], axis=1)
    grad_in = product_left(normed_one, both_low)
    partial = lowered(product_right(both_low, in_full))
    partial, grad_in, grad_recur_out = lax.optimization_barrier(
        (partial, lowered(grad_in), lowered(grad_recur_out))
    )
    blocks = high * LO
    wire = jnp.concatenate(
        [
            jnp.concatenate(
                [
                    grad_in.reshape(blocks, weight_rows, 2 * channels),
                    grad_recur_out.reshape(blocks, weight_rows, channels),
                ],
                axis=2,
            ),
            jnp.concatenate(
                [
                    lowered(grad_recur_gate).reshape(blocks, gate_rows, channels),
                    lowered(grad_input_gate).reshape(blocks, gate_rows, channels),
                    jnp.zeros((blocks, gate_rows, channels), jnp.bfloat16),
                ],
                axis=2,
            ),
            grad_keyvalue.reshape(blocks, -1, 3 * channels),
        ],
        axis=1,
    )
    layer_own = lowered((stream_three + summed_four) * valid[:, None])
    layer_own, both_low = lax.optimization_barrier((layer_own, both_low))
    (layer_out,) = gather([layer_own], False, cid["gather_half"])
    wire, done_one, layer_out = lax.optimization_barrier((wire, done_one, layer_out))
    last = exchanged(reduce_high(wire.reshape(-1, 3 * channels)))
    keyvalue_grad = jnp.sum(last[:, weight_rows + gate_rows :].astype(jnp.float32), axis=0)
    last_rows, last_gates = (last[:, :weight_rows], last[:, weight_rows : weight_rows + gate_rows])
    gain_one = jnp.sum(normed_one.astype(jnp.float32) * partial.astype(jnp.float32), axis=0)
    gain_one = gain_one / norm_gains[0]
    grad_normed, gains_sum, small = scatter_and_sums(
        partial,
        jnp.concatenate(
            [jnp.stack([gain_one, gain_two, gain_three, gain_four]), jnp.zeros_like(norm_gains)]
        ),
        jnp.concatenate(
            [grad_taps, grad_conv_bias[None], grad_biases, grad_decay_param[None]], axis=0
        ),
        high,
        cid["last"],
    )
    rms_local = functools.partial(rms_norm, gain=norm_gains[0])
    stream_grad = jax.vjp(rms_local, stream_in)[1](grad_normed)[0]
    (input_grad,) = gather([lowered(grad_stream + stream_grad)], False, cid["gather_half"])
    gains_sum = gains_sum[: norm_gains.shape[0]]
    input_grad = input_grad.astype(jnp.float32)
    return (
        layer_out,
        input_grad,
        gains_sum,
        joined(last_rows[:, :, :channels]),
        joined(last_rows[:, :, channels : 2 * channels]),
        small[:CONV],
        small[CONV],
        joined(last_gates[:, :, :channels]).T,
        joined(last_gates[:, :, channels : 2 * channels]).T,
        small[CONV + 1 : CONV + 3],
        small[CONV + 3],
        joined(last_rows[:, :, 2 * channels :]).T,
        *dense_grads(done_one),
        done_attn[:, :query_width],
        keyvalue_grad.reshape(keyvalue_weight.shape),
        done_attn[:, query_width:].T,
        *done_two,
    )


def solution(mesh):
    placed = (
        P("seq", None),
        P("seq", None),
        P(),
        P(),
        P("seq", "tp"),
        P("seq", "tp"),
        P(None, "tp"),
        P("tp"),
        P("tp", "seq"),
        P("tp", "seq"),
        P(None, "tp"),
        P("tp"),
        P("tp", "seq"),
        P("seq", "tp"),
        P("seq", "tp"),
        P("tp", "seq"),
        P("seq", "tp"),
        P(("seq", "tp"), None),
        P("tp", "seq"),
        P("seq", "tp"),
        P("seq", "tp"),
        P("tp", "seq"),
    )
    return jax.shard_map(
        local,
        mesh=mesh,
        in_specs=placed,
        out_specs=(
            P("seq", None),
            P("seq", None),
            P(),
            P("seq", "tp"),
            P("seq", "tp"),
            P(None, "tp"),
            P("tp"),
            P("tp", "seq"),
            P("tp", "seq"),
            P(None, "tp"),
            P("tp"),
            P("tp", "seq"),
            P("seq", "tp"),
            P("seq", "tp"),
            P("tp", "seq"),
            P("seq", "tp"),
            P(("seq", "tp"), None),
            P("tp", "seq"),
            P("seq", "tp"),
            P("seq", "tp"),
            P("tp", "seq"),
        ),
        check_vma=False,
    )
```

```python
import functools
import math

import jax
import jax.numpy as jnp
from jax import lax
from jax.experimental import pallas as pl
from jax.experimental.pallas import tpu as pltpu
from jax.sharding import PartitionSpec as P

HD = 128
CONV = 4
WINDOW = 1024


def product(left, right):
    return jnp.dot(left, right, preferred_element_type=jnp.float32)


def product_left(left, right):
    return lax.dot_general(
        left, right, (((0,), (0,)), ((), ())), preferred_element_type=jnp.float32
    )


def product_right(left, right):
    return lax.dot_general(
        left, right, (((1,), (1,)), ((), ())), preferred_element_type=jnp.float32
    )


def lowered(values):
    return values.astype(jnp.bfloat16)


def rms_norm(values, gain):
    return values * lax.rsqrt(jnp.mean(values * values, axis=-1, keepdims=True) + 1e-06) * gain


def gated(gate_values, up_values):
    return jax.nn.gelu(gate_values) * up_values


def layout(doc_lengths, first_slot, count):
    ends = jnp.cumsum(doc_lengths, dtype=jnp.int32)
    slots = first_slot + jnp.arange(count, dtype=jnp.int32)
    passed = slots[:, None] >= ends[None, :]
    segment = jnp.sum(passed.astype(jnp.int32), axis=1)
    begin = jnp.max(jnp.where(passed, ends[None, :], 0), axis=1)
    segment = jnp.where(slots < 0, -1, segment)
    position = slots - begin
    reset = (slots != begin).astype(jnp.float32)
    valid = (segment < doc_lengths.shape[0]).astype(jnp.float32)
    return (segment, position, reset, valid)


def convolve(extended, taps, bias, segment):
    leading = CONV - 1
    total_rows = extended.shape[0] - leading
    result = bias[None, :] + taps[0][None, :] * extended[leading:]
    for lag_index in range(1, CONV):
        same = (
            segment[leading:] == segment[leading - lag_index : leading - lag_index + total_rows]
        ).astype(jnp.float32)
        result = (
            result
            + same[:, None]
            * taps[lag_index][None, :]
            * extended[leading - lag_index : leading - lag_index + total_rows]
        )
    return result


def coefficients(recur_raw, input_raw, conv_values, bias_pair, decay_values, reset):
    recur_rate = jax.nn.sigmoid(recur_raw + bias_pair[0][None, :])
    input_rate = jax.nn.sigmoid(input_raw + bias_pair[1][None, :])
    log_decay = -8.0 * recur_rate * jax.nn.softplus(-decay_values)[None, :]
    multiplier = jnp.sqrt(jnp.maximum(-jnp.expm1(2.0 * log_decay), 0.01))
    return (jnp.exp(log_decay) * reset[:, None], multiplier * input_rate * conv_values)


def combine_state(earlier, later):
    return (earlier[0] * later[0], later[0] * earlier[1] + later[1])


MESH = pl.DeviceIdType.MESH
LO = 2
EIGHTEEN_US = pl.CostEstimate(flops=0, bytes_accessed=60_000_000, transcendentals=0)
TEN_US = pl.CostEstimate(flops=0, bytes_accessed=33_000_000, transcendentals=0)
ANY = pl.BlockSpec(memory_space=pl.ANY)
VMEM = pl.BlockSpec(memory_space=pltpu.VMEM)


def cube():
    seq = lax.axis_index("seq")
    tp = lax.axis_index("tp")
    a = lax.rem(seq, LO)
    b = tp // 2
    c = lax.rem(tp, 2)
    across_a = (seq - a + 1 - a, tp)
    across_b = (seq, (1 - b) * 2 + c)
    across_c = (seq, b * 2 + 1 - c)
    return (a, b, c, across_a, across_b, across_c)


def hail(devices):
    for device in devices:
        pl.semaphore_signal(
            pltpu.get_barrier_semaphore(), inc=1, device_id=device, device_id_type=MESH
        )


def greet(devices):
    hail(devices)
    pl.semaphore_wait(pltpu.get_barrier_semaphore(), len(devices))


def remote(src, dst, send_sem, recv_sem, slot, device):
    return pltpu.make_async_remote_copy(
        src_ref=src,
        dst_ref=dst,
        send_sem=send_sem.at[slot],
        recv_sem=recv_sem.at[slot],
        device_id=device,
        device_id_type=MESH,
    )


def in_turn(*runs):
    runs = list(runs)
    while runs:
        for run in list(runs):
            if next(run, "end") == "end":
                runs.remove(run)


def neighbours(full):
    across_a, across_b, across_c = cube()[3:]
    return [across_c, across_b] + ([across_a] if full else [])


def gather_steps(full, in_ref, out_ref, send_sem, recv_sem, local_sem):
    a, b, c, across_a, across_b, across_c = cube()
    half = in_ref.shape[0] // 2

    def index(pa, pb, pc):
        return pa * 4 + pb * 2 + pc if full else pb * 2 + pc

    me, an, bn, dn = (
        index(a, b, c),
        index(1 - a, b, c),
        index(a, 1 - b, c),
        index(1 - a, 1 - b, c),
    )
    low, high = (pl.ds(0, half), pl.ds(half, half))
    sent = {}

    def go(slot, src, dst, device):
        copy = remote(src, dst, send_sem, recv_sem, slot, device)
        copy.start()
        sent[slot] = copy

    def own(slot, part, device):
        go(slot, in_ref.at[part], out_ref.at[me, part], device)

    def onward(slot, block, part, device):
        go(slot, out_ref.at[block, part], out_ref.at[block, part], device)

    if full:
        own(0, low, across_a)
    own(1, high, across_b)
    if full:
        own(2, high, across_a)
    own(3, low, across_b)
    go(4, in_ref, out_ref.at[me], across_c)
    mine = pltpu.make_async_copy(in_ref, out_ref.at[me], local_sem)
    mine.start()
    yield
    if full:
        sent[0].wait_recv()
        onward(5, an, low, across_b)
        onward(6, an, low, across_c)
        yield
    sent[1].wait_recv()
    if full:
        onward(7, bn, high, across_a)
    onward(8, bn, high, across_c)
    yield
    if full:
        sent[2].wait_recv()
        onward(9, an, high, across_c)
        yield
    sent[3].wait_recv()
    onward(10, bn, low, across_c)
    yield
    if full:
        sent[5].wait_recv()
        onward(11, dn, low, across_c)
        yield
        sent[7].wait_recv()
        onward(12, dn, high, across_c)
        yield
    for slot in (4, 6, 8, 9, 10, 11, 12):
        if slot in sent:
            sent[slot].wait_recv()
    for copy in sent.values():
        copy.wait_send()
    mine.wait()


def gather_kernel(full, count, *refs):
    in_refs, out_refs = (refs[:count], refs[count : 2 * count])
    send_sem, recv_sem, local_sem = refs[2 * count :]
    greet(neighbours(full))
    in_turn(
        *[
            gather_steps(
                full, in_refs[k], out_refs[k], send_sem.at[k], recv_sem.at[k], local_sem.at[k]
            )
            for k in range(count)
        ]
    )


def gather(blocks, full, collective_id):
    ways = 8 if full else 4
    count = len(blocks)
    results = pl.pallas_call(
        functools.partial(gather_kernel, full, count),
        out_shape=[
            jax.ShapeDtypeStruct((ways, *block.shape), block.dtype) for block in blocks
        ],
        in_specs=[ANY] * count,
        out_specs=[ANY] * count,
        scratch_shapes=[
            pltpu.SemaphoreType.DMA((count, 13)),
            pltpu.SemaphoreType.DMA((count, 13)),
            pltpu.SemaphoreType.DMA((count,)),
        ],
        name="gather_full" if full else "gather_half",
        cost_estimate=EIGHTEEN_US,
        compiler_params=pltpu.CompilerParams(collective_id=collective_id, has_side_effects=True),
    )(*blocks)
    return [
        result.reshape(ways * block.shape[0], block.shape[1])
        for result, block in zip(results, blocks)
    ]


def scatter_steps(
    full, part_ref, out_ref, cbuf, sx, sy, tx, ty, ax, by, rx, ry, csend, crecv, send_sem, recv_sem
):
    a, b, c, across_a, across_b, across_c = cube()
    half = part_ref.shape[1] // 2

    def index(pa, pb, pc):
        return pa * 4 + pb * 2 + pc if full else pb * 2 + pc

    def pair(pa, pb):
        return pa * 2 + pb if full else pb

    low, high = (pl.ds(0, half), pl.ds(half, half))
    if full:
        order = [
            (1 - a, 1 - b, low),
            (1 - a, 1 - b, high),
            (1 - a, b, low),
            (a, 1 - b, high),
            (a, 1 - b, low),
            (1 - a, b, high),
            (a, b, low),
            (a, b, high),
        ]
    else:
        order = [(a, 1 - b, low), (a, 1 - b, high), (a, b, low), (a, b, high)]
    core = {}

    def share(*which):
        for k in which:
            pa, pb, part = order[k]
            core[k] = remote(
                part_ref.at[index(pa, pb, 1 - c), part],
                cbuf.at[pair(pa, pb), part],
                csend,
                crecv,
                k,
                across_c,
            )
            core[k].start()

    def summed(k):
        pa, pb, part = order[k]
        core[k].wait_recv()
        return part_ref[index(pa, pb, c), part].astype(jnp.float32) + cbuf[
            pair(pa, pb), part
        ].astype(jnp.float32)

    sent = []

    def go(src, dst, slot, device):
        copy = remote(src, dst, send_sem, recv_sem, slot, device)
        copy.start()
        sent.append(copy)
        return copy

    if full:
        yield
        share(0, 1)
        yield
        share(2, 5)
        sx[0] = lowered(summed(0))
        x0 = go(sx.at[0], ax.at[0], 0, across_a)
        sy[0] = lowered(summed(1))
        y0 = go(sy.at[0], by.at[0], 1, across_b)
        yield
        share(3, 4)
        sx[1] = lowered(summed(2))
        x1 = go(sx.at[1], ax.at[1], 2, across_a)
        yield
        share(6, 7)
        sy[1] = lowered(summed(3))
        y1 = go(sy.at[1], by.at[1], 3, across_b)
        yield
        total = summed(4)
        x0.wait_recv()
        ty[...] = lowered(total + ax[0].astype(jnp.float32))
        last_y = go(ty, ry, 4, across_b)
        total = summed(5)
        y0.wait_recv()
        tx[...] = lowered(total + by[0].astype(jnp.float32))
        last_x = go(tx, rx, 5, across_a)
        yield
        total = summed(6)
        x1.wait_recv()
        total = total + ax[1].astype(jnp.float32)
        last_y.wait_recv()
        out_ref[low] = total + ry[...].astype(jnp.float32)
        total = summed(7)
        y1.wait_recv()
        total = total + by[1].astype(jnp.float32)
        last_x.wait_recv()
        out_ref[high] = total + rx[...].astype(jnp.float32)
    else:
        share(0, 1, 2, 3)
        sy[0] = lowered(summed(0))
        y0 = go(sy.at[0], by.at[0], 1, across_b)
        sy[1] = lowered(summed(1))
        y1 = go(sy.at[1], by.at[1], 3, across_b)
        yield
        total = summed(2)
        y0.wait_recv()
        out_ref[low] = total + by[0].astype(jnp.float32)
        total = summed(3)
        y1.wait_recv()
        out_ref[high] = total + by[1].astype(jnp.float32)
    for copy in [*core.values(), *sent]:
        copy.wait_send()


def scatter_kernel(full, count, *refs):
    greet(neighbours(full))
    in_turn(
        *[
            scatter_steps(full, refs[k], refs[count + k], *refs[2 * count + 13 * k :][:13])
            for k in range(count)
        ]
    )


def scatter_scratch(ways, rows, width):
    half = rows // 2
    shapes = [(ways // 2, rows, width)] + [(2, half, width)] * 2 + [(half, width)] * 2
    shapes += [(2, half, width)] * 2 + [(half, width)] * 2
    return [pltpu.VMEM(shape, jnp.bfloat16) for shape in shapes] + [
        pltpu.SemaphoreType.DMA((k,)) for k in (8, 8, 6, 6)
    ]


def scatter(partials, full, collective_id):
    ways = 8 if full else 4
    count = len(partials)
    rows = partials[0].shape[0] // ways
    scratch = []
    for partial in partials:
        scratch += scatter_scratch(ways, rows, partial.shape[1])
    return pl.pallas_call(
        functools.partial(scatter_kernel, full, count),
        out_shape=[
            jax.ShapeDtypeStruct((rows, partial.shape[1]), jnp.float32) for partial in partials
        ],
        in_specs=[VMEM] * count,
        out_specs=[VMEM] * count,
        scratch_shapes=scratch,
        name="scatter_full" if full else "scatter_half",
        cost_estimate=EIGHTEEN_US,
        compiler_params=pltpu.CompilerParams(
            collective_id=collective_id, has_side_effects=True, vmem_limit_bytes=48 * 2**20
        ),
    )(*[lowered(partial).reshape(ways, rows, -1) for partial in partials])


def scan_kernel(
    high, reverse, decay_ref, drive_ref, end_ref, state_ref, carry_ref, cum, strips, sendbuf, recvbuf, send_sem, recv_sem
):
    rows, width = decay_ref.shape
    strands = 8
    steps = rows // strands
    lanes = 128
    blocks = width // lanes
    mine = lax.axis_index("seq") // LO
    peers = high_peers(high)
    greet(peers)
    for n in range(blocks):
        cum[n] = decay_ref[:, n * lanes : (n + 1) * lanes]
        strips[n] = drive_ref[:, n * lanes : (n + 1) * lanes]

    def step(i, carry):
        r = steps - 1 - i if reverse else i
        at = pl.ds(r, strands, stride=steps)
        new = []
        for n in range(blocks):
            a = cum[n, at, :]
            product_now = carry[2 * n] * a
            state_now = carry[2 * n + 1] * a + strips[n, at, :]
            cum[n, at, :] = product_now
            strips[n, at, :] = state_now
            new += [product_now, state_now]
        return tuple(new)

    ones = jnp.ones((strands, lanes), jnp.float32)
    ends = lax.fori_loop(0, steps, step, (ones, jnp.zeros_like(ones)) * blocks, unroll=8)
    strand_order = list(range(strands - 1, -1, -1)) if reverse else list(range(strands))
    before = {}
    for n in range(blocks):
        total_a = jnp.ones((1, lanes), jnp.float32)
        total_h = jnp.zeros((1, lanes), jnp.float32)
        for k in strand_order:
            before[n, k] = (total_a, total_h)
            a, h = (ends[2 * n][k : k + 1], ends[2 * n + 1][k : k + 1])
            total_h = a * total_h + h
            total_a = a * total_a
        scale = end_ref[0:1, n * lanes : (n + 1) * lanes]
        sendbuf[n, 0:1, :] = total_a * scale
        sendbuf[n, 1:2, :] = total_h * scale
        sendbuf[n, 2:8, :] = jnp.zeros((6, lanes), jnp.float32)
    copies = []
    for k, peer in enumerate(peers):
        copy = remote(sendbuf, recvbuf.at[k], send_sem, recv_sem, k, peer)
        copy.start()
        copies.append(copy)
    for copy in copies:
        copy.wait_recv()
    for n in range(blocks):
        carry = jnp.zeros((1, lanes), jnp.float32)
        for turn in range(high - 1):
            plane = high - 1 - turn if reverse else turn
            away = lax.rem(mine - plane + high, high)
            reached = plane > mine if reverse else plane < mine
            got = recvbuf[jnp.where(reached, away - 1, 0), n]
            carry = jnp.where(reached, got[0:1] * carry + got[1:2], carry)
        span = pl.ds(n * lanes, lanes)
        carry_ref[:, span] = jnp.broadcast_to(carry, (carry_ref.shape[0], lanes))
        for k in range(strands):
            enter = before[n, k][0] * carry + before[n, k][1]
            at = pl.ds(k * steps, steps)
            state_ref[at, span] = strips[n, at, :] + cum[n, at, :] * enter
    for copy in copies:
        copy.wait_send()


def plane_scan(decay, drive, end_scale, high, reverse, collective_id):
    rows, width = decay.shape
    return pl.pallas_call(
        functools.partial(scan_kernel, high, reverse),
        out_shape=(
            jax.ShapeDtypeStruct((rows, width), jnp.float32),
            jax.ShapeDtypeStruct((8, width), jnp.float32),
        ),
        in_specs=[VMEM] * 3,
        out_specs=(VMEM, VMEM),
        scratch_shapes=[
            pltpu.VMEM((width // 128, rows, 128), jnp.float32),
            pltpu.VMEM((width // 128, rows, 128), jnp.float32),
            pltpu.VMEM((width // 128, 8, 128), jnp.float32),
            pltpu.VMEM((high - 1, width // 128, 8, 128), jnp.float32),
            pltpu.SemaphoreType.DMA((high - 1,)),
            pltpu.SemaphoreType.DMA((high - 1,)),
        ],
        name="scan_back" if reverse else "scan",
        cost_estimate=TEN_US,
        compiler_params=pltpu.CompilerParams(
            collective_id=collective_id, has_side_effects=True, vmem_limit_bytes=32 * 2**20
        ),
    )(decay, drive, end_scale)


def small_steps(high, gains_ref, rest_ref, gains_out, rest_out, gbuf, rbuf, ghold, rhold, gpair, rpair, send_sem, recv_sem):
    a, b, c, across_a, across_b, across_c = cube()
    peers = high_peers(high)
    copies = []
    for k, peer in enumerate(peers):
        for n, (src, dst) in enumerate(((gains_ref, gbuf.at[k]), (rest_ref, rbuf.at[k]))):
            copy = remote(src, dst, send_sem, recv_sem, 2 * k + n, peer)
            copy.start()
            copies.append(copy)
    yield
    for copy in copies:
        copy.wait_recv()
    gains = gains_ref[...]
    rest = rest_ref[...]
    for k in range(high - 1):
        gains = gains + gbuf[k]
        rest = rest + rbuf[k]
    rhold[...] = rest
    slot = 2 * (high - 1)
    swap = remote(rhold, rpair, send_sem, recv_sem, slot, across_a)
    swap.start()
    copies.append(swap)
    for n, device in enumerate((across_a, across_b, across_c)):
        ghold[n] = gains
        copy = remote(ghold.at[n], gpair.at[n], send_sem, recv_sem, slot + 1 + n, device)
        copy.start()
        copies.append(copy)
        yield
        copy.wait_recv()
        gains = gains + gpair[n]
    swap.wait_recv()
    gains_out[...] = gains
    other = rpair[...]
    width = rest.shape[1]
    rest_out[:, :width] = jnp.where(a == 0, rest, other)
    rest_out[:, width:] = jnp.where(a == 0, other, rest)
    for copy in copies:
        copy.wait_send()


def high_peers(high):
    seq = lax.axis_index("seq")
    tp = lax.axis_index("tp")
    return [(lax.rem(seq // LO + k, high) * LO + lax.rem(seq, LO), tp) for k in range(1, high)]


def last_kernel(high, part_ref, gains_ref, rest_ref, out_ref, gains_out, rest_out, *more):
    greet(high_peers(high) + neighbours(True))
    in_turn(
        scatter_steps(True, part_ref, out_ref, *more[:13]),
        small_steps(high, gains_ref, rest_ref, gains_out, rest_out, *more[13:]),
    )


def scatter_and_sums(partial, gains, rest, high, collective_id):
    slots = 2 * (high - 1) + 4
    ways = 8
    width = partial.shape[1]
    rows = partial.shape[0] // ways
    return pl.pallas_call(
        functools.partial(last_kernel, high),
        out_shape=[
            jax.ShapeDtypeStruct((rows, width), jnp.float32),
            jax.ShapeDtypeStruct(gains.shape, jnp.float32),
            jax.ShapeDtypeStruct((rest.shape[0], LO * rest.shape[1]), jnp.float32),
        ],
        in_specs=[VMEM] * 3,
        out_specs=[VMEM] * 3,
        scratch_shapes=scatter_scratch(ways, rows, width)
        + [
            pltpu.VMEM((high - 1, *gains.shape), jnp.float32),
            pltpu.VMEM((high - 1, *rest.shape), jnp.float32),
            pltpu.VMEM((3, *gains.shape), jnp.float32),
            pltpu.VMEM(rest.shape, jnp.float32),
            pltpu.VMEM((3, *gains.shape), jnp.float32),
            pltpu.VMEM(rest.shape, jnp.float32),
            pltpu.SemaphoreType.DMA((slots,)),
            pltpu.SemaphoreType.DMA((slots,)),
        ],
        name="scatter_and_sums",
        cost_estimate=EIGHTEEN_US,
        compiler_params=pltpu.CompilerParams(
            collective_id=collective_id, has_side_effects=True, vmem_limit_bytes=40 * 2**20
        ),
    )(lowered(partial).reshape(ways, rows, width), gains, rest)


def gelu_parts(x):
    inner = math.sqrt(2 / math.pi)
    curve = jnp.tanh(inner * (x + 0.044715 * x * x * x))
    half = 0.5 * (1 + curve)
    slope = half + 0.5 * x * (1 - curve * curve) * inner * (1 + 3 * 0.044715 * x * x)
    return (x * half, slope)


def dense_kernel(mode, main, *refs):
    forward, backward = (mode != "backward", mode != "forward")
    refs = list(refs)

    def take(count):
        taken, refs[:] = (refs[:count], refs[count:])
        return taken

    (n_hbm,) = take(1)
    g_hbm = take(1)[0] if backward else None
    (w_hbm,) = take(1)
    ab_hbm = take(1)[0] if mode == "backward" else None
    (out_ref,) = take(1)
    wire_hbm = take(1)[0] if backward else None
    ab_out = take(1)[0] if mode == "forward" else None
    p4_hbm = take(1)[0] if mode == "both" else None
    n_v, w_v, hid_v, part_v = take(4)
    g_v, low_v, wire_v = take(3) if backward else (None, None, None)
    ab_v = take(1)[0] if mode != "both" else None
    p4_v = take(1)[0] if mode == "both" else None
    buffers = take(13)
    (sems,) = take(1)
    lanes = 128
    both = 2 * main + lanes
    tile = 256
    rows = n_v.shape[0]
    a, b = cube()[:2]
    near = neighbours(True)
    hail(near)
    loads = [pltpu.make_async_copy(n_hbm, n_v, sems.at[0])]
    loads.append(pltpu.make_async_copy(w_hbm, w_v, sems.at[1]))
    if backward:
        loads.append(pltpu.make_async_copy(g_hbm, g_v, sems.at[2]))
    if mode == "backward":
        loads.append(pltpu.make_async_copy(ab_hbm, ab_v, sems.at[3]))
    for load in loads:
        load.start()
    for load in loads:
        load.wait()

    def work(pa, pb):
        block = pa * 4 + pb * 2
        at = pl.ds(pl.multiple_of(block * lanes, tile), tile)
        if forward:
            ab = product(n_v[at, :], w_v[:, :both])
            if mode == "forward":
                ab_v[at, :] = ab
        else:
            ab = ab_v[at, :]
        gate, up, tail = (ab[:, :main], ab[:, main : 2 * main], ab[:, 2 * main :])
        first = lax.broadcasted_iota(jnp.int32, tail.shape, 1) < lanes // 2
        turned = pltpu.roll(tail, lanes // 2, 1)
        act, slope = gelu_parts(gate)
        tail_act, tail_slope = gelu_parts(tail)
        hid_v[at, :main] = lowered(act * up)
        hid_v[at, main:] = lowered(jnp.where(first, tail_act * turned, 0.0))
        if backward:
            grad = product(g_v[at, :], w_v[:, both:])
            grad_main, grad_tail = (grad[:, :main], grad[:, main:])
            low_v[at, :main] = lowered(grad_main * up * slope)
            low_v[at, main : 2 * main] = lowered(grad_main * act)
            turned_grad = pltpu.roll(grad_tail, lanes // 2, 1)
            turned_act = pltpu.roll(tail_act, lanes // 2, 1)
            low_v[at, 2 * main :] = lowered(
                jnp.where(first, grad_tail * turned * tail_slope, turned_grad * turned_act)
            )
            part = lowered(product_right(low_v[at, :], w_v[:, :both]))
        else:
            part = lowered(product_right(hid_v[at, :], w_v[:, both:]))
        part_v[pl.ds(block, 2)] = part.reshape(2, lanes, part.shape[1])

    schedule = scatter_steps(True, part_v, out_ref, *buffers)
    next(schedule)
    for turn, (pa, pb) in enumerate(((1 - a, 1 - b), (1 - a, b), (a, 1 - b), (a, b))):
        work(pa, pb)
        if turn == 0:
            pl.semaphore_wait(pltpu.get_barrier_semaphore(), len(near))
        next(schedule)
    stores = []

    def store(src, dst, slot):
        copy = pltpu.make_async_copy(src, dst, sems.at[slot])
        copy.start()
        stores.append(copy)

    if mode == "forward":
        store(ab_v, ab_out, 4)
        next(schedule)
    else:
        depth = w_v.shape[0]

        def grads(i, carry):
            cols = pl.ds(pl.multiple_of(i * tile, tile), tile)
            wire_v[cols, :both] = lowered(product_left(n_v[:, cols], low_v[...]))
            wire_v[cols, both:] = lowered(product_left(g_v[:, cols], hid_v[...]))
            return carry

        split = depth // tile // 2
        lax.fori_loop(0, split, grads, 0)
        store(wire_v.at[pl.ds(0, split * tile)], wire_hbm.at[pl.ds(0, split * tile)], 4)
        next(schedule)
        lax.fori_loop(split, depth // tile, grads, 0)
        rest = pl.ds(split * tile, depth - split * tile)
        store(wire_v.at[rest], wire_hbm.at[rest], 5)
    if mode == "both":

        def onward(i, carry):
            at = pl.ds(pl.multiple_of(i * tile, tile), tile)
            p4_v[at, :] = lowered(product_right(hid_v[at, :], w_v[:, both:]))
            return carry

        lax.fori_loop(0, rows // tile, onward, 0)
        store(p4_v, p4_hbm, 6)
    next(schedule, None)
    for copy in stores:
        copy.wait()


def dense_call(mode, normed, grad_low, weights, ab, collective_id):
    rows, depth = normed.shape
    columns = weights.shape[1]
    main = (columns // 128 - 2) // 3 * 128
    both = 2 * main + 128
    backward = mode != "forward"
    low = jnp.bfloat16
    operands = [normed] + ([grad_low] if backward else []) + [weights]
    shapes = [jax.ShapeDtypeStruct((rows // 8, depth), jnp.float32)]
    scratch = [(normed.shape, low), (weights.shape, low), ((rows, columns - both), low)]
    scratch += [((8, rows // 8, depth), low)]
    if backward:
        shapes.append(jax.ShapeDtypeStruct(weights.shape, low))
        scratch += [(normed.shape, low), ((rows, both), low), (weights.shape, low)]
    if mode == "forward":
        shapes.append(jax.ShapeDtypeStruct((rows, both), jnp.float32))
    if mode == "backward":
        operands.append(ab)
    if mode == "both":
        shapes.append(jax.ShapeDtypeStruct((rows, depth), low))
        scratch.append(((rows, depth), low))
    else:
        scratch.append(((rows, both), jnp.float32))
    return pl.pallas_call(
        functools.partial(dense_kernel, mode, main),
        out_shape=shapes,
        in_specs=[ANY] * len(operands),
        out_specs=[VMEM] + [ANY] * (len(shapes) - 1),
        scratch_shapes=[pltpu.VMEM(shape, kind) for shape, kind in scratch]
        + scatter_scratch(8, rows // 8, depth)
        + [pltpu.SemaphoreType.DMA((7,))],
        name="dense_" + mode,
        cost_estimate=pl.CostEstimate(
            flops=0, bytes_accessed=100_000_000 if backward else 80_000_000, transcendentals=0
        ),
        compiler_params=pltpu.CompilerParams(
            collective_id=collective_id, has_side_effects=True, vmem_limit_bytes=56 * 2**20
        ),
    )(*operands)


def attention_kernel(
    shift, query_ref, ext_ref, here_ref, there_ref, cos_ref, sin_ref, out_ref, rot_ref, log_ref
):
    tile = 256
    rows, width = query_ref.shape
    heads = width // HD
    reach = shift + tile
    scale = HD ** (-0.5)
    log_ref[...] = jnp.zeros_like(log_ref)

    def turn(n, carry):
        h = n // (rows // tile)
        first = pl.multiple_of(lax.rem(n, rows // tile) * tile, tile)
        lanes = pl.ds(pl.multiple_of(h * HD, HD), HD)
        at = pl.ds(first, tile)
        seen = pl.ds(first, reach)
        query = query_ref[at, lanes]
        query = query * cos_ref[at, :] + pltpu.roll(query, HD // 2, 1) * sin_ref[at, :]
        query = lowered(query)
        rot_ref[at, lanes] = query
        allowed = visible(shift, there_ref[seen, :], here_ref[0:1, at])
        scores = jnp.where(allowed, product_right(ext_ref[seen, :HD], query) * scale, -1e30)
        top = jnp.max(scores, axis=0, keepdims=True)
        probs = jnp.exp(scores - top)
        total = jnp.sum(probs, axis=0, keepdims=True)
        log_ref[pl.ds(h, 1), at] = top + jnp.log(total)
        out_ref[at, lanes] = lowered(product_left(lowered(probs / total), ext_ref[seen, HD:]))
        return carry

    lax.fori_loop(0, heads * (rows // tile), turn, 0)


def visible(shift, there, here):
    shape = (there.shape[0], here.shape[1])
    distance = (
        lax.broadcasted_iota(jnp.int32, shape, 1) - lax.broadcasted_iota(jnp.int32, shape, 0) + shift
    )
    return (there == here) & (distance >= 0) & (distance < WINDOW)


def attention(query, extended, here, there, cosine, sine):
    rows, width = query.shape
    return pl.pallas_call(
        functools.partial(attention_kernel, extended.shape[0] - rows),
        out_shape=[
            jax.ShapeDtypeStruct((rows, width), jnp.bfloat16),
            jax.ShapeDtypeStruct((rows, width), jnp.bfloat16),
            jax.ShapeDtypeStruct((8, rows), jnp.float32),
        ],
        in_specs=[VMEM] * 6,
        out_specs=[VMEM] * 3,
        name="attention",
        cost_estimate=TEN_US,
        compiler_params=pltpu.CompilerParams(vmem_limit_bytes=48 * 2**20),
    )(query, extended, here, there, cosine, sine)


def attention_back_kernel(
    shift, query_ref, ext_ref, grad_ref, log_ref, here_ref, there_ref, cos_ref, sin_ref, dquery_ref, dext_ref, total
):
    tile = 256
    rows, width = query_ref.shape
    heads = width // HD
    reach = shift + tile
    scale = HD ** (-0.5)
    total[...] = jnp.zeros_like(total)

    def turn(n, carry):
        h = n // (rows // tile)
        first = pl.multiple_of(lax.rem(n, rows // tile) * tile, tile)
        lanes = pl.ds(pl.multiple_of(h * HD, HD), HD)
        at = pl.ds(first, tile)
        seen = pl.ds(first, reach)
        query = query_ref[at, lanes]
        grad = grad_ref[at, lanes]
        keys = ext_ref[seen, :HD]
        values = ext_ref[seen, HD:]
        allowed = visible(shift, there_ref[seen, :], here_ref[0:1, at])
        scores = jnp.where(allowed, product_right(keys, query) * scale, -1e30)
        probs = jnp.exp(scores - log_ref[pl.ds(h, 1), at])
        grad_probs = product_right(values, grad)
        mean = jnp.sum(probs * grad_probs, axis=0, keepdims=True)
        grad_scores = lowered(probs * (grad_probs - mean) * scale)
        total[seen, :HD] += product(grad_scores, query)
        total[seen, HD:] += product(lowered(probs), grad)
        turned = product_left(grad_scores, keys)
        turned = turned * cos_ref[at, :] - pltpu.roll(turned, HD // 2, 1) * sin_ref[at, :]
        dquery_ref[at, lanes] = lowered(turned)
        return carry

    lax.fori_loop(0, heads * (rows // tile), turn, 0)
    dext_ref[...] = lowered(total[...])


def attention_back(query_rot, extended, grad, log_total, here, there, cosine, sine):
    rows, width = query_rot.shape
    seen = extended.shape[0]
    return pl.pallas_call(
        functools.partial(attention_back_kernel, seen - rows),
        out_shape=[
            jax.ShapeDtypeStruct((rows, width), jnp.bfloat16),
            jax.ShapeDtypeStruct((seen, 2 * HD), jnp.bfloat16),
        ],
        in_specs=[VMEM] * 8,
        out_specs=[VMEM] * 2,
        scratch_shapes=[pltpu.VMEM((seen, 2 * HD), jnp.float32)],
        name="attention_back",
        cost_estimate=EIGHTEEN_US,
        compiler_params=pltpu.CompilerParams(vmem_limit_bytes=48 * 2**20),
    )(query_rot, extended, grad, log_total, here, there, cosine, sine)


def stacked_by_low(mine, other):
    lo = lax.rem(lax.axis_index("seq"), LO)
    return jnp.stack([jnp.where(lo == 0, mine, other), jnp.where(lo == 0, other, mine)])


def swap_low(block):
    count = lax.axis_size("seq")
    return lax.ppermute(block, "seq", [(s, s // LO * LO + (1 - s % LO)) for s in range(count)])


def high_groups():
    count = lax.axis_size("seq")
    return [[h * LO + l for h in range(count // LO)] for l in range(LO)]


def swap_columns(*parts):
    return swap_pieces([jnp.concatenate(each, axis=1) for each in zip(*map(split_columns, parts))])


def swap_pieces(halves):
    lo = lax.rem(lax.axis_index("seq"), LO)
    kept = jnp.where(lo == 0, halves[0], halves[1])
    given = jnp.where(lo == 0, halves[1], halves[0])
    both = stacked_by_low(kept, swap_low(given))
    return both.reshape(-1, both.shape[2])


def gather_high(rows):
    return lax.all_gather(rows, "seq", axis=0, tiled=True, axis_index_groups=high_groups())


def reduce_high(grad):
    return lax.psum_scatter(
        lowered(grad), "seq", scatter_dimension=0, tiled=True, axis_index_groups=high_groups()
    )


def exchanged(both):
    lo = lax.rem(lax.axis_index("seq"), LO)
    both = both.reshape(LO, -1, both.shape[1])
    kept = jnp.where(lo == 0, both[0], both[1])
    given = jnp.where(lo == 0, both[1], both[0])
    return stacked_by_low(kept, swap_low(given))


def split_columns(block):
    width = block.shape[1] // LO
    return [block[:, l * width : (l + 1) * width] for l in range(LO)]


def joined(blocks):
    return jnp.concatenate([blocks[l] for l in range(LO)], axis=1).astype(jnp.float32)


def block_product(values, weight):
    block_width = weight.shape[0]
    blocks = weight.shape[1] // block_width
    return jnp.concatenate(
        [
            product_right(
                values[:, n * block_width : (n + 1) * block_width],
                weight[:, n * block_width : (n + 1) * block_width],
            )
            for n in range(blocks)
        ],
        axis=1,
    )


def block_grads(values, weight, upstream):
    block_width = weight.shape[0]
    cuts = [slice(n * block_width, (n + 1) * block_width) for n in range(weight.shape[1] // block_width)]
    return (
        jnp.concatenate([product_left(upstream[:, s], values[:, s]) for s in cuts], axis=1),
        jnp.concatenate([product(upstream[:, s], weight[:, s]) for s in cuts], axis=1),
    )


def shifted(block, distance):
    count = lax.axis_size("seq")
    route = [(i - distance, i) for i in range(count) if 0 <= i - distance < count]
    return lax.ppermute(block, "seq", route)


CIDS = {
    "gather_full": 0,
    "gather_half": 1,
    "scatter_full": 2,
    "scatter_half": 3,
    "scan": 4,
    "scan_back": 5,
    "scatter_wide": 6,
    "last": 7,
    "gather_narrow": 8,
    "gather_two": 9,
    "forward": 10,
    "both": 11,
    "backward": 12,
    "gather_weight": 13,
    "gather_seen": 14,
}


def dense_wire(gate, up, down):
    pieces = []
    for g, u, d in zip(*map(split_columns, (gate, up, down))):
        main = g.shape[1] // 128 * 128
        blank = jnp.zeros((d.shape[0], -d.shape[1] % 128), d.dtype)
        pieces.append(
            jnp.concatenate([g[:, :main], u[:, :main], g[:, main:], u[:, main:], d, blank], axis=1)
        )
    return pieces


def dense_grads(both):
    columns = both.shape[2]
    main = (columns // 128 - 2) // 3 * 128
    tail = 64
    ends = 2 * main

    def part(first, last):
        return jnp.concatenate([both[:, :, first : first + main], both[:, :, last : last + tail]], axis=2)

    return (
        joined(part(0, ends)),
        joined(part(main, ends + tail)),
        joined(both[:, :, ends + 2 * tail : ends + 3 * tail + main]).T,
    )


def turns(position):
    half_width = HD // 2
    frequency = 10000.0 ** (-jnp.arange(half_width, dtype=jnp.float32) / half_width)
    angle = position.astype(jnp.float32)[:, None] * jnp.tile(frequency, 2)[None, :]
    sign = jnp.where(jnp.arange(HD) < half_width, -1.0, 1.0)
    return (jnp.cos(angle), jnp.sin(angle) * sign[None, :])


def rotate(values, factors):
    cosine, sine = factors
    half_width = HD // 2
    swapped = jnp.concatenate([values[..., half_width:], values[..., :half_width]], axis=-1)
    return values * cosine + swapped * sine


def rotate_back(values, factors):
    cosine, sine = factors
    half_width = HD // 2
    swapped = jnp.concatenate([values[..., half_width:], values[..., :half_width]], axis=-1)
    return values * cosine - swapped * sine


def both_lows(lanes):
    other = swap_low(lanes)
    lo = lax.rem(lax.axis_index("seq"), LO)
    both = jnp.stack([jnp.where(lo == 0, lanes, other), jnp.where(lo == 0, other, lanes)], axis=1)
    return both.reshape(-1, lanes.shape[2])


def swap_sums(grad):
    lo = lax.rem(lax.axis_index("seq"), LO)
    pairs = grad.reshape(lax.axis_size("seq") // LO, LO, -1, grad.shape[1])
    kept = jnp.where(lo == 0, pairs[:, 0], pairs[:, 1])
    given = jnp.where(lo == 0, pairs[:, 1], pairs[:, 0])
    return (kept.reshape(-1, grad.shape[1]), swap_low(given).reshape(-1, grad.shape[1]))


def local(
    tokens,
    cotangent,
    doc_lengths,
    norm_gains,
    input_branch,
    gate_branch,
    conv_taps,
    conv_bias,
    recur_gate,
    input_gate,
    gate_biases,
    decay_param,
    recur_output,
    dense_gate_one,
    dense_up_one,
    dense_down_one,
    query_weight,
    keyvalue_weight,
    attention_out,
    dense_gate_two,
    dense_up_two,
    dense_down_two,
):
    cid = CIDS
    shard_rows = tokens.shape[0]
    seq = lax.axis_index("seq")
    tp = lax.axis_index("tp")
    lo = lax.rem(seq, LO)
    high = lax.axis_size("seq") // LO
    ways = lax.axis_size("tp")
    own_rows = shard_rows // ways
    plane_rows = shard_rows * LO
    channels = conv_bias.shape[0] // LO
    leading = CONV - 1
    halo_shards = WINDOW // shard_rows
    first_slot = seq * shard_rows
    plane_slot = (seq // LO) * plane_rows
    own_slot = first_slot + tp * own_rows
    valid = layout(doc_lengths, own_slot, own_rows)[3]
    segment, position, _, _ = layout(doc_lengths, first_slot, shard_rows)
    plane_reset = layout(doc_lengths, plane_slot, plane_rows)[2]
    conv_segment = layout(doc_lengths, plane_slot - leading, plane_rows + leading)[0]
    key_segment = layout(
        doc_lengths, first_slot - halo_shards * shard_rows, (halo_shards + 1) * shard_rows
    )[0]

    def ours(block, axis):
        return lax.dynamic_slice_in_dim(block, lo * channels, channels, axis)

    taps, bias = (ours(conv_taps, 1), ours(conv_bias, 0))
    bias_pair, decay_values = (ours(gate_biases, 1), ours(decay_param, 0))

    gate_rows = recur_gate.shape[1]
    weight_rows = input_branch.shape[0]
    attn_rows = jnp.concatenate([query_weight, attention_out.T], axis=1)
    query_width = query_weight.shape[1]
    third = lax.all_gather(
        jnp.concatenate(
            [attn_rows, keyvalue_weight.reshape(-1, attn_rows.shape[1])], axis=0
        ),
        "seq",
        axis_index_groups=high_groups(),
    )
    own_tokens = lax.dynamic_slice_in_dim(tokens, tp * own_rows, own_rows, 0)
    own_cotangent = lax.dynamic_slice_in_dim(cotangent, tp * own_rows, own_rows, 0)
    stream_in = own_tokens.astype(jnp.float32)
    grad_stream = own_cotangent.astype(jnp.float32) * valid[:, None]
    (normed_one,) = gather([lowered(rms_norm(stream_in, norm_gains[0]))], True, cid["gather_full"])
    first = swap_columns(
        jnp.concatenate([input_branch, recur_gate.T], axis=0),
        jnp.concatenate([gate_branch, input_gate.T], axis=0),
        jnp.concatenate([recur_output.T, jnp.zeros_like(recur_gate.T)], axis=0),
    )
    first, third, normed_one = lax.optimization_barrier((first, third, normed_one))
    first_full = gather_high(first).reshape(high * LO, weight_rows + gate_rows, 3 * channels)
    in_full = first_full[:, :weight_rows, : 2 * channels].reshape(-1, 2 * channels)
    output_full = first_full[:, :weight_rows, 2 * channels :].reshape(-1, channels)
    recur_full = first_full[:, weight_rows:, :channels].reshape(-1, channels)
    input_gate_full = first_full[:, weight_rows:, channels : 2 * channels].reshape(-1, channels)
    third = both_lows(third)
    second = swap_pieces(dense_wire(dense_gate_one, dense_up_one, dense_down_one.T))

    (grad_low,) = gather([lowered(grad_stream)], True, cid["gather_full"])
    normed_one, in_full, second, third, grad_low = lax.optimization_barrier(
        (normed_one, in_full, second, third, grad_low)
    )
    weights_one = gather_high(second)
    both = product(normed_one, in_full)
    both, dense_gate_two, dense_up_two, dense_down_two = lax.optimization_barrier(
        (both, dense_gate_two, dense_up_two, dense_down_two)
    )
    fourth = swap_pieces(dense_wire(dense_gate_two, dense_up_two, dense_down_two.T))

    branch = both[:, :channels]
    gating = both[:, channels:]
    rim = shifted(branch[plane_rows - leading :], LO)
    branch_ext = jnp.concatenate([rim, branch], axis=0)
    conv_local = functools.partial(convolve, segment=conv_segment)
    conv_out, conv_pull = jax.vjp(conv_local, branch_ext, taps, bias)
    conv_low = lowered(conv_out)
    recur_raw = block_product(conv_low, recur_full)
    input_raw = block_product(conv_low, input_gate_full)
    rate_local = functools.partial(coefficients, reset=plane_reset)
    (decay, drive), rate_pull = jax.vjp(
        rate_local, recur_raw, input_raw, conv_out, bias_pair, decay_values
    )
    ones = jnp.ones((8, channels), jnp.float32)
    state, state_in = plane_scan(decay, drive, ones, high, False, cid["scan"])
    gate_act, gate_pull = jax.vjp(jax.nn.gelu, gating)
    mixed = lowered(state * gate_act)
    mixed, fourth = lax.optimization_barrier((mixed, fourth))
    (summed,) = scatter([product_right(mixed, output_full)], True, cid["scatter_full"])
    stream_one = stream_in + summed
    (normed_two,) = gather([lowered(rms_norm(stream_one, norm_gains[1]))], True, cid["gather_full"])
    third = third.reshape(high * LO, -1, third.shape[1])
    query_full = third[:, :weight_rows, :query_width].reshape(-1, query_width)
    attn_full = third[:, :weight_rows, query_width:].reshape(-1, third.shape[2] - query_width)
    part_rows, part_width = keyvalue_weight.shape
    (keyvalue_full,) = gather(
        [third[:, weight_rows:].reshape(-1, part_width)], False, cid["gather_weight"]
    )
    keyvalue_full = keyvalue_full.reshape(ways, high * LO, part_rows, part_width)
    keyvalue_full = keyvalue_full.transpose(1, 0, 2, 3).reshape(-1, part_width)
    factors = turns(position)
    own_factors = [lax.dynamic_slice_in_dim(each, tp * own_rows, own_rows, 0) for each in factors]
    segment_rows = jnp.broadcast_to(segment[None], (8, shard_rows))
    key_column = key_segment[:, None]
    early = (keyvalue_full, query_full, attn_full, factors, own_factors, segment_rows, key_column)
    normed_two, early = lax.optimization_barrier((normed_two, early))
    keyvalue_full, query_full, attn_full, factors, own_factors, segment_rows, key_column = early
    normed_two, weights_one, fourth = lax.optimization_barrier((normed_two, weights_one, fourth))
    weights_two = gather_high(fourth)
    summed, ab_one = dense_call("forward", normed_two, None, weights_one, None, cid["forward"])
    stream_two = stream_one + summed

    normed_own = lowered(rms_norm(stream_two, norm_gains[2]))
    keyval = product(normed_own, keyvalue_full)
    key_rot = lowered(rotate(keyval[:, :HD], own_factors))
    packed = jnp.concatenate([key_rot, lowered(keyval[:, HD:])], axis=1)
    earlier = [shifted(packed, offset) for offset in range(halo_shards, 0, -1)]
    normed_three, seen = gather(
        [normed_own, jnp.concatenate(earlier + [packed], axis=1)], False, cid["gather_seen"]
    )
    extended = jnp.concatenate(
        [seen[:, 2 * HD * k : 2 * HD * (k + 1)] for k in range(halo_shards + 1)], axis=0
    )
    query = product(normed_three, query_full)
    attended, query_rot, log_total = attention(
        query, extended, segment_rows, key_column, *factors
    )
    (summed,) = scatter([product_right(attended, attn_full)], False, cid["scatter_half"])
    stream_three = stream_two + summed

    (normed_four,) = gather(
        [lowered(rms_norm(stream_three, norm_gains[3]))], True, cid["gather_full"]
    )
    grad_normed, wire_two, partial_four = dense_call(
        "both", normed_four, grad_low, weights_two, None, cid["both"]
    )
    done_two = reduce_high(wire_two)
    stream_grad, gain_four = jax.vjp(rms_norm, stream_three, norm_gains[3])[1](grad_normed)
    grad_stream = grad_stream + stream_grad
    (grad_attn_low,) = gather([lowered(grad_stream)], False, cid["gather_half"])
    grad_attn_out = product_left(grad_attn_low, attended)
    grad_attended = lowered(product(grad_attn_low, attn_full))
    grad_query_low, grad_ext = attention_back(
        query_rot,
        extended,
        grad_attended,
        log_total,
        segment_rows,
        key_column,
        *factors,
    )
    grad_query = product_left(normed_three, grad_query_low)
    grad_pieces = grad_ext.reshape(halo_shards + 1, shard_rows, 2 * HD)
    partial = jnp.concatenate(
        [lowered(product_right(grad_query_low, query_full))] + list(grad_pieces), axis=1
    )
    partial, grad_query, grad_attn_out = lax.optimization_barrier(
        (partial, lowered(grad_query), lowered(grad_attn_out))
    )
    attn_kept, attn_given = swap_sums(jnp.concatenate([grad_query, grad_attn_out], axis=1))
    (summed,) = scatter([partial], False, cid["scatter_wide"])
    summed, partial_four, attn_given = lax.optimization_barrier(
        (summed, partial_four, attn_given)
    )
    attn_wire = lowered(attn_kept.astype(jnp.float32) + attn_given.astype(jnp.float32))
    (summed_four,) = scatter([partial_four], True, cid["scatter_full"])
    width = normed_own.shape[1]
    pieces = [
        summed[:, width + 2 * HD * k : width + 2 * HD * (k + 1)] for k in range(halo_shards + 1)
    ]
    keyvalue_total = pieces[halo_shards]
    for offset in range(1, halo_shards + 1):
        piece = shifted(lowered(pieces[halo_shards - offset]), -offset)
        keyvalue_total = keyvalue_total + piece.astype(jnp.float32)
    keyvalue_total, summed_four = lax.optimization_barrier((keyvalue_total, summed_four))
    key_grad = rotate_back(keyvalue_total[:, :HD], own_factors)
    keyvalue_low = lowered(jnp.concatenate([key_grad, keyvalue_total[:, HD:]], axis=1))
    grad_normed = summed[:, :width] + product_right(keyvalue_low, keyvalue_full)
    stream_grad, gain_three = jax.vjp(rms_norm, stream_two, norm_gains[2])[1](grad_normed)
    grad_stream = grad_stream + stream_grad

    (grad_low,) = gather([lowered(grad_stream)], True, cid["gather_full"])
    grad_low, attn_wire, done_two = lax.optimization_barrier((grad_low, attn_wire, done_two))
    done_attn = reduce_high(attn_wire)
    done_two = dense_grads(exchanged(done_two))
    grad_normed, one_wire = dense_call(
        "backward", normed_two, grad_low, weights_one, ab_one, cid["backward"]
    )
    stream_grad, gain_two = jax.vjp(rms_norm, stream_one, norm_gains[1])[1](grad_normed)
    grad_stream = grad_stream + stream_grad
    grad_stream, one_wire, done_attn = lax.optimization_barrier(
        (grad_stream, one_wire, done_attn)
    )
    grad_stream, keyvalue_low = lax.optimization_barrier((grad_stream, keyvalue_low))
    done_one = reduce_high(one_wire)
    (keyvalue_grads,) = gather([keyvalue_low], False, cid["gather_narrow"])
    grad_keyvalue = lowered(product_left(normed_three, keyvalue_grads))
    grad_keyvalue = grad_keyvalue.reshape(high * LO, ways, part_rows, part_width)
    grad_keyvalue = lax.dynamic_slice_in_dim(grad_keyvalue, tp, 1, 1)
    (grad_out_low,) = gather([lowered(grad_stream)], True, cid["gather_full"])
    grad_recur_out = product_left(grad_out_low, mixed)
    grad_mixed = product(grad_out_low, output_full)
    grad_mixed, done_attn, done_two = lax.optimization_barrier((grad_mixed, done_attn, done_two))
    done_attn = done_attn.astype(jnp.float32)
    grad_state = grad_mixed * gate_act
    grad_gating = lowered(gate_pull(grad_mixed * state)[0])
    decay_next = jnp.concatenate([decay[1:], jnp.ones((1, channels), jnp.float32)], axis=0)
    first_decay = jnp.broadcast_to(decay[:1], (8, channels))
    grad_drive, _ = plane_scan(decay_next, grad_state, first_decay, high, True, cid["scan_back"])
    state_prev = jnp.concatenate([state_in[:1], state[:-1]], axis=0)
    grad_decay = grad_drive * state_prev
    grad_recur_raw, grad_input_raw, grad_conv, grad_biases, grad_decay_param = rate_pull(
        (grad_decay, grad_drive)
    )
    grad_recur_gate, conv_back_recur = block_grads(conv_low, recur_full, lowered(grad_recur_raw))
    grad_input_gate, conv_back_input = block_grads(
        conv_low, input_gate_full, lowered(grad_input_raw)
    )
    grad_branch_ext, grad_taps, grad_conv_bias = conv_pull(
        grad_conv + conv_back_recur + conv_back_input
    )
    returned_rim = shifted(grad_branch_ext[:leading], -LO)
    grad_branch = grad_branch_ext[leading:] + jnp.pad(
        returned_rim, ((plane_rows - leading, 0), (0, 0))
    )
    both_low = jnp.concatenate([lowered(grad_branch), grad_gating], axis=1)
    grad_in = product_left(normed_one, both_low)
    partial = lowered(product_right(both_low, in_full))
    partial, grad_in, grad_recur_out = lax.optimization_barrier(
        (partial, lowered(grad_in), lowered(grad_recur_out))
    )
    blocks = high * LO
    wire = jnp.concatenate(
        [
            jnp.concatenate(
                [
                    grad_in.reshape(blocks, weight_rows, 2 * channels),
                    grad_recur_out.reshape(blocks, weight_rows, channels),
                ],
                axis=2,
            ),
            jnp.concatenate(
                [
                    lowered(grad_recur_gate).reshape(blocks, gate_rows, channels),
                    lowered(grad_input_gate).reshape(blocks, gate_rows, channels),
                    jnp.zeros((blocks, gate_rows, channels), jnp.bfloat16),
                ],
                axis=2,
            ),
            grad_keyvalue.reshape(blocks, -1, 3 * channels),
        ],
        axis=1,
    )
    layer_own = lowered((stream_three + summed_four) * valid[:, None])
    layer_own, wire = lax.optimization_barrier((layer_own, wire))
    (layer_out,) = gather([layer_own], False, cid["gather_half"])
    wire, done_one, layer_out = lax.optimization_barrier((wire, done_one, layer_out))
    last = exchanged(reduce_high(wire.reshape(-1, 3 * channels)))
    keyvalue_grad = jnp.sum(last[:, weight_rows + gate_rows :].astype(jnp.float32), axis=0)
    last_rows, last_gates = (last[:, :weight_rows], last[:, weight_rows : weight_rows + gate_rows])
    gain_one = jnp.sum(normed_one.astype(jnp.float32) * partial.astype(jnp.float32), axis=0)
    gain_one = gain_one / norm_gains[0]
    grad_normed, gains_sum, small = scatter_and_sums(
        partial,
        jnp.concatenate(
            [jnp.stack([gain_one, gain_two, gain_three, gain_four]), jnp.zeros_like(norm_gains)]
        ),
        jnp.concatenate(
            [grad_taps, grad_conv_bias[None], grad_biases, grad_decay_param[None]], axis=0
        ),
        high,
        cid["last"],
    )
    rms_local = functools.partial(rms_norm, gain=norm_gains[0])
    stream_grad = jax.vjp(rms_local, stream_in)[1](grad_normed)[0]
    input_own = lowered(grad_stream + stream_grad)
    done_one = exchanged(done_one)
    (input_grad,) = gather([input_own], False, cid["gather_half"])
    gains_sum = gains_sum[: norm_gains.shape[0]]
    input_grad, done_one = lax.optimization_barrier((input_grad, done_one))
    input_grad = input_grad.astype(jnp.float32)
    return (
        layer_out,
        input_grad,
        gains_sum,
        joined(last_rows[:, :, :channels]),
        joined(last_rows[:, :, channels : 2 * channels]),
        small[:CONV],
        small[CONV],
        joined(last_gates[:, :, :channels]).T,
        joined(last_gates[:, :, channels : 2 * channels]).T,
        small[CONV + 1 : CONV + 3],
        small[CONV + 3],
        joined(last_rows[:, :, 2 * channels :]).T,
        *dense_grads(done_one),
        done_attn[:, :query_width],
        keyvalue_grad.reshape(keyvalue_weight.shape),
        done_attn[:, query_width:].T,
        *done_two,
    )


def solution(mesh):
    placed = (
        P("seq", None),
        P("seq", None),
        P(),
        P(),
        P("seq", "tp"),
        P("seq", "tp"),
        P(None, "tp"),
        P("tp"),
        P("tp", "seq"),
        P("tp", "seq"),
        P(None, "tp"),
        P("tp"),
        P("tp", "seq"),
        P("seq", "tp"),
        P("seq", "tp"),
        P("tp", "seq"),
        P("seq", "tp"),
        P(("seq", "tp"), None),
        P("tp", "seq"),
        P("seq", "tp"),
        P("seq", "tp"),
        P("tp", "seq"),
    )
    return jax.shard_map(
        local,
        mesh=mesh,
        in_specs=placed,
        out_specs=(
            P("seq", None),
            P("seq", None),
            P(),
            P("seq", "tp"),
            P("seq", "tp"),
            P(None, "tp"),
            P("tp"),
            P("tp", "seq"),
            P("tp", "seq"),
            P(None, "tp"),
            P("tp"),
            P("tp", "seq"),
            P("seq", "tp"),
            P("seq", "tp"),
            P("tp", "seq"),
            P("seq", "tp"),
            P(("seq", "tp"), None),
            P("tp", "seq"),
            P("seq", "tp"),
            P("seq", "tp"),
            P("tp", "seq"),
        ),
        check_vma=False,
    )
```

```python
import functools
import math

import jax
import jax.numpy as jnp
from jax import lax
from jax.experimental import pallas as pl
from jax.experimental.pallas import tpu as pltpu
from jax.sharding import PartitionSpec as P

HD = 128
CONV = 4
WINDOW = 1024


def product(left, right):
    return jnp.dot(left, right, preferred_element_type=jnp.float32)


def product_left(left, right):
    return lax.dot_general(
        left, right, (((0,), (0,)), ((), ())), preferred_element_type=jnp.float32
    )


def product_right(left, right):
    return lax.dot_general(
        left, right, (((1,), (1,)), ((), ())), preferred_element_type=jnp.float32
    )


def lowered(values):
    return values.astype(jnp.bfloat16)


def rms_norm(values, gain):
    return values * lax.rsqrt(jnp.mean(values * values, axis=-1, keepdims=True) + 1e-06) * gain


def gated(gate_values, up_values):
    return jax.nn.gelu(gate_values) * up_values


def layout(doc_lengths, first_slot, count):
    ends = jnp.cumsum(doc_lengths, dtype=jnp.int32)
    slots = first_slot + jnp.arange(count, dtype=jnp.int32)
    passed = slots[:, None] >= ends[None, :]
    segment = jnp.sum(passed.astype(jnp.int32), axis=1)
    begin = jnp.max(jnp.where(passed, ends[None, :], 0), axis=1)
    segment = jnp.where(slots < 0, -1, segment)
    position = slots - begin
    reset = (slots != begin).astype(jnp.float32)
    valid = (segment < doc_lengths.shape[0]).astype(jnp.float32)
    return (segment, position, reset, valid)


def convolve(extended, taps, bias, segment):
    leading = CONV - 1
    total_rows = extended.shape[0] - leading
    result = bias[None, :] + taps[0][None, :] * extended[leading:]
    for lag_index in range(1, CONV):
        same = (
            segment[leading:] == segment[leading - lag_index : leading - lag_index + total_rows]
        ).astype(jnp.float32)
        result = (
            result
            + same[:, None]
            * taps[lag_index][None, :]
            * extended[leading - lag_index : leading - lag_index + total_rows]
        )
    return result


def coefficients(recur_raw, input_raw, conv_values, bias_pair, decay_values, reset):
    recur_rate = jax.nn.sigmoid(recur_raw + bias_pair[0][None, :])
    input_rate = jax.nn.sigmoid(input_raw + bias_pair[1][None, :])
    log_decay = -8.0 * recur_rate * jax.nn.softplus(-decay_values)[None, :]
    multiplier = jnp.sqrt(jnp.maximum(-jnp.expm1(2.0 * log_decay), 0.01))
    return (jnp.exp(log_decay) * reset[:, None], multiplier * input_rate * conv_values)


def combine_state(earlier, later):
    return (earlier[0] * later[0], later[0] * earlier[1] + later[1])


MESH = pl.DeviceIdType.MESH
LO = 2
EIGHTEEN_US = pl.CostEstimate(flops=0, bytes_accessed=60_000_000, transcendentals=0)
TEN_US = pl.CostEstimate(flops=0, bytes_accessed=33_000_000, transcendentals=0)
ANY = pl.BlockSpec(memory_space=pl.ANY)
VMEM = pl.BlockSpec(memory_space=pltpu.VMEM)


def cube():
    seq = lax.axis_index("seq")
    tp = lax.axis_index("tp")
    a = lax.rem(seq, LO)
    b = tp // 2
    c = lax.rem(tp, 2)
    across_a = (seq - a + 1 - a, tp)
    across_b = (seq, (1 - b) * 2 + c)
    across_c = (seq, b * 2 + 1 - c)
    return (a, b, c, across_a, across_b, across_c)


def hail(devices):
    for device in devices:
        pl.semaphore_signal(
            pltpu.get_barrier_semaphore(), inc=1, device_id=device, device_id_type=MESH
        )


def greet(devices):
    hail(devices)
    pl.semaphore_wait(pltpu.get_barrier_semaphore(), len(devices))


def remote(src, dst, send_sem, recv_sem, slot, device):
    return pltpu.make_async_remote_copy(
        src_ref=src,
        dst_ref=dst,
        send_sem=send_sem.at[slot],
        recv_sem=recv_sem.at[slot],
        device_id=device,
        device_id_type=MESH,
    )


def in_turn(*runs):
    runs = list(runs)
    while runs:
        for run in list(runs):
            if next(run, "end") == "end":
                runs.remove(run)


def neighbours(full):
    across_a, across_b, across_c = cube()[3:]
    return [across_c, across_b] + ([across_a] if full else [])


def gather_steps(full, in_ref, out_ref, send_sem, recv_sem, local_sem):
    a, b, c, across_a, across_b, across_c = cube()
    half = in_ref.shape[0] // 2

    def index(pa, pb, pc):
        return pa * 4 + pb * 2 + pc if full else pb * 2 + pc

    me, an, bn, dn = (
        index(a, b, c),
        index(1 - a, b, c),
        index(a, 1 - b, c),
        index(1 - a, 1 - b, c),
    )
    low, high = (pl.ds(0, half), pl.ds(half, half))
    sent = {}

    def go(slot, src, dst, device):
        copy = remote(src, dst, send_sem, recv_sem, slot, device)
        copy.start()
        sent[slot] = copy

    def own(slot, part, device):
        go(slot, in_ref.at[part], out_ref.at[me, part], device)

    def onward(slot, block, part, device):
        go(slot, out_ref.at[block, part], out_ref.at[block, part], device)

    if full:
        own(0, low, across_a)
    own(1, high, across_b)
    if full:
        own(2, high, across_a)
    own(3, low, across_b)
    go(4, in_ref, out_ref.at[me], across_c)
    mine = pltpu.make_async_copy(in_ref, out_ref.at[me], local_sem)
    mine.start()
    yield
    if full:
        sent[0].wait_recv()
        onward(5, an, low, across_b)
        onward(6, an, low, across_c)
        yield
    sent[1].wait_recv()
    if full:
        onward(7, bn, high, across_a)
    onward(8, bn, high, across_c)
    yield
    if full:
        sent[2].wait_recv()
        onward(9, an, high, across_c)
        yield
    sent[3].wait_recv()
    onward(10, bn, low, across_c)
    yield
    if full:
        sent[5].wait_recv()
        onward(11, dn, low, across_c)
        yield
        sent[7].wait_recv()
        onward(12, dn, high, across_c)
        yield
    for slot in (4, 6, 8, 9, 10, 11, 12):
        if slot in sent:
            sent[slot].wait_recv()
    for copy in sent.values():
        copy.wait_send()
    mine.wait()


def gather_kernel(spans, *refs):
    count = len(spans)
    in_refs, out_refs = (refs[:count], refs[count : 2 * count])
    send_sem, recv_sem, local_sem = refs[2 * count :]
    greet(neighbours(any(spans)))
    in_turn(
        *[
            gather_steps(
                spans[k], in_refs[k], out_refs[k], send_sem.at[k], recv_sem.at[k], local_sem.at[k]
            )
            for k in range(count)
        ]
    )


def gather(blocks, spans, collective_id):
    count = len(blocks)
    ways = [8 if span else 4 for span in spans]
    results = pl.pallas_call(
        functools.partial(gather_kernel, spans),
        out_shape=[
            jax.ShapeDtypeStruct((n, *block.shape), block.dtype) for n, block in zip(ways, blocks)
        ],
        in_specs=[ANY] * count,
        out_specs=[ANY] * count,
        scratch_shapes=[
            pltpu.SemaphoreType.DMA((count, 13)),
            pltpu.SemaphoreType.DMA((count, 13)),
            pltpu.SemaphoreType.DMA((count,)),
        ],
        name="gather_full" if any(spans) else "gather_half",
        cost_estimate=EIGHTEEN_US,
        compiler_params=pltpu.CompilerParams(collective_id=collective_id, has_side_effects=True),
    )(*blocks)
    return [
        result.reshape(n * block.shape[0], block.shape[1])
        for n, result, block in zip(ways, results, blocks)
    ]


def scatter_steps(
    full, part_ref, out_ref, cbuf, sx, sy, tx, ty, ax, by, rx, ry, csend, crecv, send_sem, recv_sem
):
    a, b, c, across_a, across_b, across_c = cube()
    half = part_ref.shape[1] // 2

    def index(pa, pb, pc):
        return pa * 4 + pb * 2 + pc if full else pb * 2 + pc

    def pair(pa, pb):
        return pa * 2 + pb if full else pb

    low, high = (pl.ds(0, half), pl.ds(half, half))
    if full:
        order = [
            (1 - a, 1 - b, low),
            (1 - a, 1 - b, high),
            (1 - a, b, low),
            (a, 1 - b, high),
            (a, 1 - b, low),
            (1 - a, b, high),
            (a, b, low),
            (a, b, high),
        ]
    else:
        order = [(a, 1 - b, low), (a, 1 - b, high), (a, b, low), (a, b, high)]
    core = {}

    def share(*which):
        for k in which:
            pa, pb, part = order[k]
            core[k] = remote(
                part_ref.at[index(pa, pb, 1 - c), part],
                cbuf.at[pair(pa, pb), part],
                csend,
                crecv,
                k,
                across_c,
            )
            core[k].start()

    def summed(k):
        pa, pb, part = order[k]
        core[k].wait_recv()
        return part_ref[index(pa, pb, c), part].astype(jnp.float32) + cbuf[
            pair(pa, pb), part
        ].astype(jnp.float32)

    sent = []

    def go(src, dst, slot, device):
        copy = remote(src, dst, send_sem, recv_sem, slot, device)
        copy.start()
        sent.append(copy)
        return copy

    if full:
        yield
        share(0, 1)
        yield
        share(2, 5)
        sx[0] = lowered(summed(0))
        x0 = go(sx.at[0], ax.at[0], 0, across_a)
        sy[0] = lowered(summed(1))
        y0 = go(sy.at[0], by.at[0], 1, across_b)
        yield
        share(3, 4)
        sx[1] = lowered(summed(2))
        x1 = go(sx.at[1], ax.at[1], 2, across_a)
        yield
        share(6, 7)
        sy[1] = lowered(summed(3))
        y1 = go(sy.at[1], by.at[1], 3, across_b)
        yield
        total = summed(4)
        x0.wait_recv()
        ty[...] = lowered(total + ax[0].astype(jnp.float32))
        last_y = go(ty, ry, 4, across_b)
        total = summed(5)
        y0.wait_recv()
        tx[...] = lowered(total + by[0].astype(jnp.float32))
        last_x = go(tx, rx, 5, across_a)
        yield
        total = summed(6)
        x1.wait_recv()
        total = total + ax[1].astype(jnp.float32)
        last_y.wait_recv()
        out_ref[low] = total + ry[...].astype(jnp.float32)
        total = summed(7)
        y1.wait_recv()
        total = total + by[1].astype(jnp.float32)
        last_x.wait_recv()
        out_ref[high] = total + rx[...].astype(jnp.float32)
    else:
        share(0, 1, 2, 3)
        sy[0] = lowered(summed(0))
        y0 = go(sy.at[0], by.at[0], 1, across_b)
        sy[1] = lowered(summed(1))
        y1 = go(sy.at[1], by.at[1], 3, across_b)
        yield
        total = summed(2)
        y0.wait_recv()
        out_ref[low] = total + by[0].astype(jnp.float32)
        total = summed(3)
        y1.wait_recv()
        out_ref[high] = total + by[1].astype(jnp.float32)
    for copy in [*core.values(), *sent]:
        copy.wait_send()


def scatter_kernel(full, count, *refs):
    greet(neighbours(full))
    in_turn(
        *[
            scatter_steps(full, refs[k], refs[count + k], *refs[2 * count + 13 * k :][:13])
            for k in range(count)
        ]
    )


def scatter_scratch(ways, rows, width):
    half = rows // 2
    shapes = [(ways // 2, rows, width)] + [(2, half, width)] * 2 + [(half, width)] * 2
    shapes += [(2, half, width)] * 2 + [(half, width)] * 2
    return [pltpu.VMEM(shape, jnp.bfloat16) for shape in shapes] + [
        pltpu.SemaphoreType.DMA((k,)) for k in (8, 8, 6, 6)
    ]


def scatter(partials, full, collective_id):
    ways = 8 if full else 4
    count = len(partials)
    rows = partials[0].shape[0] // ways
    scratch = []
    for partial in partials:
        scratch += scatter_scratch(ways, rows, partial.shape[1])
    return pl.pallas_call(
        functools.partial(scatter_kernel, full, count),
        out_shape=[
            jax.ShapeDtypeStruct((rows, partial.shape[1]), jnp.float32) for partial in partials
        ],
        in_specs=[VMEM] * count,
        out_specs=[VMEM] * count,
        scratch_shapes=scratch,
        name="scatter_full" if full else "scatter_half",
        cost_estimate=EIGHTEEN_US,
        compiler_params=pltpu.CompilerParams(
            collective_id=collective_id, has_side_effects=True, vmem_limit_bytes=48 * 2**20
        ),
    )(*[lowered(partial).reshape(ways, rows, -1) for partial in partials])


def scan_kernel(
    high, reverse, decay_ref, drive_ref, end_ref, state_ref, carry_ref, cum, strips, sendbuf, recvbuf, send_sem, recv_sem
):
    rows, width = decay_ref.shape
    strands = 8
    steps = rows // strands
    lanes = 128
    blocks = width // lanes
    mine = lax.axis_index("seq") // LO
    peers = high_peers(high)
    greet(peers)
    for n in range(blocks):
        cum[n] = decay_ref[:, n * lanes : (n + 1) * lanes]
        strips[n] = drive_ref[:, n * lanes : (n + 1) * lanes]

    def step(i, carry):
        r = steps - 1 - i if reverse else i
        at = pl.ds(r, strands, stride=steps)
        new = []
        for n in range(blocks):
            a = cum[n, at, :]
            product_now = carry[2 * n] * a
            state_now = carry[2 * n + 1] * a + strips[n, at, :]
            cum[n, at, :] = product_now
            strips[n, at, :] = state_now
            new += [product_now, state_now]
        return tuple(new)

    ones = jnp.ones((strands, lanes), jnp.float32)
    ends = lax.fori_loop(0, steps, step, (ones, jnp.zeros_like(ones)) * blocks, unroll=8)
    strand_order = list(range(strands - 1, -1, -1)) if reverse else list(range(strands))
    before = {}
    for n in range(blocks):
        total_a = jnp.ones((1, lanes), jnp.float32)
        total_h = jnp.zeros((1, lanes), jnp.float32)
        for k in strand_order:
            before[n, k] = (total_a, total_h)
            a, h = (ends[2 * n][k : k + 1], ends[2 * n + 1][k : k + 1])
            total_h = a * total_h + h
            total_a = a * total_a
        scale = end_ref[0:1, n * lanes : (n + 1) * lanes]
        sendbuf[n, 0:1, :] = total_a * scale
        sendbuf[n, 1:2, :] = total_h * scale
        sendbuf[n, 2:8, :] = jnp.zeros((6, lanes), jnp.float32)
    copies = []
    for k, peer in enumerate(peers):
        copy = remote(sendbuf, recvbuf.at[k], send_sem, recv_sem, k, peer)
        copy.start()
        copies.append(copy)
    for copy in copies:
        copy.wait_recv()
    for n in range(blocks):
        carry = jnp.zeros((1, lanes), jnp.float32)
        for turn in range(high - 1):
            plane = high - 1 - turn if reverse else turn
            away = lax.rem(mine - plane + high, high)
            reached = plane > mine if reverse else plane < mine
            got = recvbuf[jnp.where(reached, away - 1, 0), n]
            carry = jnp.where(reached, got[0:1] * carry + got[1:2], carry)
        span = pl.ds(n * lanes, lanes)
        carry_ref[:, span] = jnp.broadcast_to(carry, (carry_ref.shape[0], lanes))
        for k in range(strands):
            enter = before[n, k][0] * carry + before[n, k][1]
            at = pl.ds(k * steps, steps)
            state_ref[at, span] = strips[n, at, :] + cum[n, at, :] * enter
    for copy in copies:
        copy.wait_send()


def plane_scan(decay, drive, end_scale, high, reverse, collective_id):
    rows, width = decay.shape
    return pl.pallas_call(
        functools.partial(scan_kernel, high, reverse),
        out_shape=(
            jax.ShapeDtypeStruct((rows, width), jnp.float32),
            jax.ShapeDtypeStruct((8, width), jnp.float32),
        ),
        in_specs=[VMEM] * 3,
        out_specs=(VMEM, VMEM),
        scratch_shapes=[
            pltpu.VMEM((width // 128, rows, 128), jnp.float32),
            pltpu.VMEM((width // 128, rows, 128), jnp.float32),
            pltpu.VMEM((width // 128, 8, 128), jnp.float32),
            pltpu.VMEM((high - 1, width // 128, 8, 128), jnp.float32),
            pltpu.SemaphoreType.DMA((high - 1,)),
            pltpu.SemaphoreType.DMA((high - 1,)),
        ],
        name="scan_back" if reverse else "scan",
        cost_estimate=TEN_US,
        compiler_params=pltpu.CompilerParams(
            collective_id=collective_id, has_side_effects=True, vmem_limit_bytes=32 * 2**20
        ),
    )(decay, drive, end_scale)


def small_steps(high, gains_ref, rest_ref, gains_out, rest_out, gbuf, rbuf, ghold, rhold, gpair, rpair, send_sem, recv_sem):
    a, b, c, across_a, across_b, across_c = cube()
    peers = high_peers(high)
    copies = []
    for k, peer in enumerate(peers):
        for n, (src, dst) in enumerate(((gains_ref, gbuf.at[k]), (rest_ref, rbuf.at[k]))):
            copy = remote(src, dst, send_sem, recv_sem, 2 * k + n, peer)
            copy.start()
            copies.append(copy)
    yield
    for copy in copies:
        copy.wait_recv()
    gains = gains_ref[...]
    rest = rest_ref[...]
    for k in range(high - 1):
        gains = gains + gbuf[k]
        rest = rest + rbuf[k]
    rhold[...] = rest
    slot = 2 * (high - 1)
    swap = remote(rhold, rpair, send_sem, recv_sem, slot, across_a)
    swap.start()
    copies.append(swap)
    for n, device in enumerate((across_a, across_b, across_c)):
        ghold[n] = gains
        copy = remote(ghold.at[n], gpair.at[n], send_sem, recv_sem, slot + 1 + n, device)
        copy.start()
        copies.append(copy)
        yield
        copy.wait_recv()
        gains = gains + gpair[n]
    swap.wait_recv()
    gains_out[...] = gains
    other = rpair[...]
    width = rest.shape[1]
    rest_out[:, :width] = jnp.where(a == 0, rest, other)
    rest_out[:, width:] = jnp.where(a == 0, other, rest)
    for copy in copies:
        copy.wait_send()


def high_peers(high):
    seq = lax.axis_index("seq")
    tp = lax.axis_index("tp")
    return [(lax.rem(seq // LO + k, high) * LO + lax.rem(seq, LO), tp) for k in range(1, high)]


def last_kernel(high, part_ref, gains_ref, rest_ref, in_ref, out_ref, gains_out, rest_out, all_ref, *more):
    greet(high_peers(high) + neighbours(True))
    in_turn(
        small_steps(high, gains_ref, rest_ref, gains_out, rest_out, *more[13:21]),
        scatter_steps(True, part_ref, out_ref, *more[:13]),
        gather_steps(False, in_ref, all_ref, *more[21:]),
    )


def scatter_and_sums(partial, gains, rest, block, high, collective_id):
    slots = 2 * (high - 1) + 4
    ways = 8
    width = partial.shape[1]
    rows = partial.shape[0] // ways
    *sums, gathered = pl.pallas_call(
        functools.partial(last_kernel, high),
        out_shape=[
            jax.ShapeDtypeStruct((rows, width), jnp.float32),
            jax.ShapeDtypeStruct(gains.shape, jnp.float32),
            jax.ShapeDtypeStruct((rest.shape[0], LO * rest.shape[1]), jnp.float32),
            jax.ShapeDtypeStruct((4, *block.shape), block.dtype),
        ],
        in_specs=[VMEM] * 3 + [ANY],
        out_specs=[VMEM] * 3 + [ANY],
        scratch_shapes=scatter_scratch(ways, rows, width)
        + [
            pltpu.VMEM((high - 1, *gains.shape), jnp.float32),
            pltpu.VMEM((high - 1, *rest.shape), jnp.float32),
            pltpu.VMEM((3, *gains.shape), jnp.float32),
            pltpu.VMEM(rest.shape, jnp.float32),
            pltpu.VMEM((3, *gains.shape), jnp.float32),
            pltpu.VMEM(rest.shape, jnp.float32),
            pltpu.SemaphoreType.DMA((slots,)),
            pltpu.SemaphoreType.DMA((slots,)),
            pltpu.SemaphoreType.DMA((13,)),
            pltpu.SemaphoreType.DMA((13,)),
            pltpu.SemaphoreType.DMA,
        ],
        name="scatter_and_sums",
        cost_estimate=EIGHTEEN_US,
        compiler_params=pltpu.CompilerParams(
            collective_id=collective_id, has_side_effects=True, vmem_limit_bytes=40 * 2**20
        ),
    )(lowered(partial).reshape(ways, rows, width), gains, rest, block)
    return (*sums, gathered.reshape(-1, block.shape[1]))


def gelu_parts(x):
    inner = math.sqrt(2 / math.pi)
    curve = jnp.tanh(inner * (x + 0.044715 * x * x * x))
    half = 0.5 * (1 + curve)
    slope = half + 0.5 * x * (1 - curve * curve) * inner * (1 + 3 * 0.044715 * x * x)
    return (x * half, slope)


def dense_kernel(mode, main, *refs):
    refs = list(refs)

    def take(wanted=True):
        return refs.pop(0) if wanted else None

    grads = mode in ("both", "backward")
    fresh = mode in ("both", "forward")
    n_hbm = take(mode != "product")
    g_hbm = take(grads)
    w_hbm = take()
    ab_hbm = take(mode == "backward")
    hid_in = take(mode == "product")
    out_ref = take()
    wire_hbm = take(grads)
    ab_out = take(mode == "forward")
    hid_out = take(mode == "both")
    w_v, hid_v, part_v = (take(), take(), take())
    n_v = take(mode != "product")
    g_v, low_v, wire_v = (take(grads), take(grads), take(grads))
    ab_v = take(mode in ("forward", "backward"))
    buffers = [take() for _ in range(13)]
    sems = take()
    lanes = 128
    both = 2 * main + lanes
    tile = 256
    a, b = cube()[:2]
    near = neighbours(True)
    hail(near)
    up_part, down_part = (pl.ds(0, both), pl.ds(both, w_v.shape[1] - both))
    loads = {}

    def load(name, src, dst):
        loads[name] = pltpu.make_async_copy(src, dst, sems.at[len(loads)])
        loads[name].start()

    def need(*names):
        for name in names:
            if name in loads:
                loads.pop(name).wait()

    tiles = ((1 - a, 1 - b), (1 - a, b), (a, 1 - b), (a, b))

    def rows_of(pa, pb):
        return pl.ds(pl.multiple_of((pa * 4 + pb * 2) * lanes, tile), tile)

    def load_rows(turn, **pairs):
        at = rows_of(*tiles[turn])
        for name, (src, dst) in pairs.items():
            if src is not None:
                load(f"{name}{turn}", src.at[at], dst.at[at])

    for turn in range(4):
        load_rows(turn, n=(n_hbm, n_v), hid=(hid_in, hid_v), ab=(ab_hbm, ab_v))
        if turn == 0 and mode != "product":
            load("up", w_hbm.at[:, up_part], w_v.at[:, up_part])
        load_rows(turn, g=(g_hbm, g_v))
        if turn == 0:
            load("down", w_hbm.at[:, down_part], w_v.at[:, down_part])

    def work(turn):
        pa, pb = tiles[turn]
        block = pa * 4 + pb * 2
        at = rows_of(pa, pb)
        if mode == "product":
            need(f"hid{turn}", "down")
            part = lowered(product_right(hid_v[at, :], w_v[:, both:]))
            part_v[pl.ds(block, 2)] = part.reshape(2, lanes, part.shape[1])
            return
        need(f"n{turn}")
        if fresh:
            need("up")
            ab = product(n_v[at, :], w_v[:, :both])
            if mode == "forward":
                ab_v[at, :] = ab
        else:
            need(f"ab{turn}")
            ab = ab_v[at, :]
        gate, up, tail = (ab[:, :main], ab[:, main : 2 * main], ab[:, 2 * main :])
        first = lax.broadcasted_iota(jnp.int32, tail.shape, 1) < lanes // 2
        turned = pltpu.roll(tail, lanes // 2, 1)
        act, slope = gelu_parts(gate)
        tail_act, tail_slope = gelu_parts(tail)
        hid_v[at, :main] = lowered(act * up)
        hid_v[at, main:] = lowered(jnp.where(first, tail_act * turned, 0.0))
        need(f"g{turn}", "down")
        if grads:
            grad = product(g_v[at, :], w_v[:, both:])
            grad_main, grad_tail = (grad[:, :main], grad[:, main:])
            low_v[at, :main] = lowered(grad_main * up * slope)
            low_v[at, main : 2 * main] = lowered(grad_main * act)
            turned_grad = pltpu.roll(grad_tail, lanes // 2, 1)
            turned_act = pltpu.roll(tail_act, lanes // 2, 1)
            low_v[at, 2 * main :] = lowered(
                jnp.where(first, grad_tail * turned * tail_slope, turned_grad * turned_act)
            )
            need("up")
            part = lowered(product_right(low_v[at, :], w_v[:, :both]))
        else:
            part = lowered(product_right(hid_v[at, :], w_v[:, both:]))
        part_v[pl.ds(block, 2)] = part.reshape(2, lanes, part.shape[1])

    schedule = scatter_steps(True, part_v, out_ref, *buffers)
    next(schedule)
    for turn in range(4):
        work(turn)
        if turn == 0:
            pl.semaphore_wait(pltpu.get_barrier_semaphore(), len(near))
        next(schedule)
    stores = []

    def store(src, dst, slot):
        copy = pltpu.make_async_copy(src, dst, sems.at[slot])
        copy.start()
        stores.append(copy)

    if mode == "both":
        store(hid_v, hid_out, 16)
    if mode == "forward":
        store(ab_v, ab_out, 16)
    if grads:
        depth = w_v.shape[0]

        def weight_grads(i, carry):
            cols = pl.ds(pl.multiple_of(i * tile, tile), tile)
            wire_v[cols, :both] = lowered(product_left(n_v[:, cols], low_v[...]))
            wire_v[cols, both:] = lowered(product_left(g_v[:, cols], hid_v[...]))
            return carry

        split = depth // tile // 2
        lax.fori_loop(0, split, weight_grads, 0)
        store(wire_v.at[pl.ds(0, split * tile)], wire_hbm.at[pl.ds(0, split * tile)], 17)
        next(schedule)
        lax.fori_loop(split, depth // tile, weight_grads, 0)
        rest = pl.ds(split * tile, depth - split * tile)
        store(wire_v.at[rest], wire_hbm.at[rest], 18)
    else:
        next(schedule)
    next(schedule, None)
    for copy in stores:
        copy.wait()


def dense_call(mode, rows_in, grad_low, weights, ab, collective_id):
    rows = rows_in.shape[0]
    depth, columns = weights.shape
    main = (columns // 128 - 2) // 3 * 128
    both = 2 * main + 128
    grads = mode in ("both", "backward")
    low = jnp.bfloat16
    wide = ((rows, depth), low)
    hidden = ((rows, columns - both), low)
    if mode == "product":
        operands = [weights, rows_in]
    else:
        operands = [rows_in] + ([grad_low] if grads else []) + [weights]
    if mode == "backward":
        operands.append(ab)
    extra = {
        "forward": [((rows, both), jnp.float32)],
        "backward": [(weights.shape, low)],
        "both": [(weights.shape, low), hidden],
        "product": [],
    }[mode]
    scratch = [(weights.shape, low), hidden, ((8, rows // 8, depth), low)]
    if mode != "product":
        scratch.append(wide)
    if grads:
        scratch += [wide, ((rows, both), low), (weights.shape, low)]
    if mode in ("forward", "backward"):
        scratch.append(((rows, both), jnp.float32))
    return pl.pallas_call(
        functools.partial(dense_kernel, mode, main),
        out_shape=[
            jax.ShapeDtypeStruct(shape, kind)
            for shape, kind in [((rows // 8, depth), jnp.float32)] + extra
        ],
        in_specs=[ANY] * len(operands),
        out_specs=[VMEM] + [ANY] * len(extra),
        scratch_shapes=[pltpu.VMEM(shape, kind) for shape, kind in scratch]
        + scatter_scratch(8, rows // 8, depth)
        + [pltpu.SemaphoreType.DMA((19,))],
        name="dense_" + mode,
        cost_estimate=pl.CostEstimate(
            flops=0, bytes_accessed=100_000_000 if grads else 75_000_000, transcendentals=0
        ),
        compiler_params=pltpu.CompilerParams(
            collective_id=collective_id, has_side_effects=True, vmem_limit_bytes=56 * 2**20
        ),
    )(*operands)


def attention_kernel(
    shift, query_ref, ext_ref, here_ref, there_ref, cos_ref, sin_ref, out_ref, rot_ref, log_ref
):
    tile = 256
    rows, width = query_ref.shape
    heads = width // HD
    reach = shift + tile
    scale = HD ** (-0.5)
    log_ref[...] = jnp.zeros_like(log_ref)

    def turn(n, carry):
        h = n // (rows // tile)
        first = pl.multiple_of(lax.rem(n, rows // tile) * tile, tile)
        lanes = pl.ds(pl.multiple_of(h * HD, HD), HD)
        at = pl.ds(first, tile)
        seen = pl.ds(first, reach)
        query = query_ref[at, lanes]
        query = query * cos_ref[at, :] + pltpu.roll(query, HD // 2, 1) * sin_ref[at, :]
        query = lowered(query)
        rot_ref[at, lanes] = query
        allowed = visible(shift, there_ref[seen, :], here_ref[0:1, at])
        scores = jnp.where(allowed, product_right(ext_ref[seen, :HD], query) * scale, -1e30)
        top = jnp.max(scores, axis=0, keepdims=True)
        probs = jnp.exp(scores - top)
        total = jnp.sum(probs, axis=0, keepdims=True)
        log_ref[pl.ds(h, 1), at] = top + jnp.log(total)
        out_ref[at, lanes] = lowered(product_left(lowered(probs / total), ext_ref[seen, HD:]))
        return carry

    lax.fori_loop(0, heads * (rows // tile), turn, 0)


def visible(shift, there, here):
    shape = (there.shape[0], here.shape[1])
    distance = (
        lax.broadcasted_iota(jnp.int32, shape, 1) - lax.broadcasted_iota(jnp.int32, shape, 0) + shift
    )
    return (there == here) & (distance >= 0) & (distance < WINDOW)


def attention(query, extended, here, there, cosine, sine):
    rows, width = query.shape
    return pl.pallas_call(
        functools.partial(attention_kernel, extended.shape[0] - rows),
        out_shape=[
            jax.ShapeDtypeStruct((rows, width), jnp.bfloat16),
            jax.ShapeDtypeStruct((rows, width), jnp.bfloat16),
            jax.ShapeDtypeStruct((8, rows), jnp.float32),
        ],
        in_specs=[VMEM] * 6,
        out_specs=[VMEM] * 3,
        name="attention",
        cost_estimate=TEN_US,
        compiler_params=pltpu.CompilerParams(vmem_limit_bytes=48 * 2**20),
    )(query, extended, here, there, cosine, sine)


def attention_back_kernel(
    shift, query_ref, ext_ref, grad_ref, log_ref, here_ref, there_ref, cos_ref, sin_ref, dquery_ref, dext_ref, total
):
    tile = 256
    rows, width = query_ref.shape
    heads = width // HD
    reach = shift + tile
    scale = HD ** (-0.5)
    total[...] = jnp.zeros_like(total)

    def turn(n, carry):
        h = n // (rows // tile)
        first = pl.multiple_of(lax.rem(n, rows // tile) * tile, tile)
        lanes = pl.ds(pl.multiple_of(h * HD, HD), HD)
        at = pl.ds(first, tile)
        seen = pl.ds(first, reach)
        query = query_ref[at, lanes]
        grad = grad_ref[at, lanes]
        keys = ext_ref[seen, :HD]
        values = ext_ref[seen, HD:]
        allowed = visible(shift, there_ref[seen, :], here_ref[0:1, at])
        scores = jnp.where(allowed, product_right(keys, query) * scale, -1e30)
        probs = jnp.exp(scores - log_ref[pl.ds(h, 1), at])
        grad_probs = product_right(values, grad)
        mean = jnp.sum(probs * grad_probs, axis=0, keepdims=True)
        grad_scores = lowered(probs * (grad_probs - mean) * scale)
        total[seen, :HD] += product(grad_scores, query)
        total[seen, HD:] += product(lowered(probs), grad)
        turned = product_left(grad_scores, keys)
        turned = turned * cos_ref[at, :] - pltpu.roll(turned, HD // 2, 1) * sin_ref[at, :]
        dquery_ref[at, lanes] = lowered(turned)
        return carry

    lax.fori_loop(0, heads * (rows // tile), turn, 0)
    dext_ref[...] = lowered(total[...])


def attention_back(query_rot, extended, grad, log_total, here, there, cosine, sine):
    rows, width = query_rot.shape
    seen = extended.shape[0]
    return pl.pallas_call(
        functools.partial(attention_back_kernel, seen - rows),
        out_shape=[
            jax.ShapeDtypeStruct((rows, width), jnp.bfloat16),
            jax.ShapeDtypeStruct((seen, 2 * HD), jnp.bfloat16),
        ],
        in_specs=[VMEM] * 8,
        out_specs=[VMEM] * 2,
        scratch_shapes=[pltpu.VMEM((seen, 2 * HD), jnp.float32)],
        name="attention_back",
        cost_estimate=EIGHTEEN_US,
        compiler_params=pltpu.CompilerParams(vmem_limit_bytes=48 * 2**20),
    )(query_rot, extended, grad, log_total, here, there, cosine, sine)


def stacked_by_low(mine, other):
    lo = lax.rem(lax.axis_index("seq"), LO)
    return jnp.stack([jnp.where(lo == 0, mine, other), jnp.where(lo == 0, other, mine)])


def swap_low(block):
    count = lax.axis_size("seq")
    return lax.ppermute(block, "seq", [(s, s // LO * LO + (1 - s % LO)) for s in range(count)])


def high_groups():
    count = lax.axis_size("seq")
    return [[h * LO + l for h in range(count // LO)] for l in range(LO)]


def swap_columns(*parts):
    return swap_pieces([jnp.concatenate(each, axis=1) for each in zip(*map(split_columns, parts))])


def swap_pieces(halves):
    lo = lax.rem(lax.axis_index("seq"), LO)
    kept = jnp.where(lo == 0, halves[0], halves[1])
    given = jnp.where(lo == 0, halves[1], halves[0])
    both = stacked_by_low(kept, swap_low(given))
    return both.reshape(-1, both.shape[2])


def gather_high(rows):
    return lax.all_gather(rows, "seq", axis=0, tiled=True, axis_index_groups=high_groups())


def reduce_high(grad):
    return lax.psum_scatter(
        lowered(grad), "seq", scatter_dimension=0, tiled=True, axis_index_groups=high_groups()
    )


def exchanged(both):
    lo = lax.rem(lax.axis_index("seq"), LO)
    both = both.reshape(LO, -1, both.shape[1])
    kept = jnp.where(lo == 0, both[0], both[1])
    given = jnp.where(lo == 0, both[1], both[0])
    return stacked_by_low(kept, swap_low(given))


def split_columns(block):
    width = block.shape[1] // LO
    return [block[:, l * width : (l + 1) * width] for l in range(LO)]


def joined(blocks):
    return jnp.concatenate([blocks[l] for l in range(LO)], axis=1).astype(jnp.float32)


def block_product(values, weight):
    block_width = weight.shape[0]
    blocks = weight.shape[1] // block_width
    return jnp.concatenate(
        [
            product_right(
                values[:, n * block_width : (n + 1) * block_width],
                weight[:, n * block_width : (n + 1) * block_width],
            )
            for n in range(blocks)
        ],
        axis=1,
    )


def block_grads(values, weight, upstream):
    block_width = weight.shape[0]
    cuts = [slice(n * block_width, (n + 1) * block_width) for n in range(weight.shape[1] // block_width)]
    return (
        jnp.concatenate([product_left(upstream[:, s], values[:, s]) for s in cuts], axis=1),
        jnp.concatenate([product(upstream[:, s], weight[:, s]) for s in cuts], axis=1),
    )


def shifted(block, distance):
    count = lax.axis_size("seq")
    route = [(i - distance, i) for i in range(count) if 0 <= i - distance < count]
    return lax.ppermute(block, "seq", route)


CIDS = {
    "gather_full": 0,
    "gather_half": 1,
    "scatter_full": 2,
    "scatter_half": 3,
    "scan": 4,
    "scan_back": 5,
    "scatter_wide": 6,
    "last": 7,
    "gather_narrow": 8,
    "gather_two": 9,
    "forward": 10,
    "both": 11,
    "backward": 12,
    "gather_weight": 13,
    "gather_seen": 14,
    "product": 15,
}


def dense_wire(gate, up, down):
    pieces = []
    for g, u, d in zip(*map(split_columns, (gate, up, down))):
        main = g.shape[1] // 128 * 128
        blank = jnp.zeros((d.shape[0], -d.shape[1] % 128), d.dtype)
        pieces.append(
            jnp.concatenate([g[:, :main], u[:, :main], g[:, main:], u[:, main:], d, blank], axis=1)
        )
    return pieces


def dense_grads(both):
    columns = both.shape[2]
    main = (columns // 128 - 2) // 3 * 128
    tail = 64
    ends = 2 * main

    def part(first, last):
        return jnp.concatenate([both[:, :, first : first + main], both[:, :, last : last + tail]], axis=2)

    return (
        joined(part(0, ends)),
        joined(part(main, ends + tail)),
        joined(both[:, :, ends + 2 * tail : ends + 3 * tail + main]).T,
    )


def turns(position):
    half_width = HD // 2
    frequency = 10000.0 ** (-jnp.arange(half_width, dtype=jnp.float32) / half_width)
    angle = position.astype(jnp.float32)[:, None] * jnp.tile(frequency, 2)[None, :]
    sign = jnp.where(jnp.arange(HD) < half_width, -1.0, 1.0)
    return (jnp.cos(angle), jnp.sin(angle) * sign[None, :])


def rotate(values, factors):
    cosine, sine = factors
    half_width = HD // 2
    swapped = jnp.concatenate([values[..., half_width:], values[..., :half_width]], axis=-1)
    return values * cosine + swapped * sine


def rotate_back(values, factors):
    cosine, sine = factors
    half_width = HD // 2
    swapped = jnp.concatenate([values[..., half_width:], values[..., :half_width]], axis=-1)
    return values * cosine - swapped * sine


def both_lows(lanes):
    other = swap_low(lanes)
    lo = lax.rem(lax.axis_index("seq"), LO)
    both = jnp.stack([jnp.where(lo == 0, lanes, other), jnp.where(lo == 0, other, lanes)], axis=1)
    return both.reshape(-1, lanes.shape[2])


def swap_sums(grad):
    lo = lax.rem(lax.axis_index("seq"), LO)
    pairs = grad.reshape(lax.axis_size("seq") // LO, LO, -1, grad.shape[1])
    kept = jnp.where(lo == 0, pairs[:, 0], pairs[:, 1])
    given = jnp.where(lo == 0, pairs[:, 1], pairs[:, 0])
    return (kept.reshape(-1, grad.shape[1]), swap_low(given).reshape(-1, grad.shape[1]))


def local(
    tokens,
    cotangent,
    doc_lengths,
    norm_gains,
    input_branch,
    gate_branch,
    conv_taps,
    conv_bias,
    recur_gate,
    input_gate,
    gate_biases,
    decay_param,
    recur_output,
    dense_gate_one,
    dense_up_one,
    dense_down_one,
    query_weight,
    keyvalue_weight,
    attention_out,
    dense_gate_two,
    dense_up_two,
    dense_down_two,
):
    cid = CIDS
    shard_rows = tokens.shape[0]
    seq = lax.axis_index("seq")
    tp = lax.axis_index("tp")
    lo = lax.rem(seq, LO)
    high = lax.axis_size("seq") // LO
    ways = lax.axis_size("tp")
    own_rows = shard_rows // ways
    plane_rows = shard_rows * LO
    channels = conv_bias.shape[0] // LO
    leading = CONV - 1
    halo_shards = WINDOW // shard_rows
    first_slot = seq * shard_rows
    plane_slot = (seq // LO) * plane_rows
    own_slot = first_slot + tp * own_rows
    valid = layout(doc_lengths, own_slot, own_rows)[3]
    segment, position, _, _ = layout(doc_lengths, first_slot, shard_rows)
    plane_reset = layout(doc_lengths, plane_slot, plane_rows)[2]
    conv_segment = layout(doc_lengths, plane_slot - leading, plane_rows + leading)[0]
    key_segment = layout(
        doc_lengths, first_slot - halo_shards * shard_rows, (halo_shards + 1) * shard_rows
    )[0]

    def ours(block, axis):
        return lax.dynamic_slice_in_dim(block, lo * channels, channels, axis)

    taps, bias = (ours(conv_taps, 1), ours(conv_bias, 0))
    bias_pair, decay_values = (ours(gate_biases, 1), ours(decay_param, 0))

    gate_rows = recur_gate.shape[1]
    weight_rows = input_branch.shape[0]
    attn_rows = jnp.concatenate([query_weight, attention_out.T], axis=1)
    query_width = query_weight.shape[1]
    third = jnp.concatenate(
        [attn_rows, keyvalue_weight.reshape(-1, attn_rows.shape[1])], axis=0
    )

    own_tokens = lax.dynamic_slice_in_dim(tokens, tp * own_rows, own_rows, 0)
    own_cotangent = lax.dynamic_slice_in_dim(cotangent, tp * own_rows, own_rows, 0)
    stream_in = own_tokens.astype(jnp.float32)
    grad_stream = own_cotangent.astype(jnp.float32) * valid[:, None]
    first = swap_columns(
        jnp.concatenate([input_branch, recur_gate.T], axis=0),
        jnp.concatenate([gate_branch, input_gate.T], axis=0),
        jnp.concatenate([recur_output.T, jnp.zeros_like(recur_gate.T)], axis=0),
    )
    normed_own = lowered(rms_norm(stream_in, norm_gains[0]))
    grad_own = lowered(grad_stream)
    first, normed_own, grad_own, dense_gate_one = lax.optimization_barrier(
        (first, normed_own, grad_own, dense_gate_one)
    )
    third_rows = third.shape[0]
    early_wires = lax.all_gather(
        jnp.concatenate([third, first], axis=0), "seq", axis_index_groups=high_groups()
    )
    normed_one, grad_low = gather([normed_own, grad_own], [True, True], cid["gather_two"])
    second = swap_pieces(dense_wire(dense_gate_one, dense_up_one, dense_down_one.T))
    second, dense_gate_two = lax.optimization_barrier((second, dense_gate_two))
    fourth = swap_pieces(dense_wire(dense_gate_two, dense_up_two, dense_down_two.T))
    normed_one, early_wires, grad_low, second, fourth = lax.optimization_barrier(
        (normed_one, early_wires, grad_low, second, fourth)
    )
    third = early_wires[:, :third_rows]
    first_full = early_wires[:, third_rows:]
    first_full = first_full.reshape(high * LO, weight_rows + gate_rows, 3 * channels)
    in_full = first_full[:, :weight_rows, : 2 * channels].reshape(-1, 2 * channels)
    output_full = first_full[:, :weight_rows, 2 * channels :].reshape(-1, channels)
    recur_full = first_full[:, weight_rows:, :channels].reshape(-1, channels)
    input_gate_full = first_full[:, weight_rows:, channels : 2 * channels].reshape(-1, channels)
    weights_one = gather_high(second)
    third = both_lows(third)
    both = product(normed_one, in_full)

    branch = both[:, :channels]
    gating = both[:, channels:]
    rim = shifted(branch[plane_rows - leading :], LO)
    branch_ext = jnp.concatenate([rim, branch], axis=0)
    conv_local = functools.partial(convolve, segment=conv_segment)
    conv_out, conv_pull = jax.vjp(conv_local, branch_ext, taps, bias)
    conv_low = lowered(conv_out)
    recur_raw = block_product(conv_low, recur_full)
    input_raw = block_product(conv_low, input_gate_full)
    rate_local = functools.partial(coefficients, reset=plane_reset)
    (decay, drive), rate_pull = jax.vjp(
        rate_local, recur_raw, input_raw, conv_out, bias_pair, decay_values
    )
    ones = jnp.ones((8, channels), jnp.float32)
    state, state_in = plane_scan(decay, drive, ones, high, False, cid["scan"])
    gate_act, gate_pull = jax.vjp(jax.nn.gelu, gating)
    mixed = lowered(state * gate_act)
    mixed, third = lax.optimization_barrier((mixed, third))
    (summed,) = scatter([product_right(mixed, output_full)], True, cid["scatter_full"])
    stream_one = stream_in + summed
    third = third.reshape(high * LO, -1, third.shape[1])
    query_full = third[:, :weight_rows, :query_width].reshape(-1, query_width)
    attn_full = third[:, :weight_rows, query_width:].reshape(-1, third.shape[2] - query_width)
    part_rows, part_width = keyvalue_weight.shape
    normed_two, keyvalue_full = gather(
        [lowered(rms_norm(stream_one, norm_gains[1])), third[:, weight_rows:].reshape(-1, part_width)],
        [True, False],
        cid["gather_weight"],
    )
    keyvalue_full = keyvalue_full.reshape(ways, high * LO, part_rows, part_width)
    keyvalue_full = keyvalue_full.transpose(1, 0, 2, 3).reshape(-1, part_width)
    factors = turns(position)
    own_factors = [lax.dynamic_slice_in_dim(each, tp * own_rows, own_rows, 0) for each in factors]
    segment_rows = jnp.broadcast_to(segment[None], (8, shard_rows))
    key_column = key_segment[:, None]
    early = (keyvalue_full, query_full, attn_full, factors, own_factors, segment_rows, key_column)
    normed_two, early = lax.optimization_barrier((normed_two, early))
    keyvalue_full, query_full, attn_full, factors, own_factors, segment_rows, key_column = early
    normed_two, weights_one, fourth = lax.optimization_barrier((normed_two, weights_one, fourth))
    weights_two = gather_high(fourth)
    summed, ab_one = dense_call("forward", normed_two, None, weights_one, None, cid["forward"])
    stream_two = stream_one + summed

    normed_own = lowered(rms_norm(stream_two, norm_gains[2]))
    keyval = product(normed_own, keyvalue_full)
    key_rot = lowered(rotate(keyval[:, :HD], own_factors))
    packed = jnp.concatenate([key_rot, lowered(keyval[:, HD:])], axis=1)
    earlier = [shifted(packed, offset) for offset in range(halo_shards, 0, -1)]
    normed_three, seen = gather(
        [normed_own, jnp.concatenate(earlier + [packed], axis=1)], [False, False], cid["gather_seen"]
    )
    extended = jnp.concatenate(
        [seen[:, 2 * HD * k : 2 * HD * (k + 1)] for k in range(halo_shards + 1)], axis=0
    )
    query = product(normed_three, query_full)
    attended, query_rot, log_total = attention(
        query, extended, segment_rows, key_column, *factors
    )
    (summed,) = scatter([product_right(attended, attn_full)], False, cid["scatter_half"])
    stream_three = stream_two + summed

    (normed_four,) = gather(
        [lowered(rms_norm(stream_three, norm_gains[3]))], [True], cid["gather_full"]
    )
    grad_normed, wire_two, hidden_two = dense_call(
        "both", normed_four, grad_low, weights_two, None, cid["both"]
    )
    done_two = reduce_high(wire_two)
    stream_grad, gain_four = jax.vjp(rms_norm, stream_three, norm_gains[3])[1](grad_normed)
    grad_stream = grad_stream + stream_grad
    (grad_attn_low,) = gather([lowered(grad_stream)], [False], cid["gather_half"])
    grad_attn_out = product_left(grad_attn_low, attended)
    grad_attended = lowered(product(grad_attn_low, attn_full))
    grad_query_low, grad_ext = attention_back(
        query_rot,
        extended,
        grad_attended,
        log_total,
        segment_rows,
        key_column,
        *factors,
    )
    grad_query = product_left(normed_three, grad_query_low)
    grad_pieces = grad_ext.reshape(halo_shards + 1, shard_rows, 2 * HD)
    partial = jnp.concatenate(
        [lowered(product_right(grad_query_low, query_full))] + list(grad_pieces), axis=1
    )
    partial, grad_query, grad_attn_out = lax.optimization_barrier(
        (partial, lowered(grad_query), lowered(grad_attn_out))
    )
    attn_kept, attn_given = swap_sums(jnp.concatenate([grad_query, grad_attn_out], axis=1))
    (summed,) = scatter([partial], False, cid["scatter_wide"])
    width = normed_own.shape[1]
    pieces = [
        summed[:, width + 2 * HD * k : width + 2 * HD * (k + 1)] for k in range(halo_shards + 1)
    ]
    keyvalue_total = pieces[halo_shards]
    for offset in range(1, halo_shards + 1):
        piece = shifted(lowered(pieces[halo_shards - offset]), -offset)
        keyvalue_total = keyvalue_total + piece.astype(jnp.float32)
    keyvalue_total, attn_given = lax.optimization_barrier((keyvalue_total, attn_given))
    done_attn = reduce_high(attn_kept.astype(jnp.float32) + attn_given.astype(jnp.float32))
    key_grad = rotate_back(keyvalue_total[:, :HD], own_factors)
    keyvalue_low = lowered(jnp.concatenate([key_grad, keyvalue_total[:, HD:]], axis=1))
    grad_normed = summed[:, :width] + product_right(keyvalue_low, keyvalue_full)
    stream_grad, gain_three = jax.vjp(rms_norm, stream_two, norm_gains[2])[1](grad_normed)
    grad_stream = grad_stream + stream_grad

    (grad_low,) = gather([lowered(grad_stream)], [True], cid["gather_full"])
    grad_low, done_two = lax.optimization_barrier((grad_low, done_two))
    done_two = dense_grads(exchanged(done_two))
    grad_normed, one_wire = dense_call(
        "backward", normed_two, grad_low, weights_one, ab_one, cid["backward"]
    )
    stream_grad, gain_two = jax.vjp(rms_norm, stream_one, norm_gains[1])[1](grad_normed)
    grad_stream = grad_stream + stream_grad
    grad_stream, one_wire, done_attn = lax.optimization_barrier(
        (grad_stream, one_wire, done_attn)
    )
    grad_stream, keyvalue_low = lax.optimization_barrier((grad_stream, keyvalue_low))
    done_one = reduce_high(one_wire)
    (keyvalue_grads,) = gather([keyvalue_low], [False], cid["gather_narrow"])
    grad_keyvalue = lowered(product_left(normed_three, keyvalue_grads))
    grad_keyvalue = grad_keyvalue.reshape(high * LO, ways, part_rows, part_width)
    grad_keyvalue = lax.dynamic_slice_in_dim(grad_keyvalue, tp, 1, 1)
    (grad_out_low,) = gather([lowered(grad_stream)], [True], cid["gather_full"])
    grad_out_low, hidden_two = lax.optimization_barrier((grad_out_low, hidden_two))
    (summed_four,) = dense_call("product", hidden_two, None, weights_two, None, cid["product"])
    grad_recur_out = product_left(grad_out_low, mixed)
    grad_mixed = product(grad_out_low, output_full)
    grad_mixed, done_attn, done_two = lax.optimization_barrier((grad_mixed, done_attn, done_two))
    done_attn = done_attn.astype(jnp.float32)
    grad_state = grad_mixed * gate_act
    grad_gating = lowered(gate_pull(grad_mixed * state)[0])
    decay_next = jnp.concatenate([decay[1:], jnp.ones((1, channels), jnp.float32)], axis=0)
    first_decay = jnp.broadcast_to(decay[:1], (8, channels))
    grad_drive, _ = plane_scan(decay_next, grad_state, first_decay, high, True, cid["scan_back"])
    state_prev = jnp.concatenate([state_in[:1], state[:-1]], axis=0)
    grad_decay = grad_drive * state_prev
    grad_recur_raw, grad_input_raw, grad_conv, grad_biases, grad_decay_param = rate_pull(
        (grad_decay, grad_drive)
    )
    grad_recur_gate, conv_back_recur = block_grads(conv_low, recur_full, lowered(grad_recur_raw))
    grad_input_gate, conv_back_input = block_grads(
        conv_low, input_gate_full, lowered(grad_input_raw)
    )
    grad_branch_ext, grad_taps, grad_conv_bias = conv_pull(
        grad_conv + conv_back_recur + conv_back_input
    )
    returned_rim = shifted(grad_branch_ext[:leading], -LO)
    grad_branch = grad_branch_ext[leading:] + jnp.pad(
        returned_rim, ((plane_rows - leading, 0), (0, 0))
    )
    both_low = jnp.concatenate([lowered(grad_branch), grad_gating], axis=1)
    grad_in = product_left(normed_one, both_low)
    partial = lowered(product_right(both_low, in_full))
    partial, grad_in, grad_recur_out = lax.optimization_barrier(
        (partial, lowered(grad_in), lowered(grad_recur_out))
    )
    blocks = high * LO
    wire = jnp.concatenate(
        [
            jnp.concatenate(
                [
                    grad_in.reshape(blocks, weight_rows, 2 * channels),
                    grad_recur_out.reshape(blocks, weight_rows, channels),
                ],
                axis=2,
            ),
            jnp.concatenate(
                [
                    lowered(grad_recur_gate).reshape(blocks, gate_rows, channels),
                    lowered(grad_input_gate).reshape(blocks, gate_rows, channels),
                    jnp.zeros((blocks, gate_rows, channels), jnp.bfloat16),
                ],
                axis=2,
            ),
            grad_keyvalue.reshape(blocks, -1, 3 * channels),
        ],
        axis=1,
    )
    wire, done_one, summed_four = lax.optimization_barrier((wire, done_one, summed_four))
    layer_own = lowered((stream_three + summed_four) * valid[:, None])
    last = reduce_high(wire.reshape(-1, 3 * channels))
    gain_one = jnp.sum(normed_one.astype(jnp.float32) * partial.astype(jnp.float32), axis=0)
    gain_one = gain_one / norm_gains[0]
    grad_normed, gains_sum, small, layer_out = scatter_and_sums(
        partial,
        jnp.concatenate(
            [jnp.stack([gain_one, gain_two, gain_three, gain_four]), jnp.zeros_like(norm_gains)]
        ),
        jnp.concatenate(
            [grad_taps, grad_conv_bias[None], grad_biases, grad_decay_param[None]], axis=0
        ),
        layer_own,
        high,
        cid["last"],
    )
    rms_local = functools.partial(rms_norm, gain=norm_gains[0])
    stream_grad = jax.vjp(rms_local, stream_in)[1](grad_normed)[0]
    input_own = lowered(grad_stream + stream_grad)
    done_one = exchanged(done_one)
    (input_grad,) = gather([input_own], [False], cid["gather_half"])
    gains_sum = gains_sum[: norm_gains.shape[0]]
    input_grad, done_one, last = lax.optimization_barrier((input_grad, done_one, last))
    input_grad = input_grad.astype(jnp.float32)
    last = exchanged(last)
    keyvalue_grad = jnp.sum(last[:, weight_rows + gate_rows :].astype(jnp.float32), axis=0)
    last_rows, last_gates = (last[:, :weight_rows], last[:, weight_rows : weight_rows + gate_rows])
    return (
        layer_out,
        input_grad,
        gains_sum,
        joined(last_rows[:, :, :channels]),
        joined(last_rows[:, :, channels : 2 * channels]),
        small[:CONV],
        small[CONV],
        joined(last_gates[:, :, :channels]).T,
        joined(last_gates[:, :, channels : 2 * channels]).T,
        small[CONV + 1 : CONV + 3],
        small[CONV + 3],
        joined(last_rows[:, :, 2 * channels :]).T,
        *dense_grads(done_one),
        done_attn[:, :query_width],
        keyvalue_grad.reshape(keyvalue_weight.shape),
        done_attn[:, query_width:].T,
        *done_two,
    )


def solution(mesh):
    placed = (
        P("seq", None),
        P("seq", None),
        P(),
        P(),
        P("seq", "tp"),
        P("seq", "tp"),
        P(None, "tp"),
        P("tp"),
        P("tp", "seq"),
        P("tp", "seq"),
        P(None, "tp"),
        P("tp"),
        P("tp", "seq"),
        P("seq", "tp"),
        P("seq", "tp"),
        P("tp", "seq"),
        P("seq", "tp"),
        P(("seq", "tp"), None),
        P("tp", "seq"),
        P("seq", "tp"),
        P("seq", "tp"),
        P("tp", "seq"),
    )
    return jax.shard_map(
        local,
        mesh=mesh,
        in_specs=placed,
        out_specs=(
            P("seq", None),
            P("seq", None),
            P(),
            P("seq", "tp"),
            P("seq", "tp"),
            P(None, "tp"),
            P("tp"),
            P("tp", "seq"),
            P("tp", "seq"),
            P(None, "tp"),
            P("tp"),
            P("tp", "seq"),
            P("seq", "tp"),
            P("seq", "tp"),
            P("tp", "seq"),
            P("seq", "tp"),
            P(("seq", "tp"), None),
            P("tp", "seq"),
            P("seq", "tp"),
            P("seq", "tp"),
            P("tp", "seq"),
        ),
        check_vma=False,
    )
```

```python
import functools
import math

import jax
import jax.numpy as jnp
from jax import lax
from jax.experimental import pallas as pl
from jax.experimental.pallas import tpu as pltpu
from jax.sharding import PartitionSpec as P

HD = 128
CONV = 4
WINDOW = 1024


def product(left, right):
    return jnp.dot(left, right, preferred_element_type=jnp.float32)


def product_left(left, right):
    return lax.dot_general(
        left, right, (((0,), (0,)), ((), ())), preferred_element_type=jnp.float32
    )


def product_right(left, right):
    return lax.dot_general(
        left, right, (((1,), (1,)), ((), ())), preferred_element_type=jnp.float32
    )


def lowered(values):
    return values.astype(jnp.bfloat16)


def rms_norm(values, gain):
    return values * lax.rsqrt(jnp.mean(values * values, axis=-1, keepdims=True) + 1e-06) * gain


def gated(gate_values, up_values):
    return jax.nn.gelu(gate_values) * up_values


def layout(doc_lengths, first_slot, count):
    ends = jnp.cumsum(doc_lengths, dtype=jnp.int32)
    slots = first_slot + jnp.arange(count, dtype=jnp.int32)
    passed = slots[:, None] >= ends[None, :]
    segment = jnp.sum(passed.astype(jnp.int32), axis=1)
    begin = jnp.max(jnp.where(passed, ends[None, :], 0), axis=1)
    segment = jnp.where(slots < 0, -1, segment)
    position = slots - begin
    reset = (slots != begin).astype(jnp.float32)
    valid = (segment < doc_lengths.shape[0]).astype(jnp.float32)
    return (segment, position, reset, valid)


def convolve(extended, taps, bias, segment):
    leading = CONV - 1
    total_rows = extended.shape[0] - leading
    result = bias[None, :] + taps[0][None, :] * extended[leading:]
    for lag_index in range(1, CONV):
        same = (
            segment[leading:] == segment[leading - lag_index : leading - lag_index + total_rows]
        ).astype(jnp.float32)
        result = (
            result
            + same[:, None]
            * taps[lag_index][None, :]
            * extended[leading - lag_index : leading - lag_index + total_rows]
        )
    return result


def coefficients(recur_raw, input_raw, conv_values, bias_pair, decay_values, reset):
    recur_rate = jax.nn.sigmoid(recur_raw + bias_pair[0][None, :])
    input_rate = jax.nn.sigmoid(input_raw + bias_pair[1][None, :])
    log_decay = -8.0 * recur_rate * jax.nn.softplus(-decay_values)[None, :]
    multiplier = jnp.sqrt(jnp.maximum(-jnp.expm1(2.0 * log_decay), 0.01))
    return (jnp.exp(log_decay) * reset[:, None], multiplier * input_rate * conv_values)


def combine_state(earlier, later):
    return (earlier[0] * later[0], later[0] * earlier[1] + later[1])


MESH = pl.DeviceIdType.MESH
LO = 2
EIGHTEEN_US = pl.CostEstimate(flops=0, bytes_accessed=60_000_000, transcendentals=0)
TEN_US = pl.CostEstimate(flops=0, bytes_accessed=33_000_000, transcendentals=0)
ANY = pl.BlockSpec(memory_space=pl.ANY)
VMEM = pl.BlockSpec(memory_space=pltpu.VMEM)


def cube():
    seq = lax.axis_index("seq")
    tp = lax.axis_index("tp")
    a = lax.rem(seq, LO)
    b = tp // 2
    c = lax.rem(tp, 2)
    across_a = (seq - a + 1 - a, tp)
    across_b = (seq, (1 - b) * 2 + c)
    across_c = (seq, b * 2 + 1 - c)
    return (a, b, c, across_a, across_b, across_c)


def hail(devices):
    for device in devices:
        pl.semaphore_signal(
            pltpu.get_barrier_semaphore(), inc=1, device_id=device, device_id_type=MESH
        )


def greet(devices):
    hail(devices)
    pl.semaphore_wait(pltpu.get_barrier_semaphore(), len(devices))


def remote(src, dst, send_sem, recv_sem, slot, device):
    return pltpu.make_async_remote_copy(
        src_ref=src,
        dst_ref=dst,
        send_sem=send_sem.at[slot],
        recv_sem=recv_sem.at[slot],
        device_id=device,
        device_id_type=MESH,
    )


def in_turn(*runs):
    runs = list(runs)
    while runs:
        for run in list(runs):
            if next(run, "end") == "end":
                runs.remove(run)


def neighbours(full):
    across_a, across_b, across_c = cube()[3:]
    return [across_c, across_b] + ([across_a] if full else [])


def gather_steps(full, in_ref, out_ref, send_sem, recv_sem, local_sem):
    a, b, c, across_a, across_b, across_c = cube()
    half = in_ref.shape[0] // 2

    def index(pa, pb, pc):
        return pa * 4 + pb * 2 + pc if full else pb * 2 + pc

    me, an, bn, dn = (
        index(a, b, c),
        index(1 - a, b, c),
        index(a, 1 - b, c),
        index(1 - a, 1 - b, c),
    )
    low, high = (pl.ds(0, half), pl.ds(half, half))
    sent = {}

    def go(slot, src, dst, device):
        copy = remote(src, dst, send_sem, recv_sem, slot, device)
        copy.start()
        sent[slot] = copy

    def own(slot, part, device):
        go(slot, in_ref.at[part], out_ref.at[me, part], device)

    def onward(slot, block, part, device):
        go(slot, out_ref.at[block, part], out_ref.at[block, part], device)

    if full:
        own(0, low, across_a)
    own(1, high, across_b)
    if full:
        own(2, high, across_a)
    own(3, low, across_b)
    go(4, in_ref, out_ref.at[me], across_c)
    mine = pltpu.make_async_copy(in_ref, out_ref.at[me], local_sem)
    mine.start()
    yield
    if full:
        sent[0].wait_recv()
        onward(5, an, low, across_b)
        onward(6, an, low, across_c)
        yield
    sent[1].wait_recv()
    if full:
        onward(7, bn, high, across_a)
    onward(8, bn, high, across_c)
    yield
    if full:
        sent[2].wait_recv()
        onward(9, an, high, across_c)
        yield
    sent[3].wait_recv()
    onward(10, bn, low, across_c)
    yield
    if full:
        sent[5].wait_recv()
        onward(11, dn, low, across_c)
        yield
        sent[7].wait_recv()
        onward(12, dn, high, across_c)
        yield
    for slot in (4, 6, 8, 9, 10, 11, 12):
        if slot in sent:
            sent[slot].wait_recv()
    for copy in sent.values():
        copy.wait_send()
    mine.wait()


def gather_kernel(spans, *refs):
    count = len(spans)
    in_refs, out_refs = (refs[:count], refs[count : 2 * count])
    send_sem, recv_sem, local_sem = refs[2 * count :]
    greet(neighbours(any(spans)))
    in_turn(
        *[
            gather_steps(
                spans[k], in_refs[k], out_refs[k], send_sem.at[k], recv_sem.at[k], local_sem.at[k]
            )
            for k in range(count)
        ]
    )


def gather(blocks, spans, collective_id):
    count = len(blocks)
    ways = [8 if span else 4 for span in spans]
    results = pl.pallas_call(
        functools.partial(gather_kernel, spans),
        out_shape=[
            jax.ShapeDtypeStruct((n, *block.shape), block.dtype) for n, block in zip(ways, blocks)
        ],
        in_specs=[ANY] * count,
        out_specs=[ANY] * count,
        scratch_shapes=[
            pltpu.SemaphoreType.DMA((count, 13)),
            pltpu.SemaphoreType.DMA((count, 13)),
            pltpu.SemaphoreType.DMA((count,)),
        ],
        name="gather_full" if any(spans) else "gather_half",
        cost_estimate=EIGHTEEN_US,
        compiler_params=pltpu.CompilerParams(collective_id=collective_id, has_side_effects=True),
    )(*blocks)
    return [
        result.reshape(n * block.shape[0], block.shape[1])
        for n, result, block in zip(ways, results, blocks)
    ]


def scatter_steps(
    full, part_ref, out_ref, cbuf, sx, sy, tx, ty, ax, by, rx, ry, csend, crecv, send_sem, recv_sem
):
    a, b, c, across_a, across_b, across_c = cube()
    half = part_ref.shape[1] // 2

    def index(pa, pb, pc):
        return pa * 4 + pb * 2 + pc if full else pb * 2 + pc

    def pair(pa, pb):
        return pa * 2 + pb if full else pb

    low, high = (pl.ds(0, half), pl.ds(half, half))
    if full:
        order = [
            (1 - a, 1 - b, low),
            (1 - a, 1 - b, high),
            (1 - a, b, low),
            (a, 1 - b, high),
            (a, 1 - b, low),
            (1 - a, b, high),
            (a, b, low),
            (a, b, high),
        ]
    else:
        order = [(a, 1 - b, low), (a, 1 - b, high), (a, b, low), (a, b, high)]
    core = {}

    def share(*which):
        for k in which:
            pa, pb, part = order[k]
            core[k] = remote(
                part_ref.at[index(pa, pb, 1 - c), part],
                cbuf.at[pair(pa, pb), part],
                csend,
                crecv,
                k,
                across_c,
            )
            core[k].start()

    def summed(k):
        pa, pb, part = order[k]
        core[k].wait_recv()
        return part_ref[index(pa, pb, c), part].astype(jnp.float32) + cbuf[
            pair(pa, pb), part
        ].astype(jnp.float32)

    sent = []

    def go(src, dst, slot, device):
        copy = remote(src, dst, send_sem, recv_sem, slot, device)
        copy.start()
        sent.append(copy)
        return copy

    if full:
        yield
        share(0, 1)
        yield
        share(2, 5)
        sx[0] = lowered(summed(0))
        x0 = go(sx.at[0], ax.at[0], 0, across_a)
        sy[0] = lowered(summed(1))
        y0 = go(sy.at[0], by.at[0], 1, across_b)
        yield
        share(3, 4)
        sx[1] = lowered(summed(2))
        x1 = go(sx.at[1], ax.at[1], 2, across_a)
        sy[1] = lowered(summed(3))
        y1 = go(sy.at[1], by.at[1], 3, across_b)
        yield
        share(6, 7)
        yield
        total = summed(4)
        x0.wait_recv()
        ty[...] = lowered(total + ax[0].astype(jnp.float32))
        last_y = go(ty, ry, 4, across_b)
        total = summed(5)
        y0.wait_recv()
        tx[...] = lowered(total + by[0].astype(jnp.float32))
        last_x = go(tx, rx, 5, across_a)
        yield
        total = summed(6)
        x1.wait_recv()
        total = total + ax[1].astype(jnp.float32)
        last_y.wait_recv()
        out_ref[low] = total + ry[...].astype(jnp.float32)
        total = summed(7)
        y1.wait_recv()
        total = total + by[1].astype(jnp.float32)
        last_x.wait_recv()
        out_ref[high] = total + rx[...].astype(jnp.float32)
    else:
        share(0, 1, 2, 3)
        sy[0] = lowered(summed(0))
        y0 = go(sy.at[0], by.at[0], 1, across_b)
        sy[1] = lowered(summed(1))
        y1 = go(sy.at[1], by.at[1], 3, across_b)
        yield
        total = summed(2)
        y0.wait_recv()
        out_ref[low] = total + by[0].astype(jnp.float32)
        total = summed(3)
        y1.wait_recv()
        out_ref[high] = total + by[1].astype(jnp.float32)
    for copy in [*core.values(), *sent]:
        copy.wait_send()


def scatter_kernel(full, count, *refs):
    greet(neighbours(full))
    in_turn(
        *[
            scatter_steps(full, refs[k], refs[count + k], *refs[2 * count + 13 * k :][:13])
            for k in range(count)
        ]
    )


def scatter_scratch(ways, rows, width):
    half = rows // 2
    shapes = [(ways // 2, rows, width)] + [(2, half, width)] * 2 + [(half, width)] * 2
    shapes += [(2, half, width)] * 2 + [(half, width)] * 2
    return [pltpu.VMEM(shape, jnp.bfloat16) for shape in shapes] + [
        pltpu.SemaphoreType.DMA((k,)) for k in (8, 8, 6, 6)
    ]


def scatter(partials, full, collective_id):
    ways = 8 if full else 4
    count = len(partials)
    rows = partials[0].shape[0] // ways
    scratch = []
    for partial in partials:
        scratch += scatter_scratch(ways, rows, partial.shape[1])
    return pl.pallas_call(
        functools.partial(scatter_kernel, full, count),
        out_shape=[
            jax.ShapeDtypeStruct((rows, partial.shape[1]), jnp.float32) for partial in partials
        ],
        in_specs=[VMEM] * count,
        out_specs=[VMEM] * count,
        scratch_shapes=scratch,
        name="scatter_full" if full else "scatter_half",
        cost_estimate=EIGHTEEN_US,
        compiler_params=pltpu.CompilerParams(
            collective_id=collective_id, has_side_effects=True, vmem_limit_bytes=48 * 2**20
        ),
    )(*[lowered(partial).reshape(ways, rows, -1) for partial in partials])


def scan_kernel(
    high, reverse, decay_ref, drive_ref, end_ref, state_ref, carry_ref, cum, strips, sendbuf, recvbuf, send_sem, recv_sem
):
    rows, width = decay_ref.shape
    strands = 8
    steps = rows // strands
    lanes = 128
    blocks = width // lanes
    mine = lax.axis_index("seq") // LO
    peers = high_peers(high)
    greet(peers)
    for n in range(blocks):
        cum[n] = decay_ref[:, n * lanes : (n + 1) * lanes]
        strips[n] = drive_ref[:, n * lanes : (n + 1) * lanes]

    def step(i, carry):
        r = steps - 1 - i if reverse else i
        at = pl.ds(r, strands, stride=steps)
        new = []
        for n in range(blocks):
            a = cum[n, at, :]
            product_now = carry[2 * n] * a
            state_now = carry[2 * n + 1] * a + strips[n, at, :]
            cum[n, at, :] = product_now
            strips[n, at, :] = state_now
            new += [product_now, state_now]
        return tuple(new)

    ones = jnp.ones((strands, lanes), jnp.float32)
    ends = lax.fori_loop(0, steps, step, (ones, jnp.zeros_like(ones)) * blocks, unroll=8)
    strand_order = list(range(strands - 1, -1, -1)) if reverse else list(range(strands))
    before = {}
    for n in range(blocks):
        total_a = jnp.ones((1, lanes), jnp.float32)
        total_h = jnp.zeros((1, lanes), jnp.float32)
        for k in strand_order:
            before[n, k] = (total_a, total_h)
            a, h = (ends[2 * n][k : k + 1], ends[2 * n + 1][k : k + 1])
            total_h = a * total_h + h
            total_a = a * total_a
        scale = end_ref[0:1, n * lanes : (n + 1) * lanes]
        sendbuf[n, 0:1, :] = total_a * scale
        sendbuf[n, 1:2, :] = total_h * scale
        sendbuf[n, 2:8, :] = jnp.zeros((6, lanes), jnp.float32)
    copies = []
    for k, peer in enumerate(peers):
        copy = remote(sendbuf, recvbuf.at[k], send_sem, recv_sem, k, peer)
        copy.start()
        copies.append(copy)
    for copy in copies:
        copy.wait_recv()
    for n in range(blocks):
        carry = jnp.zeros((1, lanes), jnp.float32)
        for turn in range(high - 1):
            plane = high - 1 - turn if reverse else turn
            away = lax.rem(mine - plane + high, high)
            reached = plane > mine if reverse else plane < mine
            got = recvbuf[jnp.where(reached, away - 1, 0), n]
            carry = jnp.where(reached, got[0:1] * carry + got[1:2], carry)
        span = pl.ds(n * lanes, lanes)
        carry_ref[:, span] = jnp.broadcast_to(carry, (carry_ref.shape[0], lanes))
        for k in range(strands):
            enter = before[n, k][0] * carry + before[n, k][1]
            at = pl.ds(k * steps, steps)
            state_ref[at, span] = strips[n, at, :] + cum[n, at, :] * enter
    for copy in copies:
        copy.wait_send()


def plane_scan(decay, drive, end_scale, high, reverse, collective_id):
    rows, width = decay.shape
    return pl.pallas_call(
        functools.partial(scan_kernel, high, reverse),
        out_shape=(
            jax.ShapeDtypeStruct((rows, width), jnp.float32),
            jax.ShapeDtypeStruct((8, width), jnp.float32),
        ),
        in_specs=[VMEM] * 3,
        out_specs=(VMEM, VMEM),
        scratch_shapes=[
            pltpu.VMEM((width // 128, rows, 128), jnp.float32),
            pltpu.VMEM((width // 128, rows, 128), jnp.float32),
            pltpu.VMEM((width // 128, 8, 128), jnp.float32),
            pltpu.VMEM((high - 1, width // 128, 8, 128), jnp.float32),
            pltpu.SemaphoreType.DMA((high - 1,)),
            pltpu.SemaphoreType.DMA((high - 1,)),
        ],
        name="scan_back" if reverse else "scan",
        cost_estimate=TEN_US,
        compiler_params=pltpu.CompilerParams(
            collective_id=collective_id, has_side_effects=True, vmem_limit_bytes=32 * 2**20
        ),
    )(decay, drive, end_scale)


def small_steps(high, gains_ref, rest_ref, gains_out, rest_out, gbuf, rbuf, ghold, rhold, gpair, rpair, send_sem, recv_sem):
    a, b, c, across_a, across_b, across_c = cube()
    peers = high_peers(high)
    copies = []
    for k, peer in enumerate(peers):
        for n, (src, dst) in enumerate(((gains_ref, gbuf.at[k]), (rest_ref, rbuf.at[k]))):
            copy = remote(src, dst, send_sem, recv_sem, 2 * k + n, peer)
            copy.start()
            copies.append(copy)
    yield
    for copy in copies:
        copy.wait_recv()
    gains = gains_ref[...]
    rest = rest_ref[...]
    for k in range(high - 1):
        gains = gains + gbuf[k]
        rest = rest + rbuf[k]
    rhold[...] = rest
    slot = 2 * (high - 1)
    swap = remote(rhold, rpair, send_sem, recv_sem, slot, across_a)
    swap.start()
    copies.append(swap)
    for n, device in enumerate((across_a, across_b, across_c)):
        ghold[n] = gains
        copy = remote(ghold.at[n], gpair.at[n], send_sem, recv_sem, slot + 1 + n, device)
        copy.start()
        copies.append(copy)
        yield
        copy.wait_recv()
        gains = gains + gpair[n]
    swap.wait_recv()
    gains_out[...] = gains
    other = rpair[...]
    width = rest.shape[1]
    rest_out[:, :width] = jnp.where(a == 0, rest, other)
    rest_out[:, width:] = jnp.where(a == 0, other, rest)
    for copy in copies:
        copy.wait_send()


def high_peers(high):
    seq = lax.axis_index("seq")
    tp = lax.axis_index("tp")
    return [(lax.rem(seq // LO + k, high) * LO + lax.rem(seq, LO), tp) for k in range(1, high)]


def last_kernel(high, part_ref, gains_ref, rest_ref, in_ref, out_ref, gains_out, rest_out, all_ref, *more):
    greet(high_peers(high) + neighbours(True))
    in_turn(
        small_steps(high, gains_ref, rest_ref, gains_out, rest_out, *more[13:21]),
        scatter_steps(True, part_ref, out_ref, *more[:13]),
        gather_steps(False, in_ref, all_ref, *more[21:]),
    )


def scatter_and_sums(partial, gains, rest, block, high, collective_id):
    slots = 2 * (high - 1) + 4
    ways = 8
    width = partial.shape[1]
    rows = partial.shape[0] // ways
    *sums, gathered = pl.pallas_call(
        functools.partial(last_kernel, high),
        out_shape=[
            jax.ShapeDtypeStruct((rows, width), jnp.float32),
            jax.ShapeDtypeStruct(gains.shape, jnp.float32),
            jax.ShapeDtypeStruct((rest.shape[0], LO * rest.shape[1]), jnp.float32),
            jax.ShapeDtypeStruct((4, *block.shape), block.dtype),
        ],
        in_specs=[VMEM] * 3 + [ANY],
        out_specs=[VMEM] * 3 + [ANY],
        scratch_shapes=scatter_scratch(ways, rows, width)
        + [
            pltpu.VMEM((high - 1, *gains.shape), jnp.float32),
            pltpu.VMEM((high - 1, *rest.shape), jnp.float32),
            pltpu.VMEM((3, *gains.shape), jnp.float32),
            pltpu.VMEM(rest.shape, jnp.float32),
            pltpu.VMEM((3, *gains.shape), jnp.float32),
            pltpu.VMEM(rest.shape, jnp.float32),
            pltpu.SemaphoreType.DMA((slots,)),
            pltpu.SemaphoreType.DMA((slots,)),
            pltpu.SemaphoreType.DMA((13,)),
            pltpu.SemaphoreType.DMA((13,)),
            pltpu.SemaphoreType.DMA,
        ],
        name="scatter_and_sums",
        cost_estimate=EIGHTEEN_US,
        compiler_params=pltpu.CompilerParams(
            collective_id=collective_id, has_side_effects=True, vmem_limit_bytes=40 * 2**20
        ),
    )(lowered(partial).reshape(ways, rows, width), gains, rest, block)
    return (*sums, gathered.reshape(-1, block.shape[1]))


def gelu_parts(x):
    inner = math.sqrt(2 / math.pi)
    curve = jnp.tanh(inner * (x + 0.044715 * x * x * x))
    half = 0.5 * (1 + curve)
    slope = half + 0.5 * x * (1 - curve * curve) * inner * (1 + 3 * 0.044715 * x * x)
    return (x * half, slope)


def dense_kernel(mode, main, *refs):
    refs = list(refs)

    def take(wanted=True):
        return refs.pop(0) if wanted else None

    grads = mode in ("both", "backward")
    fresh = mode in ("both", "forward")
    n_hbm = take(mode != "product")
    g_hbm = take(grads)
    w_hbm = take()
    ab_hbm = take(mode == "backward")
    hid_in = take(mode == "product")
    out_ref = take()
    wire_hbm = take(grads)
    ab_out = take(mode == "forward")
    hid_out = take(mode == "both")
    w_v, hid_v, part_v = (take(), take(), take())
    n_v = take(mode != "product")
    g_v, low_v, wire_v = (take(grads), take(grads), take(grads))
    ab_v = take(mode in ("forward", "backward"))
    buffers = [take() for _ in range(13)]
    sems = take()
    lanes = 128
    both = 2 * main + lanes
    tile = 256
    a, b = cube()[:2]
    near = neighbours(True)
    hail(near)
    up_part, down_part = (pl.ds(0, both), pl.ds(both, w_v.shape[1] - both))
    loads = {}

    def load(name, src, dst):
        loads[name] = pltpu.make_async_copy(src, dst, sems.at[len(loads)])
        loads[name].start()

    def need(*names):
        for name in names:
            if name in loads:
                loads.pop(name).wait()

    tiles = ((1 - a, 1 - b), (1 - a, b), (a, 1 - b), (a, b))

    def rows_of(pa, pb):
        return pl.ds(pl.multiple_of((pa * 4 + pb * 2) * lanes, tile), tile)

    def load_rows(turn, **pairs):
        at = rows_of(*tiles[turn])
        for name, (src, dst) in pairs.items():
            if src is not None:
                load(f"{name}{turn}", src.at[at], dst.at[at])

    for turn in range(4):
        load_rows(turn, n=(n_hbm, n_v), hid=(hid_in, hid_v), ab=(ab_hbm, ab_v))
        if turn == 0 and mode != "product":
            load("up", w_hbm.at[:, up_part], w_v.at[:, up_part])
        load_rows(turn, g=(g_hbm, g_v))
        if turn == 0:
            load("down", w_hbm.at[:, down_part], w_v.at[:, down_part])

    def work(turn):
        pa, pb = tiles[turn]
        block = pa * 4 + pb * 2
        at = rows_of(pa, pb)
        if mode == "product":
            need(f"hid{turn}", "down")
            part = lowered(product_right(hid_v[at, :], w_v[:, both:]))
            part_v[pl.ds(block, 2)] = part.reshape(2, lanes, part.shape[1])
            return
        need(f"n{turn}")
        if fresh:
            need("up")
            ab = product(n_v[at, :], w_v[:, :both])
            if mode == "forward":
                ab_v[at, :] = ab
        else:
            need(f"ab{turn}")
            ab = ab_v[at, :]
        gate, up, tail = (ab[:, :main], ab[:, main : 2 * main], ab[:, 2 * main :])
        first = lax.broadcasted_iota(jnp.int32, tail.shape, 1) < lanes // 2
        turned = pltpu.roll(tail, lanes // 2, 1)
        act, slope = gelu_parts(gate)
        tail_act, tail_slope = gelu_parts(tail)
        hid_v[at, :main] = lowered(act * up)
        hid_v[at, main:] = lowered(jnp.where(first, tail_act * turned, 0.0))
        need(f"g{turn}", "down")
        if grads:
            grad = product(g_v[at, :], w_v[:, both:])
            grad_main, grad_tail = (grad[:, :main], grad[:, main:])
            low_v[at, :main] = lowered(grad_main * up * slope)
            low_v[at, main : 2 * main] = lowered(grad_main * act)
            turned_grad = pltpu.roll(grad_tail, lanes // 2, 1)
            turned_act = pltpu.roll(tail_act, lanes // 2, 1)
            low_v[at, 2 * main :] = lowered(
                jnp.where(first, grad_tail * turned * tail_slope, turned_grad * turned_act)
            )
            need("up")
            part = lowered(product_right(low_v[at, :], w_v[:, :both]))
        else:
            part = lowered(product_right(hid_v[at, :], w_v[:, both:]))
        part_v[pl.ds(block, 2)] = part.reshape(2, lanes, part.shape[1])

    schedule = scatter_steps(True, part_v, out_ref, *buffers)
    next(schedule)
    for turn in range(4):
        work(turn)
        if turn == 0:
            pl.semaphore_wait(pltpu.get_barrier_semaphore(), len(near))
        next(schedule)
    next(schedule)
    stores = []

    def store(src, dst, slot):
        copy = pltpu.make_async_copy(src, dst, sems.at[slot])
        copy.start()
        stores.append(copy)

    if mode == "both":
        store(hid_v, hid_out, 16)
    if mode == "forward":
        store(ab_v, ab_out, 16)
    if grads:
        half = w_v.shape[0] // 2
        for part in range(2):
            cols = pl.ds(part * half, half)
            wire_v[cols, :both] = lowered(product_left(n_v[:, cols], low_v[...]))
            wire_v[cols, both:] = lowered(product_left(g_v[:, cols], hid_v[...]))
            store(wire_v.at[cols], wire_hbm.at[cols], 17 + part)
    next(schedule, None)
    for copy in stores:
        copy.wait()


def dense_call(mode, rows_in, grad_low, weights, ab, collective_id):
    rows = rows_in.shape[0]
    depth, columns = weights.shape
    main = (columns // 128 - 2) // 3 * 128
    both = 2 * main + 128
    grads = mode in ("both", "backward")
    low = jnp.bfloat16
    wide = ((rows, depth), low)
    hidden = ((rows, columns - both), low)
    if mode == "product":
        operands = [weights, rows_in]
    else:
        operands = [rows_in] + ([grad_low] if grads else []) + [weights]
    if mode == "backward":
        operands.append(ab)
    extra = {
        "forward": [((rows, both), jnp.float32)],
        "backward": [(weights.shape, low)],
        "both": [(weights.shape, low), hidden],
        "product": [],
    }[mode]
    scratch = [(weights.shape, low), hidden, ((8, rows // 8, depth), low)]
    if mode != "product":
        scratch.append(wide)
    if grads:
        scratch += [wide, ((rows, both), low), (weights.shape, low)]
    if mode in ("forward", "backward"):
        scratch.append(((rows, both), jnp.float32))
    return pl.pallas_call(
        functools.partial(dense_kernel, mode, main),
        out_shape=[
            jax.ShapeDtypeStruct(shape, kind)
            for shape, kind in [((rows // 8, depth), jnp.float32)] + extra
        ],
        in_specs=[ANY] * len(operands),
        out_specs=[VMEM] + [ANY] * len(extra),
        scratch_shapes=[pltpu.VMEM(shape, kind) for shape, kind in scratch]
        + scatter_scratch(8, rows // 8, depth)
        + [pltpu.SemaphoreType.DMA((19,))],
        name="dense_" + mode,
        cost_estimate=pl.CostEstimate(
            flops=0, bytes_accessed=100_000_000 if grads else 75_000_000, transcendentals=0
        ),
        compiler_params=pltpu.CompilerParams(
            collective_id=collective_id, has_side_effects=True, vmem_limit_bytes=56 * 2**20
        ),
    )(*operands)


def attention_kernel(
    shift, query_ref, ext_ref, here_ref, there_ref, cos_ref, sin_ref, out_ref, rot_ref, log_ref
):
    tile = 256
    rows, width = query_ref.shape
    heads = width // HD
    reach = shift + tile
    scale = HD ** (-0.5)
    log_ref[...] = jnp.zeros_like(log_ref)

    def turn(n, carry):
        h = n // (rows // tile)
        first = pl.multiple_of(lax.rem(n, rows // tile) * tile, tile)
        lanes = pl.ds(pl.multiple_of(h * HD, HD), HD)
        at = pl.ds(first, tile)
        seen = pl.ds(first, reach)
        query = query_ref[at, lanes]
        query = query * cos_ref[at, :] + pltpu.roll(query, HD // 2, 1) * sin_ref[at, :]
        query = lowered(query)
        rot_ref[at, lanes] = query
        allowed = visible(shift, there_ref[seen, :], here_ref[0:1, at])
        scores = jnp.where(allowed, product_right(ext_ref[seen, :HD], query) * scale, -1e30)
        top = jnp.max(scores, axis=0, keepdims=True)
        probs = jnp.exp(scores - top)
        total = jnp.sum(probs, axis=0, keepdims=True)
        log_ref[pl.ds(h, 1), at] = top + jnp.log(total)
        out_ref[at, lanes] = lowered(product_left(lowered(probs / total), ext_ref[seen, HD:]))
        return carry

    lax.fori_loop(0, heads * (rows // tile), turn, 0)


def visible(shift, there, here):
    shape = (there.shape[0], here.shape[1])
    distance = (
        lax.broadcasted_iota(jnp.int32, shape, 1) - lax.broadcasted_iota(jnp.int32, shape, 0) + shift
    )
    return (there == here) & (distance >= 0) & (distance < WINDOW)


def attention(query, extended, here, there, cosine, sine):
    rows, width = query.shape
    return pl.pallas_call(
        functools.partial(attention_kernel, extended.shape[0] - rows),
        out_shape=[
            jax.ShapeDtypeStruct((rows, width), jnp.bfloat16),
            jax.ShapeDtypeStruct((rows, width), jnp.bfloat16),
            jax.ShapeDtypeStruct((8, rows), jnp.float32),
        ],
        in_specs=[VMEM] * 6,
        out_specs=[VMEM] * 3,
        name="attention",
        cost_estimate=TEN_US,
        compiler_params=pltpu.CompilerParams(vmem_limit_bytes=48 * 2**20),
    )(query, extended, here, there, cosine, sine)


def attention_back_kernel(
    shift, query_ref, ext_ref, grad_ref, log_ref, here_ref, there_ref, cos_ref, sin_ref, dquery_ref, dext_ref, total
):
    tile = 256
    rows, width = query_ref.shape
    heads = width // HD
    reach = shift + tile
    scale = HD ** (-0.5)
    total[...] = jnp.zeros_like(total)

    def turn(n, carry):
        h = n // (rows // tile)
        first = pl.multiple_of(lax.rem(n, rows // tile) * tile, tile)
        lanes = pl.ds(pl.multiple_of(h * HD, HD), HD)
        at = pl.ds(first, tile)
        seen = pl.ds(first, reach)
        query = query_ref[at, lanes]
        grad = grad_ref[at, lanes]
        keys = ext_ref[seen, :HD]
        values = ext_ref[seen, HD:]
        allowed = visible(shift, there_ref[seen, :], here_ref[0:1, at])
        scores = jnp.where(allowed, product_right(keys, query) * scale, -1e30)
        probs = jnp.exp(scores - log_ref[pl.ds(h, 1), at])
        grad_probs = product_right(values, grad)
        mean = jnp.sum(probs * grad_probs, axis=0, keepdims=True)
        grad_scores = lowered(probs * (grad_probs - mean) * scale)
        total[seen, :HD] += product(grad_scores, query)
        total[seen, HD:] += product(lowered(probs), grad)
        turned = product_left(grad_scores, keys)
        turned = turned * cos_ref[at, :] - pltpu.roll(turned, HD // 2, 1) * sin_ref[at, :]
        dquery_ref[at, lanes] = lowered(turned)
        return carry

    lax.fori_loop(0, heads * (rows // tile), turn, 0)
    dext_ref[...] = lowered(total[...])


def attention_back(query_rot, extended, grad, log_total, here, there, cosine, sine):
    rows, width = query_rot.shape
    seen = extended.shape[0]
    return pl.pallas_call(
        functools.partial(attention_back_kernel, seen - rows),
        out_shape=[
            jax.ShapeDtypeStruct((rows, width), jnp.bfloat16),
            jax.ShapeDtypeStruct((seen, 2 * HD), jnp.bfloat16),
        ],
        in_specs=[VMEM] * 8,
        out_specs=[VMEM] * 2,
        scratch_shapes=[pltpu.VMEM((seen, 2 * HD), jnp.float32)],
        name="attention_back",
        cost_estimate=EIGHTEEN_US,
        compiler_params=pltpu.CompilerParams(vmem_limit_bytes=48 * 2**20),
    )(query_rot, extended, grad, log_total, here, there, cosine, sine)


def stacked_by_low(mine, other):
    lo = lax.rem(lax.axis_index("seq"), LO)
    return jnp.stack([jnp.where(lo == 0, mine, other), jnp.where(lo == 0, other, mine)])


def swap_low(block):
    count = lax.axis_size("seq")
    return lax.ppermute(block, "seq", [(s, s // LO * LO + (1 - s % LO)) for s in range(count)])


def high_groups():
    count = lax.axis_size("seq")
    return [[h * LO + l for h in range(count // LO)] for l in range(LO)]


def swap_columns(*parts):
    return swap_pieces([jnp.concatenate(each, axis=1) for each in zip(*map(split_columns, parts))])


def swap_pieces(halves):
    lo = lax.rem(lax.axis_index("seq"), LO)
    kept = jnp.where(lo == 0, halves[0], halves[1])
    given = jnp.where(lo == 0, halves[1], halves[0])
    both = stacked_by_low(kept, swap_low(given))
    return both.reshape(-1, both.shape[2])


def gather_high(rows):
    return lax.all_gather(rows, "seq", axis=0, tiled=True, axis_index_groups=high_groups())


def reduce_high(grad):
    return lax.psum_scatter(
        lowered(grad), "seq", scatter_dimension=0, tiled=True, axis_index_groups=high_groups()
    )


def exchanged(both):
    lo = lax.rem(lax.axis_index("seq"), LO)
    both = both.reshape(LO, -1, both.shape[1])
    kept = jnp.where(lo == 0, both[0], both[1])
    given = jnp.where(lo == 0, both[1], both[0])
    return stacked_by_low(kept, swap_low(given))


def split_columns(block):
    width = block.shape[1] // LO
    return [block[:, l * width : (l + 1) * width] for l in range(LO)]


def joined(blocks):
    return jnp.concatenate([blocks[l] for l in range(LO)], axis=1).astype(jnp.float32)


def block_product(values, weight):
    block_width = weight.shape[0]
    blocks = weight.shape[1] // block_width
    return jnp.concatenate(
        [
            product_right(
                values[:, n * block_width : (n + 1) * block_width],
                weight[:, n * block_width : (n + 1) * block_width],
            )
            for n in range(blocks)
        ],
        axis=1,
    )


def block_grads(values, weight, upstream):
    block_width = weight.shape[0]
    cuts = [slice(n * block_width, (n + 1) * block_width) for n in range(weight.shape[1] // block_width)]
    return (
        jnp.concatenate([product_left(upstream[:, s], values[:, s]) for s in cuts], axis=1),
        jnp.concatenate([product(upstream[:, s], weight[:, s]) for s in cuts], axis=1),
    )


def shifted(block, distance):
    count = lax.axis_size("seq")
    route = [(i - distance, i) for i in range(count) if 0 <= i - distance < count]
    return lax.ppermute(block, "seq", route)


CIDS = {
    "gather_full": 0,
    "gather_half": 1,
    "scatter_full": 2,
    "scatter_half": 3,
    "scan": 4,
    "scan_back": 5,
    "scatter_wide": 6,
    "last": 7,
    "gather_narrow": 8,
    "gather_two": 9,
    "forward": 10,
    "both": 11,
    "backward": 12,
    "gather_weight": 13,
    "gather_seen": 14,
    "product": 15,
}


def dense_wire(gate, up, down):
    pieces = []
    for g, u, d in zip(*map(split_columns, (gate, up, down))):
        main = g.shape[1] // 128 * 128
        blank = jnp.zeros((d.shape[0], -d.shape[1] % 128), d.dtype)
        pieces.append(
            jnp.concatenate([g[:, :main], u[:, :main], g[:, main:], u[:, main:], d, blank], axis=1)
        )
    return pieces


def dense_grads(both):
    columns = both.shape[2]
    main = (columns // 128 - 2) // 3 * 128
    tail = 64
    ends = 2 * main

    def part(first, last):
        return jnp.concatenate([both[:, :, first : first + main], both[:, :, last : last + tail]], axis=2)

    return (
        joined(part(0, ends)),
        joined(part(main, ends + tail)),
        joined(both[:, :, ends + 2 * tail : ends + 3 * tail + main]).T,
    )


def turns(position):
    half_width = HD // 2
    frequency = 10000.0 ** (-jnp.arange(half_width, dtype=jnp.float32) / half_width)
    angle = position.astype(jnp.float32)[:, None] * jnp.tile(frequency, 2)[None, :]
    sign = jnp.where(jnp.arange(HD) < half_width, -1.0, 1.0)
    return (jnp.cos(angle), jnp.sin(angle) * sign[None, :])


def rotate(values, factors):
    cosine, sine = factors
    half_width = HD // 2
    swapped = jnp.concatenate([values[..., half_width:], values[..., :half_width]], axis=-1)
    return values * cosine + swapped * sine


def rotate_back(values, factors):
    cosine, sine = factors
    half_width = HD // 2
    swapped = jnp.concatenate([values[..., half_width:], values[..., :half_width]], axis=-1)
    return values * cosine - swapped * sine


def both_lows(lanes):
    other = swap_low(lanes)
    lo = lax.rem(lax.axis_index("seq"), LO)
    both = jnp.stack([jnp.where(lo == 0, lanes, other), jnp.where(lo == 0, other, lanes)], axis=1)
    return both.reshape(-1, lanes.shape[2])


def swap_sums(grad):
    lo = lax.rem(lax.axis_index("seq"), LO)
    pairs = grad.reshape(lax.axis_size("seq") // LO, LO, -1, grad.shape[1])
    kept = jnp.where(lo == 0, pairs[:, 0], pairs[:, 1])
    given = jnp.where(lo == 0, pairs[:, 1], pairs[:, 0])
    return (kept.reshape(-1, grad.shape[1]), swap_low(given).reshape(-1, grad.shape[1]))


def local(
    tokens,
    cotangent,
    doc_lengths,
    norm_gains,
    input_branch,
    gate_branch,
    conv_taps,
    conv_bias,
    recur_gate,
    input_gate,
    gate_biases,
    decay_param,
    recur_output,
    dense_gate_one,
    dense_up_one,
    dense_down_one,
    query_weight,
    keyvalue_weight,
    attention_out,
    dense_gate_two,
    dense_up_two,
    dense_down_two,
):
    cid = CIDS
    shard_rows = tokens.shape[0]
    seq = lax.axis_index("seq")
    tp = lax.axis_index("tp")
    lo = lax.rem(seq, LO)
    high = lax.axis_size("seq") // LO
    ways = lax.axis_size("tp")
    own_rows = shard_rows // ways
    plane_rows = shard_rows * LO
    channels = conv_bias.shape[0] // LO
    leading = CONV - 1
    halo_shards = WINDOW // shard_rows
    first_slot = seq * shard_rows
    plane_slot = (seq // LO) * plane_rows
    own_slot = first_slot + tp * own_rows
    valid = layout(doc_lengths, own_slot, own_rows)[3]
    segment, position, _, _ = layout(doc_lengths, first_slot, shard_rows)
    plane_reset = layout(doc_lengths, plane_slot, plane_rows)[2]
    conv_segment = layout(doc_lengths, plane_slot - leading, plane_rows + leading)[0]
    key_segment = layout(
        doc_lengths, first_slot - halo_shards * shard_rows, (halo_shards + 1) * shard_rows
    )[0]

    def ours(block, axis):
        return lax.dynamic_slice_in_dim(block, lo * channels, channels, axis)

    taps, bias = (ours(conv_taps, 1), ours(conv_bias, 0))
    bias_pair, decay_values = (ours(gate_biases, 1), ours(decay_param, 0))

    gate_rows = recur_gate.shape[1]
    weight_rows = input_branch.shape[0]
    attn_rows = jnp.concatenate([query_weight, attention_out.T], axis=1)
    query_width = query_weight.shape[1]
    third = jnp.concatenate(
        [attn_rows, keyvalue_weight.reshape(-1, attn_rows.shape[1])], axis=0
    )

    own_tokens = lax.dynamic_slice_in_dim(tokens, tp * own_rows, own_rows, 0)
    own_cotangent = lax.dynamic_slice_in_dim(cotangent, tp * own_rows, own_rows, 0)
    stream_in = own_tokens.astype(jnp.float32)
    grad_stream = own_cotangent.astype(jnp.float32) * valid[:, None]
    first = swap_columns(
        jnp.concatenate([input_branch, recur_gate.T], axis=0),
        jnp.concatenate([gate_branch, input_gate.T], axis=0),
        jnp.concatenate([recur_output.T, jnp.zeros_like(recur_gate.T)], axis=0),
    )
    normed_own = lowered(rms_norm(stream_in, norm_gains[0]))
    grad_own = lowered(grad_stream)
    first, normed_own, grad_own, dense_gate_one = lax.optimization_barrier(
        (first, normed_own, grad_own, dense_gate_one)
    )
    third_rows = third.shape[0]
    early_wires = lax.all_gather(
        jnp.concatenate([third, first], axis=0), "seq", axis_index_groups=high_groups()
    )
    normed_one, grad_low = gather([normed_own, grad_own], [True, True], cid["gather_two"])
    second = swap_pieces(dense_wire(dense_gate_one, dense_up_one, dense_down_one.T))
    second, dense_gate_two = lax.optimization_barrier((second, dense_gate_two))
    fourth = swap_pieces(dense_wire(dense_gate_two, dense_up_two, dense_down_two.T))
    normed_one, early_wires, grad_low, second, fourth = lax.optimization_barrier(
        (normed_one, early_wires, grad_low, second, fourth)
    )
    third = early_wires[:, :third_rows]
    first_full = early_wires[:, third_rows:]
    first_full = first_full.reshape(high * LO, weight_rows + gate_rows, 3 * channels)
    in_full = first_full[:, :weight_rows, : 2 * channels].reshape(-1, 2 * channels)
    output_full = first_full[:, :weight_rows, 2 * channels :].reshape(-1, channels)
    recur_full = first_full[:, weight_rows:, :channels].reshape(-1, channels)
    input_gate_full = first_full[:, weight_rows:, channels : 2 * channels].reshape(-1, channels)
    weights_one = gather_high(second)
    third = both_lows(third)
    both = product(normed_one, in_full)

    branch = both[:, :channels]
    gating = both[:, channels:]
    rim = shifted(branch[plane_rows - leading :], LO)
    branch_ext = jnp.concatenate([rim, branch], axis=0)
    conv_local = functools.partial(convolve, segment=conv_segment)
    conv_out, conv_pull = jax.vjp(conv_local, branch_ext, taps, bias)
    conv_low = lowered(conv_out)
    recur_raw = block_product(conv_low, recur_full)
    input_raw = block_product(conv_low, input_gate_full)
    rate_local = functools.partial(coefficients, reset=plane_reset)
    (decay, drive), rate_pull = jax.vjp(
        rate_local, recur_raw, input_raw, conv_out, bias_pair, decay_values
    )
    ones = jnp.ones((8, channels), jnp.float32)
    state, state_in = plane_scan(decay, drive, ones, high, False, cid["scan"])
    gate_act, gate_pull = jax.vjp(jax.nn.gelu, gating)
    mixed = lowered(state * gate_act)
    mixed, third = lax.optimization_barrier((mixed, third))
    (summed,) = scatter([product_right(mixed, output_full)], True, cid["scatter_full"])
    stream_one = stream_in + summed
    third = third.reshape(high * LO, -1, third.shape[1])
    query_full = third[:, :weight_rows, :query_width].reshape(-1, query_width)
    attn_full = third[:, :weight_rows, query_width:].reshape(-1, third.shape[2] - query_width)
    part_rows, part_width = keyvalue_weight.shape
    normed_two, keyvalue_full = gather(
        [lowered(rms_norm(stream_one, norm_gains[1])), third[:, weight_rows:].reshape(-1, part_width)],
        [True, False],
        cid["gather_weight"],
    )
    keyvalue_full = keyvalue_full.reshape(ways, high * LO, part_rows, part_width)
    keyvalue_full = keyvalue_full.transpose(1, 0, 2, 3).reshape(-1, part_width)
    factors = turns(position)
    own_factors = [lax.dynamic_slice_in_dim(each, tp * own_rows, own_rows, 0) for each in factors]
    segment_rows = jnp.broadcast_to(segment[None], (8, shard_rows))
    key_column = key_segment[:, None]
    early = (keyvalue_full, query_full, attn_full, factors, own_factors, segment_rows, key_column)
    normed_two, early = lax.optimization_barrier((normed_two, early))
    keyvalue_full, query_full, attn_full, factors, own_factors, segment_rows, key_column = early
    normed_two, weights_one, fourth = lax.optimization_barrier((normed_two, weights_one, fourth))
    weights_two = gather_high(fourth)
    summed, ab_one = dense_call("forward", normed_two, None, weights_one, None, cid["forward"])
    stream_two = stream_one + summed

    normed_own = lowered(rms_norm(stream_two, norm_gains[2]))
    keyval = product(normed_own, keyvalue_full)
    key_rot = lowered(rotate(keyval[:, :HD], own_factors))
    packed = jnp.concatenate([key_rot, lowered(keyval[:, HD:])], axis=1)
    earlier = [shifted(packed, offset) for offset in range(halo_shards, 0, -1)]
    normed_three, seen = gather(
        [normed_own, jnp.concatenate(earlier + [packed], axis=1)], [False, False], cid["gather_seen"]
    )
    extended = jnp.concatenate(
        [seen[:, 2 * HD * k : 2 * HD * (k + 1)] for k in range(halo_shards + 1)], axis=0
    )
    query = product(normed_three, query_full)
    attended, query_rot, log_total = attention(
        query, extended, segment_rows, key_column, *factors
    )
    (summed,) = scatter([product_right(attended, attn_full)], False, cid["scatter_half"])
    stream_three = stream_two + summed

    (normed_four,) = gather(
        [lowered(rms_norm(stream_three, norm_gains[3]))], [True], cid["gather_full"]
    )
    grad_normed, wire_two, hidden_two = dense_call(
        "both", normed_four, grad_low, weights_two, None, cid["both"]
    )
    done_two = reduce_high(wire_two)
    stream_grad, gain_four = jax.vjp(rms_norm, stream_three, norm_gains[3])[1](grad_normed)
    grad_stream = grad_stream + stream_grad
    (grad_attn_low,) = gather([lowered(grad_stream)], [False], cid["gather_half"])
    grad_attn_out = product_left(grad_attn_low, attended)
    grad_attended = lowered(product(grad_attn_low, attn_full))
    grad_query_low, grad_ext = attention_back(
        query_rot,
        extended,
        grad_attended,
        log_total,
        segment_rows,
        key_column,
        *factors,
    )
    grad_query = product_left(normed_three, grad_query_low)
    grad_pieces = grad_ext.reshape(halo_shards + 1, shard_rows, 2 * HD)
    partial = jnp.concatenate(
        [lowered(product_right(grad_query_low, query_full))] + list(grad_pieces), axis=1
    )
    partial, grad_query, grad_attn_out = lax.optimization_barrier(
        (partial, lowered(grad_query), lowered(grad_attn_out))
    )
    attn_kept, attn_given = swap_sums(jnp.concatenate([grad_query, grad_attn_out], axis=1))
    (summed,) = scatter([partial], False, cid["scatter_wide"])
    width = normed_own.shape[1]
    pieces = [
        summed[:, width + 2 * HD * k : width + 2 * HD * (k + 1)] for k in range(halo_shards + 1)
    ]
    keyvalue_total = pieces[halo_shards]
    for offset in range(1, halo_shards + 1):
        piece = shifted(lowered(pieces[halo_shards - offset]), -offset)
        keyvalue_total = keyvalue_total + piece.astype(jnp.float32)
    keyvalue_total, attn_given = lax.optimization_barrier((keyvalue_total, attn_given))
    done_attn = reduce_high(attn_kept.astype(jnp.float32) + attn_given.astype(jnp.float32))
    key_grad = rotate_back(keyvalue_total[:, :HD], own_factors)
    keyvalue_low = lowered(jnp.concatenate([key_grad, keyvalue_total[:, HD:]], axis=1))
    grad_normed = summed[:, :width] + product_right(keyvalue_low, keyvalue_full)
    stream_grad, gain_three = jax.vjp(rms_norm, stream_two, norm_gains[2])[1](grad_normed)
    grad_stream = grad_stream + stream_grad

    (grad_low,) = gather([lowered(grad_stream)], [True], cid["gather_full"])
    grad_low, done_two = lax.optimization_barrier((grad_low, done_two))
    done_two = dense_grads(exchanged(done_two))
    grad_normed, one_wire = dense_call(
        "backward", normed_two, grad_low, weights_one, ab_one, cid["backward"]
    )
    stream_grad, gain_two = jax.vjp(rms_norm, stream_one, norm_gains[1])[1](grad_normed)
    grad_stream = grad_stream + stream_grad
    grad_stream, one_wire, done_attn = lax.optimization_barrier(
        (grad_stream, one_wire, done_attn)
    )
    grad_stream, keyvalue_low = lax.optimization_barrier((grad_stream, keyvalue_low))
    done_one = reduce_high(one_wire)
    (keyvalue_grads,) = gather([keyvalue_low], [False], cid["gather_narrow"])
    grad_keyvalue = lowered(product_left(normed_three, keyvalue_grads))
    grad_keyvalue = grad_keyvalue.reshape(high * LO, ways, part_rows, part_width)
    grad_keyvalue = lax.dynamic_slice_in_dim(grad_keyvalue, tp, 1, 1)
    (grad_out_low,) = gather([lowered(grad_stream)], [True], cid["gather_full"])
    grad_out_low, hidden_two = lax.optimization_barrier((grad_out_low, hidden_two))
    (summed_four,) = dense_call("product", hidden_two, None, weights_two, None, cid["product"])
    grad_recur_out = product_left(grad_out_low, mixed)
    grad_mixed = product(grad_out_low, output_full)
    grad_mixed, done_attn, done_two = lax.optimization_barrier((grad_mixed, done_attn, done_two))
    done_attn = done_attn.astype(jnp.float32)
    grad_state = grad_mixed * gate_act
    grad_gating = lowered(gate_pull(grad_mixed * state)[0])
    decay_next = jnp.concatenate([decay[1:], jnp.ones((1, channels), jnp.float32)], axis=0)
    first_decay = jnp.broadcast_to(decay[:1], (8, channels))
    grad_drive, _ = plane_scan(decay_next, grad_state, first_decay, high, True, cid["scan_back"])
    state_prev = jnp.concatenate([state_in[:1], state[:-1]], axis=0)
    grad_decay = grad_drive * state_prev
    grad_recur_raw, grad_input_raw, grad_conv, grad_biases, grad_decay_param = rate_pull(
        (grad_decay, grad_drive)
    )
    grad_recur_gate, conv_back_recur = block_grads(conv_low, recur_full, lowered(grad_recur_raw))
    grad_input_gate, conv_back_input = block_grads(
        conv_low, input_gate_full, lowered(grad_input_raw)
    )
    grad_branch_ext, grad_taps, grad_conv_bias = conv_pull(
        grad_conv + conv_back_recur + conv_back_input
    )
    returned_rim = shifted(grad_branch_ext[:leading], -LO)
    grad_branch = grad_branch_ext[leading:] + jnp.pad(
        returned_rim, ((plane_rows - leading, 0), (0, 0))
    )
    both_low = jnp.concatenate([lowered(grad_branch), grad_gating], axis=1)
    grad_in = product_left(normed_one, both_low)
    partial = lowered(product_right(both_low, in_full))
    partial, grad_in, grad_recur_out = lax.optimization_barrier(
        (partial, lowered(grad_in), lowered(grad_recur_out))
    )
    blocks = high * LO
    wire = jnp.concatenate(
        [
            jnp.concatenate(
                [
                    grad_in.reshape(blocks, weight_rows, 2 * channels),
                    grad_recur_out.reshape(blocks, weight_rows, channels),
                ],
                axis=2,
            ),
            jnp.concatenate(
                [
                    lowered(grad_recur_gate).reshape(blocks, gate_rows, channels),
                    lowered(grad_input_gate).reshape(blocks, gate_rows, channels),
                    jnp.zeros((blocks, gate_rows, channels), jnp.bfloat16),
                ],
                axis=2,
            ),
            grad_keyvalue.reshape(blocks, -1, 3 * channels),
        ],
        axis=1,
    )
    wire, done_one, summed_four = lax.optimization_barrier((wire, done_one, summed_four))
    layer_own = lowered(stream_three + summed_four)
    last = reduce_high(wire.reshape(-1, 3 * channels))
    gain_one = jnp.sum(normed_one.astype(jnp.float32) * partial.astype(jnp.float32), axis=0)
    gain_one = gain_one / norm_gains[0]
    grad_normed, gains_sum, small, layer_out = scatter_and_sums(
        partial,
        jnp.concatenate(
            [jnp.stack([gain_one, gain_two, gain_three, gain_four]), jnp.zeros_like(norm_gains)]
        ),
        jnp.concatenate(
            [grad_taps, grad_conv_bias[None], grad_biases, grad_decay_param[None]], axis=0
        ),
        layer_own,
        high,
        cid["last"],
    )
    rms_local = functools.partial(rms_norm, gain=norm_gains[0])
    stream_grad = jax.vjp(rms_local, stream_in)[1](grad_normed)[0]
    input_own = lowered(grad_stream + stream_grad)
    done_one = exchanged(done_one)
    (input_grad,) = gather([input_own], [False], cid["gather_half"])
    gains_sum = gains_sum[: norm_gains.shape[0]]
    input_grad, layer_out, done_one, last = lax.optimization_barrier(
        (input_grad, layer_out, done_one, last)
    )
    input_grad = input_grad.astype(jnp.float32)
    layer_out = jnp.where(segment[:, None] < doc_lengths.shape[0], layer_out, 0)
    last = exchanged(last)
    keyvalue_grad = jnp.sum(last[:, weight_rows + gate_rows :].astype(jnp.float32), axis=0)
    last_rows, last_gates = (last[:, :weight_rows], last[:, weight_rows : weight_rows + gate_rows])
    return (
        layer_out,
        input_grad,
        gains_sum,
        joined(last_rows[:, :, :channels]),
        joined(last_rows[:, :, channels : 2 * channels]),
        small[:CONV],
        small[CONV],
        joined(last_gates[:, :, :channels]).T,
        joined(last_gates[:, :, channels : 2 * channels]).T,
        small[CONV + 1 : CONV + 3],
        small[CONV + 3],
        joined(last_rows[:, :, 2 * channels :]).T,
        *dense_grads(done_one),
        done_attn[:, :query_width],
        keyvalue_grad.reshape(keyvalue_weight.shape),
        done_attn[:, query_width:].T,
        *done_two,
    )


def solution(mesh):
    placed = (
        P("seq", None),
        P("seq", None),
        P(),
        P(),
        P("seq", "tp"),
        P("seq", "tp"),
        P(None, "tp"),
        P("tp"),
        P("tp", "seq"),
        P("tp", "seq"),
        P(None, "tp"),
        P("tp"),
        P("tp", "seq"),
        P("seq", "tp"),
        P("seq", "tp"),
        P("tp", "seq"),
        P("seq", "tp"),
        P(("seq", "tp"), None),
        P("tp", "seq"),
        P("seq", "tp"),
        P("seq", "tp"),
        P("tp", "seq"),
    )
    return jax.shard_map(
        local,
        mesh=mesh,
        in_specs=placed,
        out_specs=(
            P("seq", None),
            P("seq", None),
            P(),
            P("seq", "tp"),
            P("seq", "tp"),
            P(None, "tp"),
            P("tp"),
            P("tp", "seq"),
            P("tp", "seq"),
            P(None, "tp"),
            P("tp"),
            P("tp", "seq"),
            P("seq", "tp"),
            P("seq", "tp"),
            P("tp", "seq"),
            P("seq", "tp"),
            P(("seq", "tp"), None),
            P("tp", "seq"),
            P("seq", "tp"),
            P("seq", "tp"),
            P("tp", "seq"),
        ),
        check_vma=False,
    )
```

```python
import functools
import math

import jax
import jax.numpy as jnp
from jax import lax
from jax.experimental import pallas as pl
from jax.experimental.pallas import tpu as pltpu
from jax.sharding import PartitionSpec as P

HD = 128
CONV = 4
WINDOW = 1024


def product(left, right):
    return jnp.dot(left, right, preferred_element_type=jnp.float32)


def product_left(left, right):
    return lax.dot_general(
        left, right, (((0,), (0,)), ((), ())), preferred_element_type=jnp.float32
    )


def product_right(left, right):
    return lax.dot_general(
        left, right, (((1,), (1,)), ((), ())), preferred_element_type=jnp.float32
    )


def lowered(values):
    return values.astype(jnp.bfloat16)


def rms_norm(values, gain):
    return values * lax.rsqrt(jnp.mean(values * values, axis=-1, keepdims=True) + 1e-06) * gain


def gated(gate_values, up_values):
    return jax.nn.gelu(gate_values) * up_values


def layout(doc_lengths, first_slot, count):
    ends = jnp.cumsum(doc_lengths, dtype=jnp.int32)
    slots = first_slot + jnp.arange(count, dtype=jnp.int32)
    passed = slots[:, None] >= ends[None, :]
    segment = jnp.sum(passed.astype(jnp.int32), axis=1)
    begin = jnp.max(jnp.where(passed, ends[None, :], 0), axis=1)
    segment = jnp.where(slots < 0, -1, segment)
    position = slots - begin
    reset = (slots != begin).astype(jnp.float32)
    valid = (segment < doc_lengths.shape[0]).astype(jnp.float32)
    return (segment, position, reset, valid)


def convolve(extended, taps, bias, segment):
    leading = CONV - 1
    total_rows = extended.shape[0] - leading
    result = bias[None, :] + taps[0][None, :] * extended[leading:]
    for lag_index in range(1, CONV):
        same = (
            segment[leading:] == segment[leading - lag_index : leading - lag_index + total_rows]
        ).astype(jnp.float32)
        result = (
            result
            + same[:, None]
            * taps[lag_index][None, :]
            * extended[leading - lag_index : leading - lag_index + total_rows]
        )
    return result


def coefficients(recur_raw, input_raw, conv_values, bias_pair, decay_values, reset):
    recur_rate = jax.nn.sigmoid(recur_raw + bias_pair[0][None, :])
    input_rate = jax.nn.sigmoid(input_raw + bias_pair[1][None, :])
    log_decay = -8.0 * recur_rate * jax.nn.softplus(-decay_values)[None, :]
    multiplier = jnp.sqrt(jnp.maximum(-jnp.expm1(2.0 * log_decay), 0.01))
    return (jnp.exp(log_decay) * reset[:, None], multiplier * input_rate * conv_values)


def combine_state(earlier, later):
    return (earlier[0] * later[0], later[0] * earlier[1] + later[1])


MESH = pl.DeviceIdType.MESH
LO = 2
EIGHTEEN_US = pl.CostEstimate(flops=0, bytes_accessed=60_000_000, transcendentals=0)
TEN_US = pl.CostEstimate(flops=0, bytes_accessed=33_000_000, transcendentals=0)
ANY = pl.BlockSpec(memory_space=pl.ANY)
VMEM = pl.BlockSpec(memory_space=pltpu.VMEM)


def cube():
    seq = lax.axis_index("seq")
    tp = lax.axis_index("tp")
    a = lax.rem(seq, LO)
    b = tp // 2
    c = lax.rem(tp, 2)
    across_a = (seq - a + 1 - a, tp)
    across_b = (seq, (1 - b) * 2 + c)
    across_c = (seq, b * 2 + 1 - c)
    return (a, b, c, across_a, across_b, across_c)


def hail(devices):
    for device in devices:
        pl.semaphore_signal(
            pltpu.get_barrier_semaphore(), inc=1, device_id=device, device_id_type=MESH
        )


def greet(devices):
    hail(devices)
    pl.semaphore_wait(pltpu.get_barrier_semaphore(), len(devices))


def remote(src, dst, send_sem, recv_sem, slot, device):
    return pltpu.make_async_remote_copy(
        src_ref=src,
        dst_ref=dst,
        send_sem=send_sem.at[slot],
        recv_sem=recv_sem.at[slot],
        device_id=device,
        device_id_type=MESH,
    )


def in_turn(*runs):
    runs = list(runs)
    while runs:
        for run in list(runs):
            if next(run, "end") == "end":
                runs.remove(run)


def neighbours(full):
    across_a, across_b, across_c = cube()[3:]
    return [across_c, across_b] + ([across_a] if full else [])


def gather_steps(full, in_ref, out_ref, send_sem, recv_sem, local_sem):
    a, b, c, across_a, across_b, across_c = cube()
    half = in_ref.shape[0] // 2

    def index(pa, pb, pc):
        return pa * 4 + pb * 2 + pc if full else pb * 2 + pc

    me, an, bn, dn = (
        index(a, b, c),
        index(1 - a, b, c),
        index(a, 1 - b, c),
        index(1 - a, 1 - b, c),
    )
    low, high = (pl.ds(0, half), pl.ds(half, half))
    sent = {}

    def go(slot, src, dst, device):
        copy = remote(src, dst, send_sem, recv_sem, slot, device)
        copy.start()
        sent[slot] = copy

    def own(slot, part, device):
        go(slot, in_ref.at[part], out_ref.at[me, part], device)

    def onward(slot, block, part, device):
        go(slot, out_ref.at[block, part], out_ref.at[block, part], device)

    if full:
        own(0, low, across_a)
    own(1, high, across_b)
    if full:
        own(2, high, across_a)
    own(3, low, across_b)
    go(4, in_ref, out_ref.at[me], across_c)
    mine = pltpu.make_async_copy(in_ref, out_ref.at[me], local_sem)
    mine.start()
    yield
    if full:
        sent[0].wait_recv()
        onward(5, an, low, across_b)
        onward(6, an, low, across_c)
        yield
    sent[1].wait_recv()
    if full:
        onward(7, bn, high, across_a)
    onward(8, bn, high, across_c)
    yield
    if full:
        sent[2].wait_recv()
        onward(9, an, high, across_c)
        yield
    sent[3].wait_recv()
    onward(10, bn, low, across_c)
    yield
    if full:
        sent[5].wait_recv()
        onward(11, dn, low, across_c)
        yield
        sent[7].wait_recv()
        onward(12, dn, high, across_c)
        yield
    for slot in (4, 6, 8, 9, 10, 11, 12):
        if slot in sent:
            sent[slot].wait_recv()
    for copy in sent.values():
        copy.wait_send()
    mine.wait()


def gather_kernel(spans, *refs):
    count = len(spans)
    in_refs, out_refs = (refs[:count], refs[count : 2 * count])
    send_sem, recv_sem, local_sem = refs[2 * count :]
    greet(neighbours(any(spans)))
    in_turn(
        *[
            gather_steps(
                spans[k], in_refs[k], out_refs[k], send_sem.at[k], recv_sem.at[k], local_sem.at[k]
            )
            for k in range(count)
        ]
    )


def gather(blocks, spans, collective_id):
    count = len(blocks)
    ways = [8 if span else 4 for span in spans]
    results = pl.pallas_call(
        functools.partial(gather_kernel, spans),
        out_shape=[
            jax.ShapeDtypeStruct((n, *block.shape), block.dtype) for n, block in zip(ways, blocks)
        ],
        in_specs=[ANY] * count,
        out_specs=[ANY] * count,
        scratch_shapes=[
            pltpu.SemaphoreType.DMA((count, 13)),
            pltpu.SemaphoreType.DMA((count, 13)),
            pltpu.SemaphoreType.DMA((count,)),
        ],
        name="gather_full" if any(spans) else "gather_half",
        cost_estimate=EIGHTEEN_US,
        compiler_params=pltpu.CompilerParams(collective_id=collective_id, has_side_effects=True),
    )(*blocks)
    return [
        result.reshape(n * block.shape[0], block.shape[1])
        for n, result, block in zip(ways, results, blocks)
    ]


def scatter_steps(
    full, part_ref, out_ref, cbuf, sx, sy, tx, ty, ax, by, rx, ry, csend, crecv, send_sem, recv_sem
):
    a, b, c, across_a, across_b, across_c = cube()
    half = part_ref.shape[1] // 2

    def index(pa, pb, pc):
        return pa * 4 + pb * 2 + pc if full else pb * 2 + pc

    def pair(pa, pb):
        return pa * 2 + pb if full else pb

    low, high = (pl.ds(0, half), pl.ds(half, half))
    if full:
        order = [
            (1 - a, 1 - b, low),
            (1 - a, 1 - b, high),
            (1 - a, b, low),
            (a, 1 - b, high),
            (a, 1 - b, low),
            (1 - a, b, high),
            (a, b, low),
            (a, b, high),
        ]
    else:
        order = [(a, 1 - b, low), (a, 1 - b, high), (a, b, low), (a, b, high)]
    core = {}

    def share(*which):
        for k in which:
            pa, pb, part = order[k]
            core[k] = remote(
                part_ref.at[index(pa, pb, 1 - c), part],
                cbuf.at[pair(pa, pb), part],
                csend,
                crecv,
                k,
                across_c,
            )
            core[k].start()

    def summed(k):
        pa, pb, part = order[k]
        core[k].wait_recv()
        return part_ref[index(pa, pb, c), part].astype(jnp.float32) + cbuf[
            pair(pa, pb), part
        ].astype(jnp.float32)

    sent = []

    def go(src, dst, slot, device):
        copy = remote(src, dst, send_sem, recv_sem, slot, device)
        copy.start()
        sent.append(copy)
        return copy

    if full:
        yield
        share(0, 1)
        yield
        share(2, 5)
        sx[0] = lowered(summed(0))
        x0 = go(sx.at[0], ax.at[0], 0, across_a)
        sy[0] = lowered(summed(1))
        y0 = go(sy.at[0], by.at[0], 1, across_b)
        yield
        share(3, 4)
        sx[1] = lowered(summed(2))
        x1 = go(sx.at[1], ax.at[1], 2, across_a)
        sy[1] = lowered(summed(3))
        y1 = go(sy.at[1], by.at[1], 3, across_b)
        yield
        share(6, 7)
        yield
        total = summed(4)
        x0.wait_recv()
        ty[...] = lowered(total + ax[0].astype(jnp.float32))
        last_y = go(ty, ry, 4, across_b)
        total = summed(5)
        y0.wait_recv()
        tx[...] = lowered(total + by[0].astype(jnp.float32))
        last_x = go(tx, rx, 5, across_a)
        yield
        total = summed(6)
        x1.wait_recv()
        total = total + ax[1].astype(jnp.float32)
        last_y.wait_recv()
        out_ref[low] = total + ry[...].astype(jnp.float32)
        total = summed(7)
        y1.wait_recv()
        total = total + by[1].astype(jnp.float32)
        last_x.wait_recv()
        out_ref[high] = total + rx[...].astype(jnp.float32)
    else:
        share(0, 1, 2, 3)
        sy[0] = lowered(summed(0))
        y0 = go(sy.at[0], by.at[0], 1, across_b)
        sy[1] = lowered(summed(1))
        y1 = go(sy.at[1], by.at[1], 3, across_b)
        yield
        total = summed(2)
        y0.wait_recv()
        out_ref[low] = total + by[0].astype(jnp.float32)
        total = summed(3)
        y1.wait_recv()
        out_ref[high] = total + by[1].astype(jnp.float32)
    for copy in [*core.values(), *sent]:
        copy.wait_send()


def scatter_kernel(full, count, *refs):
    greet(neighbours(full))
    in_turn(
        *[
            scatter_steps(full, refs[k], refs[count + k], *refs[2 * count + 13 * k :][:13])
            for k in range(count)
        ]
    )


def scatter_scratch(ways, rows, width):
    half = rows // 2
    shapes = [(ways // 2, rows, width)] + [(2, half, width)] * 2 + [(half, width)] * 2
    shapes += [(2, half, width)] * 2 + [(half, width)] * 2
    return [pltpu.VMEM(shape, jnp.bfloat16) for shape in shapes] + [
        pltpu.SemaphoreType.DMA((k,)) for k in (8, 8, 6, 6)
    ]


def scatter(partials, full, collective_id):
    ways = 8 if full else 4
    count = len(partials)
    rows = partials[0].shape[0] // ways
    scratch = []
    for partial in partials:
        scratch += scatter_scratch(ways, rows, partial.shape[1])
    return pl.pallas_call(
        functools.partial(scatter_kernel, full, count),
        out_shape=[
            jax.ShapeDtypeStruct((rows, partial.shape[1]), jnp.float32) for partial in partials
        ],
        in_specs=[VMEM] * count,
        out_specs=[VMEM] * count,
        scratch_shapes=scratch,
        name="scatter_full" if full else "scatter_half",
        cost_estimate=EIGHTEEN_US,
        compiler_params=pltpu.CompilerParams(
            collective_id=collective_id, has_side_effects=True, vmem_limit_bytes=48 * 2**20
        ),
    )(*[lowered(partial).reshape(ways, rows, -1) for partial in partials])


def scan_kernel(
    high, reverse, decay_ref, drive_ref, end_ref, state_ref, carry_ref, cum, strips, sendbuf, recvbuf, send_sem, recv_sem
):
    rows, width = decay_ref.shape
    strands = 8
    steps = rows // strands
    lanes = 128
    blocks = width // lanes
    mine = lax.axis_index("seq") // LO
    peers = high_peers(high)
    greet(peers)
    for n in range(blocks):
        cum[n] = decay_ref[:, n * lanes : (n + 1) * lanes]
        strips[n] = drive_ref[:, n * lanes : (n + 1) * lanes]

    def step(i, carry):
        r = steps - 1 - i if reverse else i
        at = pl.ds(r, strands, stride=steps)
        new = []
        for n in range(blocks):
            a = cum[n, at, :]
            product_now = carry[2 * n] * a
            state_now = carry[2 * n + 1] * a + strips[n, at, :]
            cum[n, at, :] = product_now
            strips[n, at, :] = state_now
            new += [product_now, state_now]
        return tuple(new)

    ones = jnp.ones((strands, lanes), jnp.float32)
    ends = lax.fori_loop(0, steps, step, (ones, jnp.zeros_like(ones)) * blocks, unroll=8)
    strand_order = list(range(strands - 1, -1, -1)) if reverse else list(range(strands))
    before = {}
    for n in range(blocks):
        total_a = jnp.ones((1, lanes), jnp.float32)
        total_h = jnp.zeros((1, lanes), jnp.float32)
        for k in strand_order:
            before[n, k] = (total_a, total_h)
            a, h = (ends[2 * n][k : k + 1], ends[2 * n + 1][k : k + 1])
            total_h = a * total_h + h
            total_a = a * total_a
        scale = end_ref[0:1, n * lanes : (n + 1) * lanes]
        sendbuf[n, 0:1, :] = total_a * scale
        sendbuf[n, 1:2, :] = total_h * scale
        sendbuf[n, 2:8, :] = jnp.zeros((6, lanes), jnp.float32)
    copies = []
    for k, peer in enumerate(peers):
        copy = remote(sendbuf, recvbuf.at[k], send_sem, recv_sem, k, peer)
        copy.start()
        copies.append(copy)
    for copy in copies:
        copy.wait_recv()
    for n in range(blocks):
        carry = jnp.zeros((1, lanes), jnp.float32)
        for turn in range(high - 1):
            plane = high - 1 - turn if reverse else turn
            away = lax.rem(mine - plane + high, high)
            reached = plane > mine if reverse else plane < mine
            got = recvbuf[jnp.where(reached, away - 1, 0), n]
            carry = jnp.where(reached, got[0:1] * carry + got[1:2], carry)
        span = pl.ds(n * lanes, lanes)
        carry_ref[:, span] = jnp.broadcast_to(carry, (carry_ref.shape[0], lanes))
        for k in range(strands):
            enter = before[n, k][0] * carry + before[n, k][1]
            at = pl.ds(k * steps, steps)
            state_ref[at, span] = strips[n, at, :] + cum[n, at, :] * enter
    for copy in copies:
        copy.wait_send()


def plane_scan(decay, drive, end_scale, high, reverse, collective_id):
    rows, width = decay.shape
    return pl.pallas_call(
        functools.partial(scan_kernel, high, reverse),
        out_shape=(
            jax.ShapeDtypeStruct((rows, width), jnp.float32),
            jax.ShapeDtypeStruct((8, width), jnp.float32),
        ),
        in_specs=[VMEM] * 3,
        out_specs=(VMEM, VMEM),
        scratch_shapes=[
            pltpu.VMEM((width // 128, rows, 128), jnp.float32),
            pltpu.VMEM((width // 128, rows, 128), jnp.float32),
            pltpu.VMEM((width // 128, 8, 128), jnp.float32),
            pltpu.VMEM((high - 1, width // 128, 8, 128), jnp.float32),
            pltpu.SemaphoreType.DMA((high - 1,)),
            pltpu.SemaphoreType.DMA((high - 1,)),
        ],
        name="scan_back" if reverse else "scan",
        cost_estimate=TEN_US,
        compiler_params=pltpu.CompilerParams(
            collective_id=collective_id, has_side_effects=True, vmem_limit_bytes=32 * 2**20
        ),
    )(decay, drive, end_scale)


def small_steps(high, gains_ref, rest_ref, gains_out, rest_out, gbuf, rbuf, ghold, rhold, gpair, rpair, send_sem, recv_sem):
    a, b, c, across_a, across_b, across_c = cube()
    peers = high_peers(high)
    copies = []
    for k, peer in enumerate(peers):
        for n, (src, dst) in enumerate(((gains_ref, gbuf.at[k]), (rest_ref, rbuf.at[k]))):
            copy = remote(src, dst, send_sem, recv_sem, 2 * k + n, peer)
            copy.start()
            copies.append(copy)
    yield
    for copy in copies:
        copy.wait_recv()
    gains = gains_ref[...]
    rest = rest_ref[...]
    for k in range(high - 1):
        gains = gains + gbuf[k]
        rest = rest + rbuf[k]
    rhold[...] = rest
    slot = 2 * (high - 1)
    swap = remote(rhold, rpair, send_sem, recv_sem, slot, across_a)
    swap.start()
    copies.append(swap)
    for n, device in enumerate((across_a, across_b, across_c)):
        ghold[n] = gains
        copy = remote(ghold.at[n], gpair.at[n], send_sem, recv_sem, slot + 1 + n, device)
        copy.start()
        copies.append(copy)
        yield
        copy.wait_recv()
        gains = gains + gpair[n]
    swap.wait_recv()
    gains_out[...] = gains
    other = rpair[...]
    width = rest.shape[1]
    rest_out[:, :width] = jnp.where(a == 0, rest, other)
    rest_out[:, width:] = jnp.where(a == 0, other, rest)
    for copy in copies:
        copy.wait_send()


def high_peers(high):
    seq = lax.axis_index("seq")
    tp = lax.axis_index("tp")
    return [(lax.rem(seq // LO + k, high) * LO + lax.rem(seq, LO), tp) for k in range(1, high)]


def last_kernel(high, part_ref, gains_ref, rest_ref, in_ref, out_ref, gains_out, rest_out, all_ref, *more):
    greet(high_peers(high) + neighbours(True))
    in_turn(
        small_steps(high, gains_ref, rest_ref, gains_out, rest_out, *more[13:21]),
        scatter_steps(True, part_ref, out_ref, *more[:13]),
        gather_steps(False, in_ref, all_ref, *more[21:]),
    )


def scatter_and_sums(partial, gains, rest, block, high, collective_id):
    slots = 2 * (high - 1) + 4
    ways = 8
    width = partial.shape[1]
    rows = partial.shape[0] // ways
    *sums, gathered = pl.pallas_call(
        functools.partial(last_kernel, high),
        out_shape=[
            jax.ShapeDtypeStruct((rows, width), jnp.float32),
            jax.ShapeDtypeStruct(gains.shape, jnp.float32),
            jax.ShapeDtypeStruct((rest.shape[0], LO * rest.shape[1]), jnp.float32),
            jax.ShapeDtypeStruct((4, *block.shape), block.dtype),
        ],
        in_specs=[VMEM] * 3 + [ANY],
        out_specs=[VMEM] * 3 + [ANY],
        scratch_shapes=scatter_scratch(ways, rows, width)
        + [
            pltpu.VMEM((high - 1, *gains.shape), jnp.float32),
            pltpu.VMEM((high - 1, *rest.shape), jnp.float32),
            pltpu.VMEM((3, *gains.shape), jnp.float32),
            pltpu.VMEM(rest.shape, jnp.float32),
            pltpu.VMEM((3, *gains.shape), jnp.float32),
            pltpu.VMEM(rest.shape, jnp.float32),
            pltpu.SemaphoreType.DMA((slots,)),
            pltpu.SemaphoreType.DMA((slots,)),
            pltpu.SemaphoreType.DMA((13,)),
            pltpu.SemaphoreType.DMA((13,)),
            pltpu.SemaphoreType.DMA,
        ],
        name="scatter_and_sums",
        cost_estimate=EIGHTEEN_US,
        compiler_params=pltpu.CompilerParams(
            collective_id=collective_id, has_side_effects=True, vmem_limit_bytes=40 * 2**20
        ),
    )(lowered(partial).reshape(ways, rows, width), gains, rest, block)
    return (*sums, gathered.reshape(-1, block.shape[1]))


def gelu_parts(x):
    inner = math.sqrt(2 / math.pi)
    curve = jnp.tanh(inner * (x + 0.044715 * x * x * x))
    half = 0.5 * (1 + curve)
    slope = half + 0.5 * x * (1 - curve * curve) * inner * (1 + 3 * 0.044715 * x * x)
    return (x * half, slope)


def dense_kernel(mode, main, *refs):
    refs = list(refs)

    def take(wanted=True):
        return refs.pop(0) if wanted else None

    grads = mode in ("both", "backward")
    fresh = mode in ("both", "forward")
    n_hbm = take(mode != "product")
    g_hbm = take(grads)
    w_hbm = take()
    ab_hbm = take(mode == "backward")
    hid_in = take(mode == "product")
    out_ref = take()
    wire_hbm = take(grads)
    ab_out = take(mode == "forward")
    hid_out = take(mode == "both")
    w_v, hid_v, part_v = (take(), take(), take())
    n_v = take(mode != "product")
    g_v, low_v, wire_v = (take(grads), take(grads), take(grads))
    ab_v = take(mode in ("forward", "backward"))
    buffers = [take() for _ in range(13)]
    sems = take()
    lanes = 128
    both = 2 * main + lanes
    tile = 256
    a, b = cube()[:2]
    near = neighbours(True)
    hail(near)
    up_part, down_part = (pl.ds(0, both), pl.ds(both, w_v.shape[1] - both))
    loads = {}

    def load(name, src, dst):
        loads[name] = pltpu.make_async_copy(src, dst, sems.at[len(loads)])
        loads[name].start()

    def need(*names):
        for name in names:
            if name in loads:
                loads.pop(name).wait()

    tiles = ((1 - a, 1 - b), (1 - a, b), (a, 1 - b), (a, b))

    def rows_of(pa, pb):
        return pl.ds(pl.multiple_of((pa * 4 + pb * 2) * lanes, tile), tile)

    def load_rows(turn, **pairs):
        at = rows_of(*tiles[turn])
        for name, (src, dst) in pairs.items():
            if src is not None:
                load(f"{name}{turn}", src.at[at], dst.at[at])

    for turn in range(4):
        load_rows(turn, n=(n_hbm, n_v), hid=(hid_in, hid_v), ab=(ab_hbm, ab_v))
        if turn == 0 and mode != "product":
            load("up", w_hbm.at[:, up_part], w_v.at[:, up_part])
        load_rows(turn, g=(g_hbm, g_v))
        if turn == 0:
            load("down", w_hbm.at[:, down_part], w_v.at[:, down_part])

    def work(turn):
        pa, pb = tiles[turn]
        block = pa * 4 + pb * 2
        at = rows_of(pa, pb)
        if mode == "product":
            need(f"hid{turn}", "down")
            part = lowered(product_right(hid_v[at, :], w_v[:, both:]))
            part_v[pl.ds(block, 2)] = part.reshape(2, lanes, part.shape[1])
            return
        need(f"n{turn}")
        if fresh:
            need("up")
            ab = product(n_v[at, :], w_v[:, :both])
            if mode == "forward":
                ab_v[at, :] = ab
        else:
            need(f"ab{turn}")
            ab = ab_v[at, :]
        gate, up, tail = (ab[:, :main], ab[:, main : 2 * main], ab[:, 2 * main :])
        first = lax.broadcasted_iota(jnp.int32, tail.shape, 1) < lanes // 2
        turned = pltpu.roll(tail, lanes // 2, 1)
        act, slope = gelu_parts(gate)
        tail_act, tail_slope = gelu_parts(tail)
        hid_v[at, :main] = lowered(act * up)
        hid_v[at, main:] = lowered(jnp.where(first, tail_act * turned, 0.0))
        need(f"g{turn}", "down")
        if grads:
            grad = product(g_v[at, :], w_v[:, both:])
            grad_main, grad_tail = (grad[:, :main], grad[:, main:])
            low_v[at, :main] = lowered(grad_main * up * slope)
            low_v[at, main : 2 * main] = lowered(grad_main * act)
            turned_grad = pltpu.roll(grad_tail, lanes // 2, 1)
            turned_act = pltpu.roll(tail_act, lanes // 2, 1)
            low_v[at, 2 * main :] = lowered(
                jnp.where(first, grad_tail * turned * tail_slope, turned_grad * turned_act)
            )
            need("up")
            part = lowered(product_right(low_v[at, :], w_v[:, :both]))
        else:
            part = lowered(product_right(hid_v[at, :], w_v[:, both:]))
        part_v[pl.ds(block, 2)] = part.reshape(2, lanes, part.shape[1])

    schedule = scatter_steps(True, part_v, out_ref, *buffers)
    next(schedule)
    for turn in range(4):
        work(turn)
        if turn == 0:
            pl.semaphore_wait(pltpu.get_barrier_semaphore(), len(near))
        next(schedule)
    next(schedule)
    stores = []

    def store(src, dst, slot):
        copy = pltpu.make_async_copy(src, dst, sems.at[slot])
        copy.start()
        stores.append(copy)

    if mode == "both":
        store(hid_v, hid_out, 16)
    if mode == "forward":
        store(ab_v, ab_out, 16)
    if grads:
        half = w_v.shape[0] // 2
        for part in range(2):
            cols = pl.ds(part * half, half)
            wire_v[cols, :both] = lowered(product_left(n_v[:, cols], low_v[...]))
            wire_v[cols, both:] = lowered(product_left(g_v[:, cols], hid_v[...]))
            store(wire_v.at[cols], wire_hbm.at[cols], 17 + part)
    next(schedule, None)
    for copy in stores:
        copy.wait()


def dense_call(mode, rows_in, grad_low, weights, ab, collective_id):
    rows = rows_in.shape[0]
    depth, columns = weights.shape
    main = (columns // 128 - 2) // 3 * 128
    both = 2 * main + 128
    grads = mode in ("both", "backward")
    low = jnp.bfloat16
    wide = ((rows, depth), low)
    hidden = ((rows, columns - both), low)
    if mode == "product":
        operands = [weights, rows_in]
    else:
        operands = [rows_in] + ([grad_low] if grads else []) + [weights]
    if mode == "backward":
        operands.append(ab)
    extra = {
        "forward": [((rows, both), jnp.float32)],
        "backward": [(weights.shape, low)],
        "both": [(weights.shape, low), hidden],
        "product": [],
    }[mode]
    scratch = [(weights.shape, low), hidden, ((8, rows // 8, depth), low)]
    if mode != "product":
        scratch.append(wide)
    if grads:
        scratch += [wide, ((rows, both), low), (weights.shape, low)]
    if mode in ("forward", "backward"):
        scratch.append(((rows, both), jnp.float32))
    return pl.pallas_call(
        functools.partial(dense_kernel, mode, main),
        out_shape=[
            jax.ShapeDtypeStruct(shape, kind)
            for shape, kind in [((rows // 8, depth), jnp.float32)] + extra
        ],
        in_specs=[ANY] * len(operands),
        out_specs=[VMEM] + [ANY] * len(extra),
        scratch_shapes=[pltpu.VMEM(shape, kind) for shape, kind in scratch]
        + scatter_scratch(8, rows // 8, depth)
        + [pltpu.SemaphoreType.DMA((19,))],
        name="dense_" + mode,
        cost_estimate=pl.CostEstimate(
            flops=0, bytes_accessed=100_000_000 if grads else 75_000_000, transcendentals=0
        ),
        compiler_params=pltpu.CompilerParams(
            collective_id=collective_id, has_side_effects=True, vmem_limit_bytes=56 * 2**20
        ),
    )(*operands)


def attention_kernel(
    shift, query_ref, ext_ref, here_ref, there_ref, cos_ref, sin_ref, out_ref, rot_ref, log_ref
):
    tile = 256
    rows, width = query_ref.shape
    heads = width // HD
    reach = shift + tile
    scale = HD ** (-0.5)
    log_ref[...] = jnp.zeros_like(log_ref)

    def turn(n, carry):
        h = n // (rows // tile)
        first = pl.multiple_of(lax.rem(n, rows // tile) * tile, tile)
        lanes = pl.ds(pl.multiple_of(h * HD, HD), HD)
        at = pl.ds(first, tile)
        seen = pl.ds(first, reach)
        query = query_ref[at, lanes]
        query = query * cos_ref[at, :] + pltpu.roll(query, HD // 2, 1) * sin_ref[at, :]
        query = lowered(query)
        rot_ref[at, lanes] = query
        allowed = visible(shift, there_ref[seen, :], here_ref[0:1, at])
        scores = jnp.where(allowed, product_right(ext_ref[seen, :HD], query) * scale, -1e30)
        top = jnp.max(scores, axis=0, keepdims=True)
        probs = jnp.exp(scores - top)
        total = jnp.sum(probs, axis=0, keepdims=True)
        log_ref[pl.ds(h, 1), at] = top + jnp.log(total)
        out_ref[at, lanes] = lowered(product_left(lowered(probs / total), ext_ref[seen, HD:]))
        return carry

    lax.fori_loop(0, heads * (rows // tile), turn, 0)


def visible(shift, there, here):
    shape = (there.shape[0], here.shape[1])
    distance = (
        lax.broadcasted_iota(jnp.int32, shape, 1) - lax.broadcasted_iota(jnp.int32, shape, 0) + shift
    )
    return (there == here) & (distance >= 0) & (distance < WINDOW)


def attention(query, extended, here, there, cosine, sine):
    rows, width = query.shape
    return pl.pallas_call(
        functools.partial(attention_kernel, extended.shape[0] - rows),
        out_shape=[
            jax.ShapeDtypeStruct((rows, width), jnp.bfloat16),
            jax.ShapeDtypeStruct((rows, width), jnp.bfloat16),
            jax.ShapeDtypeStruct((8, rows), jnp.float32),
        ],
        in_specs=[VMEM] * 6,
        out_specs=[VMEM] * 3,
        name="attention",
        cost_estimate=TEN_US,
        compiler_params=pltpu.CompilerParams(vmem_limit_bytes=48 * 2**20),
    )(query, extended, here, there, cosine, sine)


def attention_back_kernel(
    shift, query_ref, ext_ref, grad_ref, log_ref, here_ref, there_ref, cos_ref, sin_ref, dquery_ref, dext_ref, total
):
    tile = 256
    rows, width = query_ref.shape
    heads = width // HD
    reach = shift + tile
    scale = HD ** (-0.5)
    total[...] = jnp.zeros_like(total)

    def turn(n, carry):
        h = n // (rows // tile)
        first = pl.multiple_of(lax.rem(n, rows // tile) * tile, tile)
        lanes = pl.ds(pl.multiple_of(h * HD, HD), HD)
        at = pl.ds(first, tile)
        seen = pl.ds(first, reach)
        query = query_ref[at, lanes]
        grad = grad_ref[at, lanes]
        keys = ext_ref[seen, :HD]
        values = ext_ref[seen, HD:]
        allowed = visible(shift, there_ref[seen, :], here_ref[0:1, at])
        scores = jnp.where(allowed, product_right(keys, query) * scale, -1e30)
        probs = jnp.exp(scores - log_ref[pl.ds(h, 1), at])
        grad_probs = product_right(values, grad)
        mean = jnp.sum(probs * grad_probs, axis=0, keepdims=True)
        grad_scores = lowered(probs * (grad_probs - mean) * scale)
        total[seen, :HD] += product(grad_scores, query)
        total[seen, HD:] += product(lowered(probs), grad)
        turned = product_left(grad_scores, keys)
        turned = turned * cos_ref[at, :] - pltpu.roll(turned, HD // 2, 1) * sin_ref[at, :]
        dquery_ref[at, lanes] = lowered(turned)
        return carry

    lax.fori_loop(0, heads * (rows // tile), turn, 0)
    dext_ref[...] = lowered(total[...])


def attention_back(query_rot, extended, grad, log_total, here, there, cosine, sine):
    rows, width = query_rot.shape
    seen = extended.shape[0]
    return pl.pallas_call(
        functools.partial(attention_back_kernel, seen - rows),
        out_shape=[
            jax.ShapeDtypeStruct((rows, width), jnp.bfloat16),
            jax.ShapeDtypeStruct((seen, 2 * HD), jnp.bfloat16),
        ],
        in_specs=[VMEM] * 8,
        out_specs=[VMEM] * 2,
        scratch_shapes=[pltpu.VMEM((seen, 2 * HD), jnp.float32)],
        name="attention_back",
        cost_estimate=EIGHTEEN_US,
        compiler_params=pltpu.CompilerParams(vmem_limit_bytes=48 * 2**20),
    )(query_rot, extended, grad, log_total, here, there, cosine, sine)


def stacked_by_low(mine, other):
    lo = lax.rem(lax.axis_index("seq"), LO)
    return jnp.stack([jnp.where(lo == 0, mine, other), jnp.where(lo == 0, other, mine)])


def swap_low(block):
    count = lax.axis_size("seq")
    return lax.ppermute(block, "seq", [(s, s // LO * LO + (1 - s % LO)) for s in range(count)])


def high_groups():
    count = lax.axis_size("seq")
    return [[h * LO + l for h in range(count // LO)] for l in range(LO)]


def swap_columns(*parts):
    return swap_pieces([jnp.concatenate(each, axis=1) for each in zip(*map(split_columns, parts))])


def swap_pieces(halves):
    lo = lax.rem(lax.axis_index("seq"), LO)
    kept = jnp.where(lo == 0, halves[0], halves[1])
    given = jnp.where(lo == 0, halves[1], halves[0])
    both = stacked_by_low(kept, swap_low(given))
    return both.reshape(-1, both.shape[2])


def gather_high(rows):
    return lax.all_gather(rows, "seq", axis=0, tiled=True, axis_index_groups=high_groups())


def reduce_high(grad):
    return lax.psum_scatter(
        lowered(grad), "seq", scatter_dimension=0, tiled=True, axis_index_groups=high_groups()
    )


def exchanged(both):
    lo = lax.rem(lax.axis_index("seq"), LO)
    both = both.reshape(LO, -1, both.shape[1])
    kept = jnp.where(lo == 0, both[0], both[1])
    given = jnp.where(lo == 0, both[1], both[0])
    return stacked_by_low(kept, swap_low(given))


def split_columns(block):
    width = block.shape[1] // LO
    return [block[:, l * width : (l + 1) * width] for l in range(LO)]


def joined(blocks):
    return jnp.concatenate([blocks[l] for l in range(LO)], axis=1).astype(jnp.float32)


def block_product(values, weight):
    block_width = weight.shape[0]
    blocks = weight.shape[1] // block_width
    return jnp.concatenate(
        [
            product_right(
                values[:, n * block_width : (n + 1) * block_width],
                weight[:, n * block_width : (n + 1) * block_width],
            )
            for n in range(blocks)
        ],
        axis=1,
    )


def block_grads(values, weight, upstream):
    block_width = weight.shape[0]
    cuts = [slice(n * block_width, (n + 1) * block_width) for n in range(weight.shape[1] // block_width)]
    return (
        jnp.concatenate([product_left(upstream[:, s], values[:, s]) for s in cuts], axis=1),
        jnp.concatenate([product(upstream[:, s], weight[:, s]) for s in cuts], axis=1),
    )


def shifted(block, distance):
    count = lax.axis_size("seq")
    route = [(i - distance, i) for i in range(count) if 0 <= i - distance < count]
    return lax.ppermute(block, "seq", route)


CIDS = {
    "gather_full": 0,
    "gather_half": 1,
    "scatter_full": 2,
    "scatter_half": 3,
    "scan": 4,
    "scan_back": 5,
    "scatter_wide": 6,
    "last": 7,
    "gather_narrow": 8,
    "gather_two": 9,
    "forward": 10,
    "both": 11,
    "backward": 12,
    "gather_weight": 13,
    "gather_seen": 14,
    "product": 15,
}


def dense_wire(gate, up, down):
    pieces = []
    for g, u, d in zip(*map(split_columns, (gate, up, down))):
        main = g.shape[1] // 128 * 128
        blank = jnp.zeros((d.shape[0], -d.shape[1] % 128), d.dtype)
        pieces.append(
            jnp.concatenate([g[:, :main], u[:, :main], g[:, main:], u[:, main:], d, blank], axis=1)
        )
    return pieces


def dense_grads(both):
    columns = both.shape[2]
    main = (columns // 128 - 2) // 3 * 128
    tail = 64
    ends = 2 * main

    def part(first, last):
        return jnp.concatenate([both[:, :, first : first + main], both[:, :, last : last + tail]], axis=2)

    return (
        joined(part(0, ends)),
        joined(part(main, ends + tail)),
        joined(both[:, :, ends + 2 * tail : ends + 3 * tail + main]).T,
    )


def turns(position):
    half_width = HD // 2
    frequency = 10000.0 ** (-jnp.arange(half_width, dtype=jnp.float32) / half_width)
    angle = position.astype(jnp.float32)[:, None] * jnp.tile(frequency, 2)[None, :]
    sign = jnp.where(jnp.arange(HD) < half_width, -1.0, 1.0)
    return (jnp.cos(angle), jnp.sin(angle) * sign[None, :])


def rotate(values, factors):
    cosine, sine = factors
    half_width = HD // 2
    swapped = jnp.concatenate([values[..., half_width:], values[..., :half_width]], axis=-1)
    return values * cosine + swapped * sine


def rotate_back(values, factors):
    cosine, sine = factors
    half_width = HD // 2
    swapped = jnp.concatenate([values[..., half_width:], values[..., :half_width]], axis=-1)
    return values * cosine - swapped * sine


def both_lows(lanes):
    other = swap_low(lanes)
    lo = lax.rem(lax.axis_index("seq"), LO)
    both = jnp.stack([jnp.where(lo == 0, lanes, other), jnp.where(lo == 0, other, lanes)], axis=1)
    return both.reshape(-1, lanes.shape[2])


def swap_sums(grad):
    lo = lax.rem(lax.axis_index("seq"), LO)
    pairs = grad.reshape(lax.axis_size("seq") // LO, LO, -1, grad.shape[1])
    kept = jnp.where(lo == 0, pairs[:, 0], pairs[:, 1])
    given = jnp.where(lo == 0, pairs[:, 1], pairs[:, 0])
    return (kept.reshape(-1, grad.shape[1]), swap_low(given).reshape(-1, grad.shape[1]))


def local(
    tokens,
    cotangent,
    doc_lengths,
    norm_gains,
    input_branch,
    gate_branch,
    conv_taps,
    conv_bias,
    recur_gate,
    input_gate,
    gate_biases,
    decay_param,
    recur_output,
    dense_gate_one,
    dense_up_one,
    dense_down_one,
    query_weight,
    keyvalue_weight,
    attention_out,
    dense_gate_two,
    dense_up_two,
    dense_down_two,
):
    cid = CIDS
    shard_rows = tokens.shape[0]
    seq = lax.axis_index("seq")
    tp = lax.axis_index("tp")
    lo = lax.rem(seq, LO)
    high = lax.axis_size("seq") // LO
    ways = lax.axis_size("tp")
    own_rows = shard_rows // ways
    plane_rows = shard_rows * LO
    channels = conv_bias.shape[0] // LO
    leading = CONV - 1
    halo_shards = WINDOW // shard_rows
    first_slot = seq * shard_rows
    plane_slot = (seq // LO) * plane_rows
    own_slot = first_slot + tp * own_rows
    valid = layout(doc_lengths, own_slot, own_rows)[3]
    segment, position, _, _ = layout(doc_lengths, first_slot, shard_rows)
    plane_reset = layout(doc_lengths, plane_slot, plane_rows)[2]
    conv_segment = layout(doc_lengths, plane_slot - leading, plane_rows + leading)[0]
    key_segment = layout(
        doc_lengths, first_slot - halo_shards * shard_rows, (halo_shards + 1) * shard_rows
    )[0]

    def ours(block, axis):
        return lax.dynamic_slice_in_dim(block, lo * channels, channels, axis)

    taps, bias = (ours(conv_taps, 1), ours(conv_bias, 0))
    bias_pair, decay_values = (ours(gate_biases, 1), ours(decay_param, 0))

    gate_rows = recur_gate.shape[1]
    weight_rows = input_branch.shape[0]
    attn_rows = jnp.concatenate([query_weight, attention_out.T], axis=1)
    query_width = query_weight.shape[1]
    third = jnp.concatenate(
        [attn_rows, keyvalue_weight.reshape(-1, attn_rows.shape[1])], axis=0
    )

    own_tokens = lax.dynamic_slice_in_dim(tokens, tp * own_rows, own_rows, 0)
    own_cotangent = lax.dynamic_slice_in_dim(cotangent, tp * own_rows, own_rows, 0)
    stream_in = own_tokens.astype(jnp.float32)
    grad_stream = own_cotangent.astype(jnp.float32) * valid[:, None]
    first = swap_columns(
        jnp.concatenate([input_branch, recur_gate.T], axis=0),
        jnp.concatenate([gate_branch, input_gate.T], axis=0),
        jnp.concatenate([recur_output.T, jnp.zeros_like(recur_gate.T)], axis=0),
    )
    normed_own = lowered(rms_norm(stream_in, norm_gains[0]))
    grad_own = lowered(grad_stream)
    first, normed_own, grad_own, dense_gate_one = lax.optimization_barrier(
        (first, normed_own, grad_own, dense_gate_one)
    )
    third_rows = third.shape[0]
    early_wires = lax.all_gather(
        jnp.concatenate([third, first], axis=0), "seq", axis_index_groups=high_groups()
    )
    normed_one, grad_low = gather([normed_own, grad_own], [True, True], cid["gather_two"])
    second = swap_pieces(dense_wire(dense_gate_one, dense_up_one, dense_down_one.T))
    second, dense_gate_two = lax.optimization_barrier((second, dense_gate_two))
    fourth = swap_pieces(dense_wire(dense_gate_two, dense_up_two, dense_down_two.T))
    normed_one, early_wires, grad_low, second, fourth = lax.optimization_barrier(
        (normed_one, early_wires, grad_low, second, fourth)
    )
    third = early_wires[:, :third_rows]
    first_full = early_wires[:, third_rows:]
    first_full = first_full.reshape(high * LO, weight_rows + gate_rows, 3 * channels)
    in_full = first_full[:, :weight_rows, : 2 * channels].reshape(-1, 2 * channels)
    output_full = first_full[:, :weight_rows, 2 * channels :].reshape(-1, channels)
    recur_full = first_full[:, weight_rows:, :channels].reshape(-1, channels)
    input_gate_full = first_full[:, weight_rows:, channels : 2 * channels].reshape(-1, channels)
    weights_one = gather_high(second)
    third = both_lows(third)
    both = product(normed_one, in_full)

    branch = both[:, :channels]
    gating = both[:, channels:]
    rim = shifted(branch[plane_rows - leading :], LO)
    branch_ext = jnp.concatenate([rim, branch], axis=0)
    conv_local = functools.partial(convolve, segment=conv_segment)
    conv_out, conv_pull = jax.vjp(conv_local, branch_ext, taps, bias)
    conv_low = lowered(conv_out)
    recur_raw = block_product(conv_low, recur_full)
    input_raw = block_product(conv_low, input_gate_full)
    rate_local = functools.partial(coefficients, reset=plane_reset)
    (decay, drive), rate_pull = jax.vjp(
        rate_local, recur_raw, input_raw, conv_out, bias_pair, decay_values
    )
    ones = jnp.ones((8, channels), jnp.float32)
    state, state_in = plane_scan(decay, drive, ones, high, False, cid["scan"])
    gate_act, gate_pull = jax.vjp(jax.nn.gelu, gating)
    mixed = lowered(state * gate_act)
    mixed, third = lax.optimization_barrier((mixed, third))
    (summed,) = scatter([product_right(mixed, output_full)], True, cid["scatter_full"])
    stream_one = stream_in + summed
    third = third.reshape(high * LO, -1, third.shape[1])
    query_full = third[:, :weight_rows, :query_width].reshape(-1, query_width)
    attn_full = third[:, :weight_rows, query_width:].reshape(-1, third.shape[2] - query_width)
    part_rows, part_width = keyvalue_weight.shape
    normed_two, keyvalue_full = gather(
        [lowered(rms_norm(stream_one, norm_gains[1])), third[:, weight_rows:].reshape(-1, part_width)],
        [True, False],
        cid["gather_weight"],
    )
    keyvalue_full = keyvalue_full.reshape(ways, high * LO, part_rows, part_width)
    keyvalue_full = keyvalue_full.transpose(1, 0, 2, 3).reshape(-1, part_width)
    factors = turns(position)
    own_factors = [lax.dynamic_slice_in_dim(each, tp * own_rows, own_rows, 0) for each in factors]
    segment_rows = jnp.broadcast_to(segment[None], (8, shard_rows))
    key_column = key_segment[:, None]
    early = (keyvalue_full, query_full, attn_full, factors, own_factors, segment_rows, key_column)
    normed_two, early = lax.optimization_barrier((normed_two, early))
    keyvalue_full, query_full, attn_full, factors, own_factors, segment_rows, key_column = early
    normed_two, weights_one, fourth = lax.optimization_barrier((normed_two, weights_one, fourth))
    weights_two = gather_high(fourth)
    summed, ab_one = dense_call("forward", normed_two, None, weights_one, None, cid["forward"])
    stream_two = stream_one + summed

    normed_own = lowered(rms_norm(stream_two, norm_gains[2]))
    keyval = product(normed_own, keyvalue_full)
    key_rot = lowered(rotate(keyval[:, :HD], own_factors))
    packed = jnp.concatenate([key_rot, lowered(keyval[:, HD:])], axis=1)
    earlier = [shifted(packed, offset) for offset in range(halo_shards, 0, -1)]
    normed_three, seen = gather(
        [normed_own, jnp.concatenate(earlier + [packed], axis=1)], [False, False], cid["gather_seen"]
    )
    extended = jnp.concatenate(
        [seen[:, 2 * HD * k : 2 * HD * (k + 1)] for k in range(halo_shards + 1)], axis=0
    )
    query = product(normed_three, query_full)
    attended, query_rot, log_total = attention(
        query, extended, segment_rows, key_column, *factors
    )
    (summed,) = scatter([product_right(attended, attn_full)], False, cid["scatter_half"])
    stream_three = stream_two + summed

    (normed_four,) = gather(
        [lowered(rms_norm(stream_three, norm_gains[3]))], [True], cid["gather_full"]
    )
    grad_normed, wire_two, hidden_two = dense_call(
        "both", normed_four, grad_low, weights_two, None, cid["both"]
    )
    done_two = reduce_high(wire_two)
    stream_grad, gain_four = jax.vjp(rms_norm, stream_three, norm_gains[3])[1](grad_normed)
    grad_stream = grad_stream + stream_grad
    (grad_attn_low,) = gather([lowered(grad_stream)], [False], cid["gather_half"])
    grad_attn_out = product_left(grad_attn_low, attended)
    grad_attended = lowered(product(grad_attn_low, attn_full))
    grad_query_low, grad_ext = attention_back(
        query_rot,
        extended,
        grad_attended,
        log_total,
        segment_rows,
        key_column,
        *factors,
    )
    grad_query = product_left(normed_three, grad_query_low)
    grad_pieces = grad_ext.reshape(halo_shards + 1, shard_rows, 2 * HD)
    partial = jnp.concatenate(
        [lowered(product_right(grad_query_low, query_full))] + list(grad_pieces), axis=1
    )
    partial, grad_query, grad_attn_out = lax.optimization_barrier(
        (partial, lowered(grad_query), lowered(grad_attn_out))
    )
    attn_kept, attn_given = swap_sums(jnp.concatenate([grad_query, grad_attn_out], axis=1))
    (summed,) = scatter([partial], False, cid["scatter_wide"])
    width = normed_own.shape[1]
    pieces = [
        summed[:, width + 2 * HD * k : width + 2 * HD * (k + 1)] for k in range(halo_shards + 1)
    ]
    keyvalue_total = pieces[halo_shards]
    for offset in range(1, halo_shards + 1):
        piece = shifted(lowered(pieces[halo_shards - offset]), -offset)
        keyvalue_total = keyvalue_total + piece.astype(jnp.float32)
    keyvalue_total, attn_given = lax.optimization_barrier((keyvalue_total, attn_given))
    done_attn = reduce_high(attn_kept.astype(jnp.float32) + attn_given.astype(jnp.float32))
    key_grad = rotate_back(keyvalue_total[:, :HD], own_factors)
    keyvalue_low = lowered(jnp.concatenate([key_grad, keyvalue_total[:, HD:]], axis=1))
    grad_normed = summed[:, :width] + product_right(keyvalue_low, keyvalue_full)
    stream_grad, gain_three = jax.vjp(rms_norm, stream_two, norm_gains[2])[1](grad_normed)
    grad_stream = grad_stream + stream_grad

    (grad_low,) = gather([lowered(grad_stream)], [True], cid["gather_full"])
    grad_low, done_two = lax.optimization_barrier((grad_low, done_two))
    done_two = dense_grads(exchanged(done_two))
    grad_normed, one_wire = dense_call(
        "backward", normed_two, grad_low, weights_one, ab_one, cid["backward"]
    )
    stream_grad, gain_two = jax.vjp(rms_norm, stream_one, norm_gains[1])[1](grad_normed)
    grad_stream = grad_stream + stream_grad
    grad_stream, one_wire = lax.optimization_barrier((grad_stream, one_wire))
    grad_stream, keyvalue_low = lax.optimization_barrier((grad_stream, keyvalue_low))
    done_one = reduce_high(one_wire)
    (keyvalue_grads,) = gather([keyvalue_low], [False], cid["gather_narrow"])
    grad_keyvalue = lowered(product_left(normed_three, keyvalue_grads))
    grad_keyvalue = grad_keyvalue.reshape(high * LO, ways, part_rows, part_width)
    grad_keyvalue = lax.dynamic_slice_in_dim(grad_keyvalue, tp, 1, 1)
    (grad_out_low,) = gather([lowered(grad_stream)], [True], cid["gather_full"])
    grad_out_low, hidden_two = lax.optimization_barrier((grad_out_low, hidden_two))
    (summed_four,) = dense_call("product", hidden_two, None, weights_two, None, cid["product"])
    grad_recur_out = product_left(grad_out_low, mixed)
    grad_mixed = product(grad_out_low, output_full)
    grad_mixed, done_attn, done_two = lax.optimization_barrier((grad_mixed, done_attn, done_two))
    done_attn = done_attn.astype(jnp.float32)
    grad_state = grad_mixed * gate_act
    grad_gating = lowered(gate_pull(grad_mixed * state)[0])
    decay_next = jnp.concatenate([decay[1:], jnp.ones((1, channels), jnp.float32)], axis=0)
    first_decay = jnp.broadcast_to(decay[:1], (8, channels))
    grad_drive, _ = plane_scan(decay_next, grad_state, first_decay, high, True, cid["scan_back"])
    state_prev = jnp.concatenate([state_in[:1], state[:-1]], axis=0)
    grad_decay = grad_drive * state_prev
    grad_recur_raw, grad_input_raw, grad_conv, grad_biases, grad_decay_param = rate_pull(
        (grad_decay, grad_drive)
    )
    grad_recur_gate, conv_back_recur = block_grads(conv_low, recur_full, lowered(grad_recur_raw))
    grad_input_gate, conv_back_input = block_grads(
        conv_low, input_gate_full, lowered(grad_input_raw)
    )
    grad_branch_ext, grad_taps, grad_conv_bias = conv_pull(
        grad_conv + conv_back_recur + conv_back_input
    )
    returned_rim = shifted(grad_branch_ext[:leading], -LO)
    grad_branch = grad_branch_ext[leading:] + jnp.pad(
        returned_rim, ((plane_rows - leading, 0), (0, 0))
    )
    both_low = jnp.concatenate([lowered(grad_branch), grad_gating], axis=1)
    grad_in = product_left(normed_one, both_low)
    partial = lowered(product_right(both_low, in_full))
    partial, grad_in, grad_recur_out = lax.optimization_barrier(
        (partial, lowered(grad_in), lowered(grad_recur_out))
    )
    blocks = high * LO
    wire = jnp.concatenate(
        [
            jnp.concatenate(
                [
                    grad_in.reshape(blocks, weight_rows, 2 * channels),
                    grad_recur_out.reshape(blocks, weight_rows, channels),
                ],
                axis=2,
            ),
            jnp.concatenate(
                [
                    lowered(grad_recur_gate).reshape(blocks, gate_rows, channels),
                    lowered(grad_input_gate).reshape(blocks, gate_rows, channels),
                    jnp.zeros((blocks, gate_rows, channels), jnp.bfloat16),
                ],
                axis=2,
            ),
            grad_keyvalue.reshape(blocks, -1, 3 * channels),
        ],
        axis=1,
    )
    wire, done_one, summed_four = lax.optimization_barrier((wire, done_one, summed_four))
    layer_own = lowered(stream_three + summed_four)
    last = reduce_high(wire.reshape(-1, 3 * channels))
    gain_one = jnp.sum(normed_one.astype(jnp.float32) * partial.astype(jnp.float32), axis=0)
    gain_one = gain_one / norm_gains[0]
    grad_normed, gains_sum, small, layer_out = scatter_and_sums(
        partial,
        jnp.concatenate(
            [jnp.stack([gain_one, gain_two, gain_three, gain_four]), jnp.zeros_like(norm_gains)]
        ),
        jnp.concatenate(
            [grad_taps, grad_conv_bias[None], grad_biases, grad_decay_param[None]], axis=0
        ),
        layer_own,
        high,
        cid["last"],
    )
    rms_local = functools.partial(rms_norm, gain=norm_gains[0])
    stream_grad = jax.vjp(rms_local, stream_in)[1](grad_normed)[0]
    input_own = lowered(grad_stream + stream_grad)
    done_one = exchanged(done_one)
    (input_grad,) = gather([input_own], [False], cid["gather_half"])
    gains_sum = gains_sum[: norm_gains.shape[0]]
    input_grad, layer_out, done_one, last = lax.optimization_barrier(
        (input_grad, layer_out, done_one, last)
    )
    input_grad = input_grad.astype(jnp.float32)
    layer_out = jnp.where(segment[:, None] < doc_lengths.shape[0], layer_out, 0)
    last = exchanged(last)
    keyvalue_grad = jnp.sum(last[:, weight_rows + gate_rows :].astype(jnp.float32), axis=0)
    last_rows, last_gates = (last[:, :weight_rows], last[:, weight_rows : weight_rows + gate_rows])
    return (
        layer_out,
        input_grad,
        gains_sum,
        joined(last_rows[:, :, :channels]),
        joined(last_rows[:, :, channels : 2 * channels]),
        small[:CONV],
        small[CONV],
        joined(last_gates[:, :, :channels]).T,
        joined(last_gates[:, :, channels : 2 * channels]).T,
        small[CONV + 1 : CONV + 3],
        small[CONV + 3],
        joined(last_rows[:, :, 2 * channels :]).T,
        *dense_grads(done_one),
        done_attn[:, :query_width],
        keyvalue_grad.reshape(keyvalue_weight.shape),
        done_attn[:, query_width:].T,
        *done_two,
    )


def solution(mesh):
    placed = (
        P("seq", None),
        P("seq", None),
        P(),
        P(),
        P("seq", "tp"),
        P("seq", "tp"),
        P(None, "tp"),
        P("tp"),
        P("tp", "seq"),
        P("tp", "seq"),
        P(None, "tp"),
        P("tp"),
        P("tp", "seq"),
        P("seq", "tp"),
        P("seq", "tp"),
        P("tp", "seq"),
        P("seq", "tp"),
        P(("seq", "tp"), None),
        P("tp", "seq"),
        P("seq", "tp"),
        P("seq", "tp"),
        P("tp", "seq"),
    )
    return jax.shard_map(
        local,
        mesh=mesh,
        in_specs=placed,
        out_specs=(
            P("seq", None),
            P("seq", None),
            P(),
            P("seq", "tp"),
            P("seq", "tp"),
            P(None, "tp"),
            P("tp"),
            P("tp", "seq"),
            P("tp", "seq"),
            P(None, "tp"),
            P("tp"),
            P("tp", "seq"),
            P("seq", "tp"),
            P("seq", "tp"),
            P("tp", "seq"),
            P("seq", "tp"),
            P(("seq", "tp"), None),
            P("tp", "seq"),
            P("seq", "tp"),
            P("seq", "tp"),
            P("tp", "seq"),
        ),
        check_vma=False,
    )
```
